32 devices in a mesh: fsdp: 4 (over z), context: 2 (over x), tensor: 4 (over y, core).
Axes of the slice: x: 2, y: 2, z: 4, core: 2. Of those that a mesh axis runs over, the one named last changes fastest.
Arguments:
- inputs: bfloat16 [4096, 2048], P(('fsdp', 'context')), may hold values from -6 to 6
- attn_gain: bfloat16 [2048], replicated, may hold values from 0.5 to 1.5
- joined_projection_weight: bfloat16 [2048, 5120], P(('fsdp', 'context'), 'tensor'), may hold values from -0.125 to 0.125
- q_gain: bfloat16 [128], replicated, may hold values from 0.5 to 1.5
- k_gain: bfloat16 [128], replicated, may hold values from 0.5 to 1.5
- w_o: bfloat16 [2048, 4096], P(('fsdp', 'context'), 'tensor'), may hold values from -0.375 to 0.375
- moe_gain: bfloat16 [2048], replicated, may hold values from 0.5 to 1.5
- router: bfloat16 [2048, 16], replicated, may hold values from -0.0625 to 0.0625
- w_experts: bfloat16 [2048, 16, 3, 768], P(('fsdp', 'context'), None, None, 'tensor'), may hold values from -0.25 to 0.25
- segments: int32 [4096], P('fsdp'), may hold values from 0 to 4, as said below
- experts: int32 [4096, 8], P(('fsdp', 'context')), may hold values from 0 to 15, all different within a row
- out_grad: bfloat16 [4096, 2048], P(('fsdp', 'context')), may hold values from -6 to 6
Outputs:
- output: bfloat16 [4096, 2048], P(('fsdp', 'context'))
- inputs_grad: bfloat16 [4096, 2048], P(('fsdp', 'context'))
- attn_gain_grad: float32 [2048], replicated
- w_qkv_grad: float32 [2048, 5120], P(('fsdp', 'context'), 'tensor')
- q_gain_grad: float32 [128], replicated
- k_gain_grad: float32 [128], replicated
- w_o_grad: float32 [2048, 4096], P(('fsdp', 'context'), 'tensor')
- moe_gain_grad: float32 [2048], replicated
- router_grad: float32 [2048, 16], replicated
- w_experts_grad: float32 [2048, 16, 3, 768], P(('fsdp', 'context'), None, None, 'tensor')
The draws below stay inside these ranges and needn't reach their ends.
Inputs may be any that keep to these rules, and one draw needn't show every extreme that they name: `segments`: within each sequence of 1024 tokens the numbers start at 0, rise by 0 or 1 from one token to the next and end at 4; one document covers the middle quarter of every sequence. Each row names 8 different experts, and every expert is named by some row.
All inputs are finite; a program needn't handle non-finite values.
Results may differ from the reference program's by a relative error of at most 0.02.
Values may be sent and summed in bfloat16 or wider, within the bound.
No kernel may reach another device: no remote copies, remote signals or barrier semaphores. Data moves between devices by JAX's collectives and lax.ppermute only.
A program may use at most 448 MiB of HBM per device.

```python
import jax
import jax.numpy as jnp
from jax import lax

D = 2048
QUERY_HEADS = 32
KEY_VALUE_HEADS = 4
HEAD_DIMENSION = 128
FF = 768
TOPK = 8
E = 16
SEQ = 1024
TOKENS = 4096
QKV = 5120


def draw_segments(key, part):
    key = jax.random.fold_in(key, 7)
    seq_count = TOKENS // SEQ
    doc_starts = max(SEQ // 256, 3)
    seq_keys = jax.random.split(key, seq_count)
    orders = jax.vmap(lambda one_key: jax.random.permutation(one_key, SEQ))(seq_keys).astype(jnp.int32)
    index_all = jnp.arange(SEQ, dtype=jnp.int32)[None, :]
    middle = (index_all >= SEQ // 2 - SEQ // 8) & (index_all < SEQ // 2 + SEQ // 8)
    eligible = (index_all > 0) & jnp.logical_not(middle)
    scored = jnp.where(eligible, orders + 1, 0).astype(jnp.int32)
    picked = lax.top_k(scored, doc_starts)[1].astype(jnp.int32)
    starts = jnp.any(index_all[:, None, :] == picked[:, :, None], axis=1)
    return jnp.cumsum(starts.astype(jnp.int32), axis=1).reshape(-1).astype(jnp.int32)


def steps_of(stream_key, shape, cuts, low, largest):
    gain = 1.0
    for position, blocks in cuts:
        heights = jax.random.uniform(jax.random.fold_in(jax.random.fold_in(stream_key, 6), position), (blocks,), jnp.float32, low / len(cuts), largest / len(cuts))
        gain = gain * jnp.repeat(jnp.exp(heights), shape[position] // blocks).reshape((-1,) + (1,) * (len(shape) - 1 - position))
    return gain


def distinct(key, rows, amount, top, lift):
    sequence = jax.random.permutation(jax.random.fold_in(key, 1), amount)
    boost = sequence
    for power in range(3):
        boost = boost * boost // amount
    boost = boost * lift // amount
    tickets = jax.random.randint(jax.random.fold_in(key, 2), (rows, amount), 0, 4096) + boost
    holders = jax.random.permutation(jax.random.fold_in(key, 3), rows)[jnp.arange(amount) % rows]
    tickets = jnp.where(jnp.arange(rows)[:, None] == holders[None, :], 1 << 14, tickets)
    score = tickets * amount + jnp.arange(amount)
    return lax.top_k(score.astype(jnp.int32), top)[1].astype(jnp.int32)


def noise(own_key, extent, scale, reach, pieces=(), held_as=jnp.bfloat16):
    values = jax.random.normal(own_key, extent, jnp.float32) * scale
    if len(pieces) > 0:
        values = steps_of(own_key, extent, pieces, -0.22, 0.18) * values
    return jnp.clip(values, min=-reach, max=reach).astype(held_as)


def setup_inputs(seed: int = 0) -> dict:
    key_of = jax.random.split(jax.random.key(seed), 13)
    inputs = noise(key_of[0], (TOKENS, D), 1.0, 6.0, ((0, 8),))
    attn_gain = jnp.clip(1.0 + 0.1 * jax.random.normal(key_of[1], (D,), jnp.float32), 0.5, 1.5).astype(jnp.bfloat16)
    joined_projection_weight = noise(key_of[2], (D, QKV), D ** -0.5, 0.125, ((0, 8), (1, 4)))
    q_gain = jnp.clip(1.0 + 0.1 * jax.random.normal(key_of[3], (HEAD_DIMENSION,), jnp.float32), 0.5, 1.5).astype(jnp.bfloat16)
    k_gain = jnp.clip(1.0 + 0.1 * jax.random.normal(key_of[4], (HEAD_DIMENSION,), jnp.float32), 0.5, 1.5).astype(jnp.bfloat16)
    w_o = noise(key_of[5], (D, QUERY_HEADS * HEAD_DIMENSION), (QUERY_HEADS * HEAD_DIMENSION // 16) ** -0.5, 0.375, ((0, 8), (1, 4)))
    moe_gain = jnp.clip(1.0 + 0.1 * jax.random.normal(key_of[6], (D,), jnp.float32), 0.5, 1.5).astype(jnp.bfloat16)
    router = noise(key_of[7], (D, E), (4 * D) ** -0.5, 0.0625)
    w_experts = noise(key_of[8], (D, E, 3, FF), (D // 4) ** -0.5, 0.25, ((0, 8), (3, 4)))
    segments = draw_segments(jax.random.fold_in(key_of[12], 71), 0)
    experts = distinct(key_of[10], TOKENS, E, TOPK, 4096)
    out_grad = noise(key_of[11], (TOKENS, D), 1.0, 6.0, ((0, 8),))
    return dict(inputs=inputs, attn_gain=attn_gain, joined_projection_weight=joined_projection_weight, q_gain=q_gain, k_gain=k_gain, w_o=w_o, moe_gain=moe_gain, router=router, w_experts=w_experts, segments=segments, experts=experts, out_grad=out_grad)


EPSILON = 1e-06
ROPE_THETA = 1000000.0
NEGATIVE = -1e+30
BEST_PRECISION = lax.Precision.HIGHEST

@jax.custom_vjp
def low(v):
    return lax.optimization_barrier(v.astype(jnp.bfloat16)).astype(jnp.float32)

@jax.custom_vjp
def reduced_backward(v):
    return v

def low_keep(v):
    return (low(v), None)

def low_pass(kept, grad):
    return (grad,)

def back_keep(v):
    return (v, None)

def back_low(kept, grad):
    return (low(grad),)
low.defvjp(low_keep, low_pass)
reduced_backward.defvjp(back_keep, back_low)

def norm_rows(matrix, scaling):
    return matrix * lax.rsqrt(lax.optimization_barrier(jnp.mean(matrix * matrix, axis=-1, keepdims=True)) + EPSILON) * scaling

def doc_positions(segment_ids):
    index_all = jnp.arange(segment_ids.shape[0], dtype=jnp.int32)
    starts = jnp.concatenate([jnp.ones((1,), jnp.int32), (segment_ids[1:] != segment_ids[:-1]).astype(jnp.int32)])
    return index_all - lax.cummax(index_all * starts, axis=0)

def rotate(tensor_array, positions):
    half_size = tensor_array.shape[-1] // 2
    inverse = ROPE_THETA ** (-2.0 * jnp.arange(half_size, dtype=jnp.float32) / tensor_array.shape[-1])
    angles = positions.astype(jnp.float32)[:, None] * inverse[None, :]
    cosine = jnp.concatenate([jnp.cos(angles), jnp.cos(angles)], axis=-1)[:, None, :]
    sine_table = jnp.concatenate([jnp.sin(angles), jnp.sin(angles)], axis=-1)[:, None, :]
    turned = jnp.concatenate([-tensor_array[..., half_size:], tensor_array[..., :half_size]], axis=-1)
    return tensor_array * cosine + turned * sine_table

def layer(inputs, attn_gain, joined_projection_weight, q_gain, k_gain, w_o, moe_gain, router, w_experts, segment_ids, expert_ids):
    sequence_length = inputs.shape[0]
    queries_per_group = QUERY_HEADS // KEY_VALUE_HEADS
    rows_per_block = min(512, sequence_length)
    block_count = sequence_length // rows_per_block
    normalized_input = low(norm_rows(inputs, attn_gain))
    projected_rows = reduced_backward(jnp.dot(normalized_input, joined_projection_weight, precision=BEST_PRECISION)).reshape(sequence_length, KEY_VALUE_HEADS, queries_per_group + 2, HEAD_DIMENSION)
    positions = doc_positions(segment_ids)
    queries = low(rotate(norm_rows(projected_rows[:, :, :queries_per_group].reshape(sequence_length, QUERY_HEADS, HEAD_DIMENSION), q_gain), positions))
    key_rows = low(rotate(norm_rows(projected_rows[:, :, queries_per_group], k_gain), positions))
    value_rows = low(projected_rows[:, :, queries_per_group + 1])
    token_index = jnp.arange(sequence_length, dtype=jnp.int32)
    score_scale = HEAD_DIMENSION ** (-0.5)

    def attend(block_args):
        block_of_queries, block_segments, block_index = block_args
        grouped_heads = block_of_queries.reshape(rows_per_block, KEY_VALUE_HEADS, queries_per_group, HEAD_DIMENSION)
        scores = reduced_backward(jnp.einsum('qghd,kgd->ghqk', grouped_heads, key_rows, precision=BEST_PRECISION) * score_scale)
        allowed = (block_segments[:, None] == segment_ids[None, :]) & (block_index[:, None] >= token_index[None, :])
        scores = jnp.where(allowed[None, None], scores, NEGATIVE)
        raised = jnp.exp(scores - lax.optimization_barrier(jnp.max(scores, axis=-1, keepdims=True)))
        attn_probs = low(raised / lax.optimization_barrier(jnp.sum(raised, axis=-1, keepdims=True)))
        mixed_block = jnp.einsum('ghqk,kgd->qghd', attn_probs, value_rows, precision=BEST_PRECISION)
        return mixed_block.reshape(rows_per_block, QUERY_HEADS * HEAD_DIMENSION)
    attended = lax.map(jax.checkpoint(attend), (queries.reshape(block_count, rows_per_block, QUERY_HEADS, HEAD_DIMENSION), segment_ids.reshape(block_count, rows_per_block), token_index.reshape(block_count, rows_per_block)))
    attended = low(reduced_backward(attended.reshape(sequence_length, QUERY_HEADS * HEAD_DIMENSION)))
    hidden_state = inputs + reduced_backward(jnp.dot(attended, w_o.T, precision=BEST_PRECISION))
    mixed_in = low(norm_rows(hidden_state, moe_gain))
    logits = reduced_backward(jnp.dot(mixed_in, router, precision=BEST_PRECISION))
    chosen = jnp.take_along_axis(logits, expert_ids, axis=1)
    raised_gate = jnp.exp(chosen - lax.optimization_barrier(jnp.max(chosen, axis=-1, keepdims=True)))
    gate_values = raised_gate / lax.optimization_barrier(jnp.sum(raised_gate, axis=-1, keepdims=True))
    picked = (expert_ids[:, :, None] == jnp.arange(E, dtype=jnp.int32)[None, None, :]).astype(jnp.float32)
    shares = jnp.einsum('sk,ske->es', gate_values, picked, precision=BEST_PRECISION)

    def expert_step(running, expert_args):
        weights, expert_share = expert_args
        gate_up = reduced_backward(jnp.einsum('sd,dcf->scf', mixed_in, weights[:, :2], precision=BEST_PRECISION))
        active = low(gate_up[:, 0] * jax.nn.sigmoid(gate_up[:, 0]) * gate_up[:, 1])
        result = reduced_backward(jnp.dot(active, weights[:, 2].T, precision=BEST_PRECISION))
        return (running + expert_share[:, None] * result, None)
    moe_total = lax.scan(jax.checkpoint(expert_step), jnp.zeros(inputs.shape, jnp.float32), (jnp.moveaxis(w_experts, 1, 0), shares))[0]
    return hidden_state + moe_total

def reference(inputs, attn_gain, joined_projection_weight, q_gain, k_gain, w_o, moe_gain, router, w_experts, segments, experts, out_grad):
    params = tuple((param.astype(jnp.float32) for param in (attn_gain, joined_projection_weight, q_gain, k_gain, w_o, moe_gain, router, w_experts)))
    seq_count = TOKENS // SEQ
    seq_inputs_all = inputs.astype(jnp.float32).reshape(seq_count, SEQ, D)
    seq_grads_all = out_grad.astype(jnp.float32).reshape(seq_count, SEQ, D)
    seq_segments_all = segments.reshape(seq_count, SEQ)
    seq_experts_all = experts.reshape(seq_count, SEQ, TOPK)

    def one_sequence(totals, seq_args):
        seq_inputs, seq_segments, seq_experts, seq_grad = seq_args

        def forward(values, *weights):
            return layer(values, *weights, seq_segments, seq_experts)
        result, pullback = jax.vjp(forward, seq_inputs, *params)
        pulled = pullback(seq_grad)
        return (tuple((total_now + part_now for total_now, part_now in zip(totals, pulled[1:]))), (result, pulled[0]))
    zero_grads = tuple((jnp.zeros(param.shape, jnp.float32) for param in params))
    totals, (results, input_grads) = lax.scan(one_sequence, zero_grads, (seq_inputs_all, seq_segments_all, seq_experts_all, seq_grads_all))
    return (results.reshape(TOKENS, D).astype(jnp.bfloat16), input_grads.reshape(TOKENS, D).astype(jnp.bfloat16), totals[0], totals[1], totals[2], totals[3], totals[4], totals[5], totals[6], totals[7])
```

```python
import functools

import jax
import jax.numpy as jnp
from jax import lax
from jax.experimental import pallas as pl
from jax.experimental.pallas import tpu as pltpu
from jax.sharding import PartitionSpec as P

QUERY_HEADS = 32
KEY_VALUE_HEADS = 4


EPSILON = 1e-06
ROPE_THETA = 1000000.0
NEGATIVE = -1e30
BEST_PRECISION = lax.Precision.HIGHEST


def norm_rows(matrix, scaling):
    return matrix * lax.rsqrt(jnp.mean(matrix * matrix, axis=-1, keepdims=True) + EPSILON) * scaling


def doc_positions(segment_ids):
    index_all = jnp.arange(segment_ids.shape[0], dtype=jnp.int32)
    starts = jnp.concatenate(
        [jnp.ones((1,), jnp.int32), (segment_ids[1:] != segment_ids[:-1]).astype(jnp.int32)]
    )
    return index_all - lax.cummax(index_all * starts, axis=0)


def rotate(tensor_array, positions):
    half_size = tensor_array.shape[-1] // 2
    inverse = ROPE_THETA ** (
        -2.0 * jnp.arange(half_size, dtype=jnp.float32) / tensor_array.shape[-1]
    )
    angles = positions.astype(jnp.float32)[:, None] * inverse[None, :]
    cosine = jnp.concatenate([jnp.cos(angles), jnp.cos(angles)], axis=-1)[:, None, :]
    sine_table = jnp.concatenate([jnp.sin(angles), jnp.sin(angles)], axis=-1)[:, None, :]
    turned = jnp.concatenate(
        [-tensor_array[..., half_size:], tensor_array[..., :half_size]], axis=-1
    )
    return tensor_array * cosine + turned * sine_table


def block_groups(group_sizes, first_row, row_count):
    group_ends = jnp.cumsum(group_sizes)
    begins = group_ends - group_sizes
    clipped_end = jnp.clip(group_ends, first_row, first_row + row_count)
    clipped_begin = jnp.clip(begins, first_row, first_row + row_count)
    return clipped_end - clipped_begin


def times_transposed(left_side, right_side):
    return lax.dot_general(
        left_side, right_side, (((1,), (1,)), ((), ())), preferred_element_type=jnp.float32
    )


def outer_rows(left_side, right_side):
    return lax.dot_general(
        left_side, right_side, (((0,), (0,)), ((), ())), preferred_element_type=jnp.float32
    )


def shards(
    inputs,
    attn_gain,
    joined_projection_weight,
    q_gain,
    k_gain,
    w_o,
    moe_gain,
    router,
    w_experts,
    segments,
    experts,
    out_grad,
):
    tok_rows, model_width = inputs.shape
    head_size = q_gain.shape[0]
    head_groups = KEY_VALUE_HEADS // lax.axis_size("tensor")
    queries_per_group = QUERY_HEADS // KEY_VALUE_HEADS
    local_heads = head_groups * queries_per_group
    top_count = experts.shape[1]
    expert_count = router.shape[1]
    sequence_length = segments.shape[0]
    weight_rows = joined_projection_weight.shape[0]
    span_start = lax.axis_index("context") * tok_rows
    first_tensor = (lax.axis_index("tensor") == 0).astype(jnp.float32)
    gain_attn = attn_gain.astype(jnp.float32)
    gain_moe = moe_gain.astype(jnp.float32)
    gain_query = q_gain.astype(jnp.float32)
    gain_key = k_gain.astype(jnp.float32)
    token_index = jnp.arange(sequence_length, dtype=jnp.int32)
    positions = lax.dynamic_slice_in_dim(doc_positions(segments), span_start, tok_rows)
    local_segments = lax.dynamic_slice_in_dim(segments, span_start, tok_rows)
    local_index = span_start + jnp.arange(tok_rows, dtype=jnp.int32)
    rows_per_block = min(512, tok_rows)
    score_scale = head_size ** (-0.5)
    attn_in, attn_out = (
        lax.all_gather(joined_projection_weight, ("fsdp", "context"), axis=0, tiled=True),
        lax.all_gather(w_o, ("fsdp", "context"), axis=0, tiled=True),
    )
    residual = inputs.astype(jnp.float32)
    inverse_attn = lax.rsqrt(jnp.mean(residual * residual, axis=-1, keepdims=True) + EPSILON)
    unit_attn = residual * inverse_attn
    normalized_input = (unit_attn * gain_attn).astype(jnp.bfloat16)
    projected_rows = jnp.dot(normalized_input, attn_in, preferred_element_type=jnp.float32).reshape(
        tok_rows, head_groups, queries_per_group + 2, head_size
    )
    query_raw = projected_rows[:, :, :queries_per_group].reshape(tok_rows, local_heads, head_size)
    key_raw = projected_rows[:, :, queries_per_group]
    value_raw = projected_rows[:, :, queries_per_group + 1]

    def prepare(query_part, key_part, query_gain, key_gain):
        return (
            rotate(norm_rows(query_part, query_gain), positions),
            rotate(norm_rows(key_part, key_gain), positions),
        )

    query_rot, key_rot = prepare(query_raw, key_raw, gain_query, gain_key)
    queries = query_rot.astype(jnp.bfloat16)
    key_values = jnp.concatenate([key_rot, value_raw], axis=-1).astype(jnp.bfloat16)
    gathered_pairs = lax.all_gather(key_values, "context", axis=0, tiled=True)
    all_keys = gathered_pairs[:, :, :head_size]
    all_values = gathered_pairs[:, :, head_size:]

    def block_scores(first_row):
        grouped_heads = queries.reshape(rows_per_block, head_groups, queries_per_group, head_size)
        scores = (
            jnp.einsum(
                "qghd,kgd->ghqk", grouped_heads, all_keys, preferred_element_type=jnp.float32
            )
            * score_scale
        )
        same_doc = local_segments[first_row : first_row + rows_per_block, None] == segments[None, :]
        earlier = local_index[first_row : first_row + rows_per_block, None] >= token_index[None, :]
        return (grouped_heads, jnp.where((same_doc & earlier)[None, None], scores, NEGATIVE))

    first_row = 0
    grouped_heads, scores = block_scores(first_row)
    row_peak = jnp.max(scores, axis=-1, keepdims=True)
    raised = jnp.exp(scores - row_peak)
    summed = jnp.sum(raised, axis=-1, keepdims=True)
    attn_probs = (raised / summed).astype(jnp.bfloat16)
    mixed_block = jnp.einsum(
        "ghqk,kgd->qghd", attn_probs, all_values, preferred_element_type=jnp.float32
    )
    mixed_parts = mixed_block.reshape(rows_per_block, local_heads * head_size)
    log_totals = [row_peak + jnp.log(summed)]
    attended = mixed_parts.astype(jnp.bfloat16)
    attn_sum = lax.psum(times_transposed(attended, attn_out), "tensor")
    hidden_state = residual + attn_sum
    inverse_moe = lax.rsqrt(jnp.mean(hidden_state * hidden_state, axis=-1, keepdims=True) + EPSILON)
    unit_moe = hidden_state * inverse_moe
    mixed_in = (unit_moe * gain_moe).astype(jnp.bfloat16)
    logits = jnp.dot(mixed_in, router, preferred_element_type=jnp.float32)
    chosen = jnp.take_along_axis(logits, experts, axis=1)
    raised_gate = jnp.exp(chosen - jnp.max(chosen, axis=-1, keepdims=True))
    gate_values = raised_gate / jnp.sum(raised_gate, axis=-1, keepdims=True)
    expert_all = lax.all_gather(w_experts, ("fsdp", "context"), axis=0, tiled=True)
    hidden_units = expert_all.shape[3]
    flat_ids = experts.reshape(-1)
    sort_order = jnp.argsort(flat_ids, stable=True)
    undo_order = jnp.argsort(sort_order, stable=True)
    token_of = sort_order // top_count
    expert_ids = jnp.arange(expert_count, dtype=jnp.int32)
    group_sizes = jnp.sum((flat_ids[:, None] == expert_ids[None, :]).astype(jnp.int32), axis=0)
    sorted_inputs = jnp.take(mixed_in, token_of, axis=0)
    sorted_gates = jnp.take(gate_values.reshape(-1), sort_order)
    weights_in = jnp.transpose(expert_all[:, :, :2], (1, 0, 2, 3)).reshape(
        expert_count, model_width, 2 * hidden_units
    )
    weights_out = jnp.transpose(expert_all[:, :, 2], (1, 2, 0))
    assigned = flat_ids.shape[0]
    slab_rows = min(2048, assigned)
    moe_part = jnp.zeros((tok_rows, model_width), jnp.float32)
    gate_up_parts = []
    active_parts = []
    gate_dot_parts = []
    for slab_start in range(0, assigned, slab_rows):
        slab_sizes = block_groups(group_sizes, slab_start, slab_rows)
        slab_tokens = token_of[slab_start : slab_start + slab_rows]
        gate_up = lax.ragged_dot(
            sorted_inputs[slab_start : slab_start + slab_rows],
            weights_in,
            slab_sizes,
            preferred_element_type=jnp.float32,
        )
        gate_half = gate_up[:, :hidden_units]
        active = (gate_half * jax.nn.sigmoid(gate_half) * gate_up[:, hidden_units:]).astype(
            jnp.bfloat16
        )
        outputs = lax.ragged_dot(
            active, weights_out, slab_sizes, preferred_element_type=jnp.float32
        )
        moe_part = moe_part.at[slab_tokens].add(
            outputs * sorted_gates[slab_start : slab_start + slab_rows][:, None]
        )
        gate_dot_parts.append(
            jnp.sum(jnp.take(out_grad, slab_tokens, axis=0).astype(jnp.float32) * outputs, axis=-1)
        )
        gate_up_parts.append(gate_up)
        active_parts.append(active)
    gate_dot_part = jnp.take(jnp.concatenate(gate_dot_parts), undo_order).reshape(
        tok_rows, top_count
    )
    moe_sum, gate_dot = (
        lax.psum(moe_part.astype(jnp.bfloat16), "tensor").astype(jnp.float32),
        lax.psum(gate_dot_part.astype(jnp.bfloat16), "tensor").astype(jnp.float32),
    )
    output = (hidden_state + moe_sum).astype(jnp.bfloat16)
    attn_in, attn_out = (
        lax.all_gather(joined_projection_weight, ("fsdp", "context"), axis=0, tiled=True),
        lax.all_gather(w_o, ("fsdp", "context"), axis=0, tiled=True),
    )
    expert_all = lax.all_gather(w_experts, ("fsdp", "context"), axis=0, tiled=True)
    cotangent = out_grad.astype(jnp.float32)
    gate_slope = gate_values * (gate_dot - jnp.sum(gate_values * gate_dot, axis=-1, keepdims=True))
    picked = (experts[:, :, None] == expert_ids[None, None, :]).astype(jnp.float32)
    logit_grad = jnp.einsum("tk,tke->te", gate_slope, picked, precision=BEST_PRECISION).astype(
        jnp.bfloat16
    )
    router_term = outer_rows(mixed_in, logit_grad) * first_tensor
    router_back = times_transposed(logit_grad, router)
    weights_down = jnp.transpose(expert_all[:, :, 2], (1, 0, 2))
    weights_back = jnp.transpose(expert_all[:, :, :2], (1, 2, 3, 0)).reshape(
        expert_count, 2 * hidden_units, model_width
    )
    back_part = jnp.zeros((tok_rows, model_width), jnp.float32)
    scaled_parts = []
    slope_parts = []
    for slab_index, slab_start in enumerate(range(0, assigned, slab_rows)):
        slab_sizes = block_groups(group_sizes, slab_start, slab_rows)
        slab_tokens = token_of[slab_start : slab_start + slab_rows]
        scaled = (
            jnp.take(out_grad, slab_tokens, axis=0).astype(jnp.float32)
            * sorted_gates[slab_start : slab_start + slab_rows][:, None]
        ).astype(jnp.bfloat16)
        act_grad = lax.ragged_dot(
            scaled, weights_down, slab_sizes, preferred_element_type=jnp.float32
        )
        gate_half = gate_up_parts[slab_index][:, :hidden_units]
        up_half = gate_up_parts[slab_index][:, hidden_units:]
        gate_sigmoid = jax.nn.sigmoid(gate_half)
        gate_up_grad = jnp.concatenate(
            [
                act_grad * up_half * gate_sigmoid * (1.0 + gate_half * (1.0 - gate_sigmoid)),
                act_grad * gate_half * gate_sigmoid,
            ],
            axis=1,
        ).astype(jnp.bfloat16)
        back_part = back_part.at[slab_tokens].add(
            lax.ragged_dot(
                gate_up_grad, weights_back, slab_sizes, preferred_element_type=jnp.float32
            )
        )
        scaled_parts.append(scaled)
        slope_parts.append(gate_up_grad)
    sorted_scaled = jnp.concatenate(scaled_parts, axis=0)
    sorted_slopes = jnp.concatenate(slope_parts, axis=0)
    active_all = jnp.concatenate(active_parts, axis=0)
    numbers = lax.RaggedDotDimensionNumbers(
        dot_dimension_numbers=(([0], [0]), ([], [])),
        lhs_ragged_dimensions=[0],
        rhs_group_dimensions=[],
    )
    grad_in = lax.ragged_dot_general(
        sorted_inputs, sorted_slopes, group_sizes, numbers, preferred_element_type=jnp.float32
    )
    grad_out = lax.ragged_dot_general(
        sorted_scaled, active_all, group_sizes, numbers, preferred_element_type=jnp.float32
    )
    stacked = jnp.concatenate(
        [
            grad_in.reshape(
                expert_count, weight_rows * lax.axis_size(("fsdp", "context")), 2, hidden_units
            ),
            grad_out[:, :, None],
        ],
        axis=2,
    )
    w_experts_grad = lax.psum_scatter(
        jnp.transpose(stacked, (1, 0, 2, 3)).astype(jnp.bfloat16),
        ("fsdp", "context"),
        scatter_dimension=0,
        tiled=True,
    ).astype(jnp.float32)
    moe_back = lax.psum(back_part, "tensor") + router_back
    unit_grad = moe_back * gain_moe
    state_grad = cotangent + inverse_moe * (
        unit_grad - unit_moe * jnp.mean(unit_grad * unit_moe, axis=-1, keepdims=True)
    )
    moe_gain_term = jnp.sum(moe_back * unit_moe, axis=0) * first_tensor
    branch_grad = state_grad.astype(jnp.bfloat16)
    attended_grad = jnp.dot(branch_grad, attn_out, preferred_element_type=jnp.float32).astype(
        jnp.bfloat16
    )
    w_o_grad = lax.psum_scatter(
        outer_rows(branch_grad, attended).astype(jnp.bfloat16),
        ("fsdp", "context"),
        scatter_dimension=0,
        tiled=True,
    ).astype(jnp.float32)
    key_grad = jnp.zeros((sequence_length, head_groups, head_size), jnp.float32)
    value_grad = jnp.zeros((sequence_length, head_groups, head_size), jnp.float32)
    query_parts = []
    for block_number, first_row in enumerate(range(0, tok_rows, rows_per_block)):
        grouped_heads, scores = block_scores(first_row)
        attn_probs = jnp.exp(scores - log_totals[block_number])
        attn_low = attn_probs.astype(jnp.bfloat16)
        mixed_grad = attended_grad.reshape(
            rows_per_block, head_groups, queries_per_group, head_size
        )
        prob_grad = jnp.einsum(
            "qghd,kgd->ghqk", mixed_grad, all_values, preferred_element_type=jnp.float32
        )
        score_grad = (
            attn_probs * (prob_grad - jnp.sum(attn_probs * prob_grad, axis=-1, keepdims=True))
        ).astype(jnp.bfloat16)
        block_of_queries = (
            jnp.einsum("ghqk,kgd->qghd", score_grad, all_keys, preferred_element_type=jnp.float32)
            * score_scale
        )
        query_parts.append(block_of_queries.reshape(rows_per_block, local_heads, head_size))
        key_grad = (
            jnp.einsum(
                "ghqk,qghd->kgd", score_grad, grouped_heads, preferred_element_type=jnp.float32
            )
            * score_scale
        )
        value_grad = jnp.einsum(
            "ghqk,qghd->kgd", attn_low, mixed_grad, preferred_element_type=jnp.float32
        )
    pair_grad = lax.psum_scatter(
        jnp.concatenate([key_grad, value_grad], axis=-1).astype(jnp.bfloat16),
        "context",
        scatter_dimension=0,
        tiled=True,
    ).astype(jnp.float32)
    query_grad = query_parts[0]
    pullback = jax.vjp(prepare, query_raw, key_raw, gain_query, gain_key)[1]
    query_back, key_back, q_gain_term, k_gain_term = pullback(
        (query_grad, pair_grad[:, :, :head_size])
    )
    projected_grad = (
        jnp.concatenate(
            [
                query_back.reshape(tok_rows, head_groups, queries_per_group, head_size),
                key_back[:, :, None],
                pair_grad[:, :, None, head_size:],
            ],
            axis=2,
        )
        .reshape(tok_rows, -1)
        .astype(jnp.bfloat16)
    )
    normed_grad = lax.psum(
        times_transposed(projected_grad, attn_in).astype(jnp.bfloat16), "tensor"
    ).astype(jnp.float32)
    w_qkv_grad = lax.psum_scatter(
        outer_rows(normalized_input, projected_grad).astype(jnp.bfloat16),
        ("fsdp", "context"),
        scatter_dimension=0,
        tiled=True,
    ).astype(jnp.float32)
    unit_back = normed_grad * gain_attn
    inputs_grad = (
        state_grad
        + inverse_attn
        * (unit_back - unit_attn * jnp.mean(unit_back * unit_attn, axis=-1, keepdims=True))
    ).astype(jnp.bfloat16)
    attn_gain_term = jnp.sum(normed_grad * unit_attn, axis=0) * first_tensor
    attn_gain_grad, q_gain_grad, k_gain_grad, moe_gain_grad, router_grad = lax.psum(
        (attn_gain_term, q_gain_term, k_gain_term, moe_gain_term, router_term),
        ("fsdp", "context", "tensor"),
    )
    return (
        output,
        inputs_grad,
        attn_gain_grad,
        w_qkv_grad,
        q_gain_grad,
        k_gain_grad,
        w_o_grad,
        moe_gain_grad,
        router_grad,
        w_experts_grad,
    )


SPREAD = ("fsdp", "context")
VMEM_BYTES = 60 * 2**20


def flip_pairs(size, bit):
    return [(place, place ^ bit) for place in range(size)]


def flip(array, name, bit):
    return lax.ppermute(array, name, flip_pairs(lax.axis_size(name), bit))


def add_low(left_side, right_side):
    return (left_side.astype(jnp.float32) + right_side.astype(jnp.float32)).astype(jnp.bfloat16)


def partner_bits():
    size = lax.axis_size("tensor")
    return [size >> step for step in range(1, size.bit_length())]


def partner_order():
    order = [0]
    for bit in partner_bits():
        order = order + [offset ^ bit for offset in order]
    return order


def own_first(array):
    place = lax.axis_index("tensor")
    rows = array.shape[0] // lax.axis_size("tensor")
    return jnp.concatenate(
        [
            lax.dynamic_slice_in_dim(array, (place ^ offset) * rows, rows)
            for offset in partner_order()
        ],
        axis=0,
    )


def own_back(array):
    place = lax.axis_index("tensor")
    order = partner_order()
    rows = array.shape[0] // len(order)
    slot_of = jnp.array([order.index(offset) for offset in range(len(order))], jnp.int32)
    return jnp.concatenate(
        [
            lax.dynamic_slice_in_dim(array, slot_of[place ^ block] * rows, rows)
            for block in range(len(order))
        ],
        axis=0,
    )


def tensor_gather_rows(piece):
    for bit in partner_bits():
        piece = jnp.concatenate([piece, flip(piece, "tensor", bit)], axis=0)
    return piece


def tensor_scatter_rows(half_of):
    bits = partner_bits()
    theirs = flip(half_of(1), "tensor", bits[-1])
    total = add_low(half_of(0), theirs)
    for bit in bits[-2::-1]:
        rows = total.shape[0] // 2
        total = add_low(total[:rows], flip(total[rows:], "tensor", bit))
    return total


def split_halves(array, axis, place):
    mine = lax.dynamic_index_in_dim(array, place, axis, keepdims=False)
    theirs = lax.dynamic_index_in_dim(array, 1 - place, axis, keepdims=False)
    return mine, theirs


def spread_scatter(array):
    fsdp_size, place = lax.axis_size("fsdp"), lax.axis_index("context")
    blocks = array.reshape(fsdp_size, 2, -1, array.shape[1])
    mine, theirs = split_halves(blocks, 1, place)
    summed = add_low(mine, flip(theirs, "context", 1))
    parts = lax.all_to_all(summed, "fsdp", 0, 0, tiled=True)
    return jnp.sum(parts.astype(jnp.float32), axis=0)


def spread_gather(piece):
    fsdp_size, place = lax.axis_size("fsdp"), lax.axis_index("context")
    sent = jnp.broadcast_to(piece[None], (fsdp_size,) + piece.shape)
    column = lax.all_to_all(sent, "fsdp", 0, 0, tiled=True)
    other = flip(column, "context", 1)
    first = jnp.where(place == 0, column, other)
    second = jnp.where(place == 0, other, column)
    return jnp.stack([first, second], axis=1).reshape(-1, piece.shape[1])


def sum_everywhere(array):
    for name in ("tensor", "context", "fsdp"):
        bit = 1
        while bit < lax.axis_size(name):
            array = array + flip(array, name, bit)
            bit *= 2
    return array


def nt_dot(left_side, right_side):
    return lax.dot_general(
        left_side, right_side, (((1,), (1,)), ((), ())), preferred_element_type=jnp.float32
    )


def nn_dot(left_side, right_side):
    return jnp.dot(left_side, right_side, preferred_element_type=jnp.float32)


def unit_rows(raw):
    inverse = lax.rsqrt(jnp.mean(raw * raw, axis=-1, keepdims=True) + EPSILON)
    return raw * inverse, inverse


def turn(array, half_size):
    return pltpu.roll(array, half_size, 1)


def attend_kernel(scale, raw_ref, cosine_ref, sine_ref, gain_ref, key_ref, value_ref, bias_ref, out_ref):
    half_size = raw_ref.shape[1] // 2
    unit, _ = unit_rows(raw_ref[...])
    scaled = unit * gain_ref[...]
    query = scaled * cosine_ref[...] + turn(scaled, half_size) * sine_ref[...]
    scores = nt_dot(key_ref[...], query.astype(jnp.bfloat16)) * scale + bias_ref[...]
    raised = jnp.exp(scores - jnp.max(scores, axis=0, keepdims=True))
    probs = (raised / jnp.sum(raised, axis=0, keepdims=True)).astype(jnp.bfloat16)
    out_ref[...] = nn_dot(value_ref[...], probs).T.astype(jnp.bfloat16)


def attend(projected, cosine, sine, gain, keys, values_turned, bias, heads, scale):
    rows, size = cosine.shape
    length = keys.shape[0]
    whole = lambda shape: pl.BlockSpec(shape, lambda head: (0, 0))
    by_head = pl.BlockSpec((rows, size), lambda head: (0, head))
    return pl.pallas_call(
        functools.partial(attend_kernel, scale),
        grid=(heads,),
        in_specs=[
            by_head,
            whole((rows, size)),
            whole((rows, size)),
            whole((1, size)),
            whole((length, size)),
            whole((size, length)),
            whole((length, rows)),
        ],
        out_specs=by_head,
        out_shape=jax.ShapeDtypeStruct((rows, heads * size), jnp.bfloat16),
        compiler_params=pltpu.CompilerParams(vmem_limit_bytes=VMEM_BYTES),
        cost_estimate=pl.CostEstimate(
            flops=8 * heads * rows * length * size,
            bytes_accessed=8 * heads * rows * size + 4 * rows * length,
            transcendentals=heads * rows * length,
        ),
        name="attend",
    )(projected, cosine, sine, gain, keys, values_turned, bias)


def attend_back_kernel(
    scale,
    raw_ref,
    cosine_ref,
    sine_ref,
    gain_ref,
    key_ref,
    key_turned_ref,
    value_ref,
    bias_ref,
    grad_ref,
    raw_grad_ref,
    key_grad_ref,
    value_grad_ref,
    gain_grad_ref,
):
    half_size = raw_ref.shape[1] // 2
    first = pl.program_id(0) == 0
    unit, inverse = unit_rows(raw_ref[...])
    scaled = unit * gain_ref[...]
    query = (scaled * cosine_ref[...] + turn(scaled, half_size) * sine_ref[...]).astype(
        jnp.bfloat16
    )
    out_grad = grad_ref[...]
    scores = nt_dot(key_ref[...], query) * scale + bias_ref[...]
    raised = jnp.exp(scores - jnp.max(scores, axis=0, keepdims=True))
    probs = raised / jnp.sum(raised, axis=0, keepdims=True)
    prob_grad = nt_dot(value_ref[...], out_grad)
    weighted = probs * prob_grad
    score_grad = (weighted - probs * jnp.sum(weighted, axis=0, keepdims=True)).astype(jnp.bfloat16)
    key_part = nn_dot(score_grad, query) * scale
    value_part = nn_dot(probs.astype(jnp.bfloat16), out_grad)
    query_grad = (nn_dot(key_turned_ref[...], score_grad) * scale).T
    scaled_grad = query_grad * cosine_ref[...] + turn(query_grad * sine_ref[...], half_size)
    gain_part = jnp.sum(
        (scaled_grad * unit).reshape(-1, 8, scaled_grad.shape[1]), axis=0
    )
    unit_grad = scaled_grad * gain_ref[...]
    raw_grad = inverse * (unit_grad - unit * jnp.mean(unit_grad * unit, axis=-1, keepdims=True))
    raw_grad_ref[...] = raw_grad.astype(jnp.bfloat16)

    @pl.when(first)
    def _():
        key_grad_ref[...] = key_part
        value_grad_ref[...] = value_part
        gain_grad_ref[...] = gain_part

    @pl.when(jnp.logical_not(first))
    def _():
        key_grad_ref[...] += key_part
        value_grad_ref[...] += value_part
        gain_grad_ref[...] += gain_part


def attend_back(projected, cosine, sine, gain, keys, values, bias, grads, heads, scale):
    rows, size = cosine.shape
    length = keys.shape[0]
    whole = lambda shape: pl.BlockSpec(shape, lambda head: (0, 0))
    by_head = pl.BlockSpec((rows, size), lambda head: (0, head))
    return pl.pallas_call(
        functools.partial(attend_back_kernel, scale),
        grid=(heads,),
        in_specs=[
            by_head,
            whole((rows, size)),
            whole((rows, size)),
            whole((1, size)),
            whole((length, size)),
            whole((size, length)),
            whole((length, size)),
            whole((length, rows)),
            by_head,
        ],
        out_specs=[by_head, whole((length, size)), whole((length, size)), whole((8, size))],
        out_shape=[
            jax.ShapeDtypeStruct((rows, heads * size), jnp.bfloat16),
            jax.ShapeDtypeStruct((length, size), jnp.float32),
            jax.ShapeDtypeStruct((length, size), jnp.float32),
            jax.ShapeDtypeStruct((8, size), jnp.float32),
        ],
        compiler_params=pltpu.CompilerParams(vmem_limit_bytes=VMEM_BYTES),
        cost_estimate=pl.CostEstimate(
            flops=20 * heads * rows * length * size,
            bytes_accessed=8 * heads * rows * size + 4 * rows * length,
            transcendentals=heads * rows * length,
        ),
        name="attend_back",
    )(projected, cosine, sine, gain, keys, keys.T, values, bias, grads)


def experts_kernel(
    local_experts,
    chunks,
    gate_lanes,
    first_ref,
    token_ref,
    gate_ref,
    grad_ref,
    weight_ref,
    result_ref,
    back_ref,
    active_ref,
    slope_ref,
    result_sum,
    back_sum,
    dot_sum,
):
    chunk = pl.program_id(1)
    expert = first_ref[0] + lax.rem(chunk, local_experts)
    units = weight_ref.shape[2]
    width = token_ref.shape[1]
    inward = weight_ref[0, :2].reshape(2 * units, width)
    outward = weight_ref[0, 2]
    gate_up = nt_dot(token_ref[...], inward)
    down_back = nt_dot(grad_ref[...], outward)
    lanes = lax.broadcasted_iota(jnp.int32, gate_ref.shape, 1)
    here = (lanes == expert) | (lanes == expert + gate_lanes)
    gate = jnp.sum(
        jnp.where(here, gate_ref[...].astype(jnp.float32), 0.0), axis=-1, keepdims=True
    )
    gate_half, up_half = gate_up[:, :units], gate_up[:, units:]
    sigmoid = jax.nn.sigmoid(gate_half)
    silu = gate_half * sigmoid
    active = silu * up_half
    scaled_active = active * gate
    act_grad = down_back * gate
    gate_slope = act_grad * up_half * (sigmoid + silu * (1.0 - sigmoid))
    slopes = jnp.concatenate([gate_slope, act_grad * silu], axis=1)
    gate_dot = jnp.sum(active * down_back, axis=-1, keepdims=True)
    dots = jnp.where(lanes == expert, gate_dot, 0.0)
    low_active = scaled_active.astype(jnp.bfloat16)
    low_slopes = slopes.astype(jnp.bfloat16)
    active_ref[...] = low_active.T
    slope_ref[...] = low_slopes.T
    result = nn_dot(low_active, outward)
    back = nn_dot(low_slopes, inward)

    @pl.when(chunk == 0)
    def _():
        result_sum[...] = result
        back_sum[...] = back
        dot_sum[...] = dots

    @pl.when((chunk > 0) & (chunk < chunks - 1))
    def _():
        result_sum[...] += result
        back_sum[...] += back
        dot_sum[...] += dots

    @pl.when(chunk == chunks - 1)
    def _():
        result_ref[...] = (result_sum[...] + result).astype(jnp.bfloat16)
        back_ref[:, :width] = (back_sum[...] + back).astype(jnp.bfloat16)
        back_ref[:, width:] = (dot_sum[...] + dots).astype(jnp.bfloat16)


def run_experts(first_expert, tokens, grads, weights, local_experts, gate_lanes):
    rows, width = grads.shape
    lanes = tokens.shape[1] - width
    chunks, _, units, _ = weights.shape
    block = min(512, rows)
    return pl.pallas_call(
        functools.partial(experts_kernel, local_experts, chunks, gate_lanes),
        grid_spec=pltpu.PrefetchScalarGridSpec(
            num_scalar_prefetch=1,
            grid=(rows // block, chunks),
            in_specs=[
                pl.BlockSpec((block, width), lambda row, chunk, first: (row, 0)),
                pl.BlockSpec((block, lanes), lambda row, chunk, first: (row, width // lanes)),
                pl.BlockSpec((block, width), lambda row, chunk, first: (row, 0)),
                pl.BlockSpec((1, 3, units, width), lambda row, chunk, first: (chunk, 0, 0, 0)),
            ],
            out_specs=[
                pl.BlockSpec((block, width), lambda row, chunk, first: (row, 0)),
                pl.BlockSpec((block, width + lanes), lambda row, chunk, first: (row, 0)),
                pl.BlockSpec((units, block), lambda row, chunk, first: (chunk, row)),
                pl.BlockSpec((2 * units, block), lambda row, chunk, first: (chunk, row)),
            ],
            scratch_shapes=[
                pltpu.VMEM((block, width), jnp.float32),
                pltpu.VMEM((block, width), jnp.float32),
                pltpu.VMEM((block, lanes), jnp.float32),
            ],
        ),
        out_shape=[
            jax.ShapeDtypeStruct((rows, width), jnp.bfloat16),
            jax.ShapeDtypeStruct((rows, width + lanes), jnp.bfloat16),
            jax.ShapeDtypeStruct((chunks * units, rows), jnp.bfloat16),
            jax.ShapeDtypeStruct((2 * chunks * units, rows), jnp.bfloat16),
        ],
        compiler_params=pltpu.CompilerParams(vmem_limit_bytes=VMEM_BYTES),
        cost_estimate=pl.CostEstimate(
            flops=12 * rows * width * chunks * units,
            bytes_accessed=2 * weights.size * (rows // block) + 10 * rows * width,
            transcendentals=rows * chunks * units,
        ),
        name="experts",
    )(first_expert.reshape(1), tokens, tokens, grads, weights)


def expert_grads_kernel(local_experts, sides, slope_ref, active_ref, token_ref, grad_ref, out_ref):
    hidden_units = active_ref.shape[0] // (local_experts * sides)
    inward = nn_dot(slope_ref[...], token_ref[...]).astype(jnp.bfloat16)
    outward = nn_dot(active_ref[...], grad_ref[...]).astype(jnp.bfloat16)
    for expert in range(local_experts):
        for side in range(sides):
            for kind in range(3):
                place = ((side * local_experts + expert) * 3 + kind) * hidden_units
                if kind < 2:
                    start = ((expert * 2 + kind) * sides + side) * hidden_units
                    rows = inward[start : start + hidden_units]
                else:
                    start = (expert * sides + side) * hidden_units
                    rows = outward[start : start + hidden_units]
                out_ref[0, place : place + hidden_units] = rows


def expert_grads(part, slopes, actives, tokens, grads, local_experts, sides, blocks):
    rows, width = grads.shape
    block = width // blocks
    units = actives.shape[0] // 2
    return pl.pallas_call(
        functools.partial(expert_grads_kernel, local_experts, sides),
        grid=(blocks,),
        in_specs=[
            pl.BlockSpec((2 * units, rows), lambda column: (part, 0)),
            pl.BlockSpec((units, rows), lambda column: (part, 0)),
            pl.BlockSpec((rows, block), lambda column: (0, column)),
            pl.BlockSpec((rows, block), lambda column: (0, column)),
        ],
        out_specs=pl.BlockSpec((1, 3 * units, block), lambda column: (column, 0, 0)),
        out_shape=jax.ShapeDtypeStruct((blocks, 3 * units, block), jnp.bfloat16),
        compiler_params=pltpu.CompilerParams(vmem_limit_bytes=VMEM_BYTES),
        cost_estimate=pl.CostEstimate(
            flops=6 * units * rows * width,
            bytes_accessed=6 * units * (rows + width) + 4 * rows * width,
            transcendentals=0,
        ),
        name="expert_grads",
    )(slopes, actives, tokens, grads)


def expert_parallel_shards(
    inputs,
    attn_gain,
    joined_projection_weight,
    q_gain,
    k_gain,
    w_o,
    moe_gain,
    router,
    w_experts,
    segments,
    experts,
    out_grad,
):
    tok_rows, model_width = inputs.shape
    head_size = q_gain.shape[0]
    half_size = head_size // 2
    tensor_size = lax.axis_size("tensor")
    heads = QUERY_HEADS // KEY_VALUE_HEADS
    expert_count = router.shape[1]
    spread_size = lax.axis_size(SPREAD)
    local_experts = expert_count // spread_size
    hidden_units = w_experts.shape[3]
    slice_rows = w_experts.shape[0]
    own_rows = tok_rows // tensor_size
    sides = tensor_size // 2
    context_place = lax.axis_index("context")
    own_start = lax.axis_index("tensor") * own_rows
    first_expert = lax.axis_index(SPREAD) * local_experts
    gain_attn = attn_gain.astype(jnp.float32)
    gain_moe = moe_gain.astype(jnp.float32)
    gain_query = q_gain.astype(jnp.float32)[None]
    gain_key = k_gain.astype(jnp.float32)
    score_scale = head_size ** (-0.5)

    attn_in = lax.all_gather(joined_projection_weight, SPREAD, axis=0, tiled=True)
    attn_out = lax.all_gather(w_o, SPREAD, axis=0, tiled=True)
    own_grad = lax.dynamic_slice_in_dim(out_grad, own_start, own_rows)
    all_grads = spread_gather(own_grad)

    sent_weights = jnp.transpose(w_experts, (1, 2, 3, 0)).reshape(
        spread_size, local_experts, 3, hidden_units, slice_rows
    )
    expert_weights = []
    for expert in range(local_experts):
        own_part = lax.all_to_all(sent_weights[:, expert], SPREAD, 0, 0, tiled=True)
        side_parts = own_part[None]
        for bit in partner_bits()[:-1]:
            side_parts = jnp.concatenate([side_parts, flip(side_parts, "tensor", bit)], axis=0)
        expert_weights.append(jnp.stack([side_parts, flip(side_parts, "tensor", 1)]))
    weights = (
        jnp.stack(expert_weights, axis=1)
        .transpose(0, 1, 4, 2, 5, 3, 6)
        .reshape(2 * local_experts, 3, sides * hidden_units, model_width)
    )

    ordered = own_first(inputs)
    own_index = own_first(jnp.arange(tok_rows, dtype=jnp.int32))
    own_tokens = context_place * tok_rows + own_index
    all_tokens = jnp.concatenate([own_tokens, (1 - context_place) * tok_rows + own_index])
    token_segments = jnp.take(segments, all_tokens)
    positions = jnp.take(doc_positions(segments), own_tokens)
    allowed = (token_segments[:, None] == token_segments[None, :tok_rows]) & (
        all_tokens[:, None] <= own_tokens[None, :]
    )
    bias = jnp.where(allowed, 0.0, NEGATIVE).astype(jnp.float32)
    inverse_angles = ROPE_THETA ** (
        -2.0 * jnp.arange(half_size, dtype=jnp.float32) / head_size
    )
    angles = positions.astype(jnp.float32)[:, None] * inverse_angles[None, :]
    cosine = jnp.concatenate([jnp.cos(angles)] * 2, axis=-1)
    half_sine = jnp.sin(angles)
    sine = jnp.concatenate([-half_sine, half_sine], axis=-1)

    residual = ordered.astype(jnp.float32)
    inverse_attn = lax.rsqrt(jnp.mean(residual * residual, axis=-1, keepdims=True) + EPSILON)
    normalized_input = (residual * inverse_attn * gain_attn).astype(jnp.bfloat16)
    projected = nn_dot(normalized_input, attn_in)
    key_raw = projected[:, heads * head_size : (heads + 1) * head_size]
    value_raw = projected[:, (heads + 1) * head_size :]

    def prepare_key(raw, gain):
        scaled = norm_rows(raw, gain)
        swapped = jnp.concatenate([scaled[:, half_size:], scaled[:, :half_size]], axis=-1)
        return scaled * cosine + swapped * sine

    key_values = jnp.concatenate([prepare_key(key_raw, gain_key), value_raw], axis=-1).astype(
        jnp.bfloat16
    )
    pairs = jnp.concatenate([key_values, flip(key_values, "context", 1)], axis=0)
    keys, values = pairs[:, :head_size], pairs[:, head_size:]
    attended = attend(
        projected, cosine, sine, gain_query, keys, values.T, bias, heads, score_scale
    )
    half_rows = tok_rows // 2
    attn_sum = tensor_scatter_rows(
        lambda half: nt_dot(
            attended[half * half_rows : (half + 1) * half_rows], attn_out
        ).astype(jnp.bfloat16)
    )

    own_inputs = ordered[:own_rows].astype(jnp.float32)
    own_experts = lax.dynamic_slice_in_dim(experts, own_start, own_rows)
    hidden_state = own_inputs + attn_sum.astype(jnp.float32)
    inverse_moe = lax.rsqrt(jnp.mean(hidden_state * hidden_state, axis=-1, keepdims=True) + EPSILON)
    unit_moe = hidden_state * inverse_moe
    mixed_in = (unit_moe * gain_moe).astype(jnp.bfloat16)
    logits = nn_dot(mixed_in, router)
    expert_ids = jnp.arange(expert_count, dtype=jnp.int32)
    picked = jnp.any(own_experts[:, :, None] == expert_ids[None, None, :], axis=1)
    peak = jnp.max(jnp.where(picked, logits, -jnp.inf), axis=-1, keepdims=True)
    raised_gate = jnp.where(picked, jnp.exp(jnp.minimum(logits - peak, 0.0)), 0.0)
    gate_values = raised_gate / jnp.sum(raised_gate, axis=-1, keepdims=True)
    gate_high = gate_values.astype(jnp.bfloat16)
    gate_low = (gate_values - gate_high.astype(jnp.float32)).astype(jnp.bfloat16)
    lane_pad = 128 - 2 * expert_count
    payload = jnp.concatenate(
        [mixed_in, gate_high, gate_low, jnp.zeros((own_rows, lane_pad), jnp.bfloat16)], axis=1
    )
    tokens = lax.all_gather(payload, SPREAD, axis=0, tiled=True)

    results, backs, actives, slopes = run_experts(
        first_expert, tokens, all_grads, weights, local_experts, expert_count
    )
    back_total = lax.psum_scatter(backs, SPREAD, scatter_dimension=0, tiled=True)
    moe_sum = spread_scatter(results)
    own_output = (hidden_state + moe_sum).astype(jnp.bfloat16)
    output = own_back(tensor_gather_rows(own_output))

    other_part = expert_grads(
        1, slopes, actives, tokens, all_grads, local_experts, sides, spread_size
    )
    own_part = expert_grads(
        0, slopes, actives, tokens, all_grads, local_experts, sides, spread_size
    )
    weight_sum = add_low(own_part, flip(other_part, "tensor", 1))
    for bit in partner_bits()[-2::-1]:
        rows = weight_sum.shape[1] // 2
        weight_sum = add_low(
            weight_sum[:, :rows], flip(weight_sum[:, rows:], "tensor", bit)
        )
    w_experts_grad = (
        lax.all_to_all(weight_sum, SPREAD, 0, 0, tiled=True)
        .reshape(expert_count, 3, hidden_units, slice_rows)
        .astype(jnp.float32)
        .transpose(3, 0, 1, 2)
    )

    cotangent = own_grad.astype(jnp.float32)
    gate_dot = back_total[:, model_width : model_width + expert_count].astype(jnp.float32)
    logit_grad = (
        gate_values * (gate_dot - jnp.sum(gate_values * gate_dot, axis=-1, keepdims=True))
    ).astype(jnp.bfloat16)
    router_term = outer_rows(logit_grad, mixed_in)
    moe_back = back_total[:, :model_width].astype(jnp.float32) + nt_dot(logit_grad, router)
    unit_grad = moe_back * gain_moe
    state_grad = cotangent + inverse_moe * (
        unit_grad - unit_moe * jnp.mean(unit_grad * unit_moe, axis=-1, keepdims=True)
    )
    moe_gain_term = jnp.sum(moe_back * unit_moe, axis=0, keepdims=True)
    early_sums = sum_everywhere(jnp.concatenate([router_term, moe_gain_term], axis=0))
    router_grad = early_sums[:expert_count].T
    moe_gain_grad = early_sums[expert_count]
    branch_grad = tensor_gather_rows(state_grad.astype(jnp.bfloat16))
    attended_grad = nn_dot(branch_grad, attn_out).astype(jnp.bfloat16)
    w_o_grad = spread_scatter(outer_rows(branch_grad, attended).astype(jnp.bfloat16))

    query_back, key_grad, value_grad, q_gain_rows = attend_back(
        projected, cosine, sine, gain_query, keys, values, bias, attended_grad, heads, score_scale
    )
    pair_grad = jnp.concatenate([key_grad, value_grad], axis=-1)
    pair_grad = pair_grad[:tok_rows] + flip(
        pair_grad[tok_rows:].astype(jnp.bfloat16), "context", 1
    ).astype(jnp.float32)
    key_back, k_gain_term = jax.vjp(prepare_key, key_raw, gain_key)[1](pair_grad[:, :head_size])
    projected_grad = jnp.concatenate(
        [
            query_back,
            key_back.astype(jnp.bfloat16),
            pair_grad[:, head_size:].astype(jnp.bfloat16),
        ],
        axis=1,
    )
    w_qkv_grad = lax.psum_scatter(
        outer_rows(normalized_input, projected_grad).astype(jnp.bfloat16),
        SPREAD,
        scatter_dimension=0,
        tiled=True,
    ).astype(jnp.float32)
    normed_grad = tensor_scatter_rows(
        lambda half: nt_dot(
            projected_grad[half * half_rows : (half + 1) * half_rows], attn_in
        ).astype(jnp.bfloat16)
    ).astype(jnp.float32)
    own_inverse = inverse_attn[:own_rows]
    own_unit = own_inputs * own_inverse
    unit_back = normed_grad * gain_attn
    own_inputs_grad = (
        state_grad
        + own_inverse
        * (unit_back - own_unit * jnp.mean(unit_back * own_unit, axis=-1, keepdims=True))
    ).astype(jnp.bfloat16)
    inputs_grad = own_back(tensor_gather_rows(own_inputs_grad))
    attn_gain_term = jnp.sum(normed_grad * own_unit, axis=0)
    late_sums = sum_everywhere(
        jnp.concatenate([attn_gain_term, jnp.sum(q_gain_rows, axis=0), k_gain_term]).reshape(
            -1, head_size
        )
    ).reshape(-1)
    return (
        output,
        inputs_grad,
        late_sums[:model_width],
        w_qkv_grad,
        late_sums[model_width : model_width + head_size],
        late_sums[model_width + head_size :],
        w_o_grad,
        moe_gain_grad,
        router_grad,
        w_experts_grad,
    )


def choose_shards(mesh, arrays):
    sizes = mesh.shape
    spread = sizes["fsdp"] * sizes["context"]
    tok_rows, width = arrays[0].shape
    head_size, expert_count = arrays[3].shape[0], arrays[7].shape[1]
    fits = (
        expert_count % spread == 0
        and 2 * expert_count <= 128
        and tok_rows % (32 * sizes["tensor"]) == 0
        and width % 128 == 0
        and head_size % 128 == 0
        and sizes["tensor"] == KEY_VALUE_HEADS
        and sizes["context"] == 2
        and sizes["fsdp"] & (sizes["fsdp"] - 1) == 0
    )
    return expert_parallel_shards if fits else shards


def solution(mesh):
    def by_shapes(*arrays):
        return choose_shards(mesh, arrays)(*arrays)

    return jax.shard_map(
        by_shapes,
        mesh=mesh,
        in_specs=(
            P(("fsdp", "context"), None),
            P(),
            P(("fsdp", "context"), "tensor"),
            P(),
            P(),
            P(("fsdp", "context"), "tensor"),
            P(),
            P(),
            P(("fsdp", "context"), None, None, "tensor"),
            P("fsdp"),
            P(("fsdp", "context"), None),
            P(("fsdp", "context"), None),
        ),
        out_specs=(
            P(("fsdp", "context"), None),
            P(("fsdp", "context"), None),
            P(),
            P(("fsdp", "context"), "tensor"),
            P(),
            P(),
            P(("fsdp", "context"), "tensor"),
            P(),
            P(),
            P(("fsdp", "context"), None, None, "tensor"),
        ),
        check_vma=False,
    )
```

```python
import functools

import jax
import jax.numpy as jnp
from jax import lax
from jax.experimental import pallas as pl
from jax.experimental.pallas import tpu as pltpu
from jax.sharding import PartitionSpec as P

QUERY_HEADS = 32
KEY_VALUE_HEADS = 4


EPSILON = 1e-06
ROPE_THETA = 1000000.0
NEGATIVE = -1e30
BEST_PRECISION = lax.Precision.HIGHEST


def norm_rows(matrix, scaling):
    return matrix * lax.rsqrt(jnp.mean(matrix * matrix, axis=-1, keepdims=True) + EPSILON) * scaling


def doc_positions(segment_ids):
    index_all = jnp.arange(segment_ids.shape[0], dtype=jnp.int32)
    starts = jnp.concatenate(
        [jnp.ones((1,), jnp.int32), (segment_ids[1:] != segment_ids[:-1]).astype(jnp.int32)]
    )
    return index_all - lax.cummax(index_all * starts, axis=0)


def rotate(tensor_array, positions):
    half_size = tensor_array.shape[-1] // 2
    inverse = ROPE_THETA ** (
        -2.0 * jnp.arange(half_size, dtype=jnp.float32) / tensor_array.shape[-1]
    )
    angles = positions.astype(jnp.float32)[:, None] * inverse[None, :]
    cosine = jnp.concatenate([jnp.cos(angles), jnp.cos(angles)], axis=-1)[:, None, :]
    sine_table = jnp.concatenate([jnp.sin(angles), jnp.sin(angles)], axis=-1)[:, None, :]
    turned = jnp.concatenate(
        [-tensor_array[..., half_size:], tensor_array[..., :half_size]], axis=-1
    )
    return tensor_array * cosine + turned * sine_table


def block_groups(group_sizes, first_row, row_count):
    group_ends = jnp.cumsum(group_sizes)
    begins = group_ends - group_sizes
    clipped_end = jnp.clip(group_ends, first_row, first_row + row_count)
    clipped_begin = jnp.clip(begins, first_row, first_row + row_count)
    return clipped_end - clipped_begin


def times_transposed(left_side, right_side):
    return lax.dot_general(
        left_side, right_side, (((1,), (1,)), ((), ())), preferred_element_type=jnp.float32
    )


def outer_rows(left_side, right_side):
    return lax.dot_general(
        left_side, right_side, (((0,), (0,)), ((), ())), preferred_element_type=jnp.float32
    )


def shards(
    inputs,
    attn_gain,
    joined_projection_weight,
    q_gain,
    k_gain,
    w_o,
    moe_gain,
    router,
    w_experts,
    segments,
    experts,
    out_grad,
):
    tok_rows, model_width = inputs.shape
    head_size = q_gain.shape[0]
    head_groups = KEY_VALUE_HEADS // lax.axis_size("tensor")
    queries_per_group = QUERY_HEADS // KEY_VALUE_HEADS
    local_heads = head_groups * queries_per_group
    top_count = experts.shape[1]
    expert_count = router.shape[1]
    sequence_length = segments.shape[0]
    weight_rows = joined_projection_weight.shape[0]
    span_start = lax.axis_index("context") * tok_rows
    first_tensor = (lax.axis_index("tensor") == 0).astype(jnp.float32)
    gain_attn = attn_gain.astype(jnp.float32)
    gain_moe = moe_gain.astype(jnp.float32)
    gain_query = q_gain.astype(jnp.float32)
    gain_key = k_gain.astype(jnp.float32)
    token_index = jnp.arange(sequence_length, dtype=jnp.int32)
    positions = lax.dynamic_slice_in_dim(doc_positions(segments), span_start, tok_rows)
    local_segments = lax.dynamic_slice_in_dim(segments, span_start, tok_rows)
    local_index = span_start + jnp.arange(tok_rows, dtype=jnp.int32)
    rows_per_block = min(512, tok_rows)
    score_scale = head_size ** (-0.5)
    attn_in, attn_out = (
        lax.all_gather(joined_projection_weight, ("fsdp", "context"), axis=0, tiled=True),
        lax.all_gather(w_o, ("fsdp", "context"), axis=0, tiled=True),
    )
    residual = inputs.astype(jnp.float32)
    inverse_attn = lax.rsqrt(jnp.mean(residual * residual, axis=-1, keepdims=True) + EPSILON)
    unit_attn = residual * inverse_attn
    normalized_input = (unit_attn * gain_attn).astype(jnp.bfloat16)
    projected_rows = jnp.dot(normalized_input, attn_in, preferred_element_type=jnp.float32).reshape(
        tok_rows, head_groups, queries_per_group + 2, head_size
    )
    query_raw = projected_rows[:, :, :queries_per_group].reshape(tok_rows, local_heads, head_size)
    key_raw = projected_rows[:, :, queries_per_group]
    value_raw = projected_rows[:, :, queries_per_group + 1]

    def prepare(query_part, key_part, query_gain, key_gain):
        return (
            rotate(norm_rows(query_part, query_gain), positions),
            rotate(norm_rows(key_part, key_gain), positions),
        )

    query_rot, key_rot = prepare(query_raw, key_raw, gain_query, gain_key)
    queries = query_rot.astype(jnp.bfloat16)
    key_values = jnp.concatenate([key_rot, value_raw], axis=-1).astype(jnp.bfloat16)
    gathered_pairs = lax.all_gather(key_values, "context", axis=0, tiled=True)
    all_keys = gathered_pairs[:, :, :head_size]
    all_values = gathered_pairs[:, :, head_size:]

    def block_scores(first_row):
        grouped_heads = queries.reshape(rows_per_block, head_groups, queries_per_group, head_size)
        scores = (
            jnp.einsum(
                "qghd,kgd->ghqk", grouped_heads, all_keys, preferred_element_type=jnp.float32
            )
            * score_scale
        )
        same_doc = local_segments[first_row : first_row + rows_per_block, None] == segments[None, :]
        earlier = local_index[first_row : first_row + rows_per_block, None] >= token_index[None, :]
        return (grouped_heads, jnp.where((same_doc & earlier)[None, None], scores, NEGATIVE))

    first_row = 0
    grouped_heads, scores = block_scores(first_row)
    row_peak = jnp.max(scores, axis=-1, keepdims=True)
    raised = jnp.exp(scores - row_peak)
    summed = jnp.sum(raised, axis=-1, keepdims=True)
    attn_probs = (raised / summed).astype(jnp.bfloat16)
    mixed_block = jnp.einsum(
        "ghqk,kgd->qghd", attn_probs, all_values, preferred_element_type=jnp.float32
    )
    mixed_parts = mixed_block.reshape(rows_per_block, local_heads * head_size)
    log_totals = [row_peak + jnp.log(summed)]
    attended = mixed_parts.astype(jnp.bfloat16)
    attn_sum = lax.psum(times_transposed(attended, attn_out), "tensor")
    hidden_state = residual + attn_sum
    inverse_moe = lax.rsqrt(jnp.mean(hidden_state * hidden_state, axis=-1, keepdims=True) + EPSILON)
    unit_moe = hidden_state * inverse_moe
    mixed_in = (unit_moe * gain_moe).astype(jnp.bfloat16)
    logits = jnp.dot(mixed_in, router, preferred_element_type=jnp.float32)
    chosen = jnp.take_along_axis(logits, experts, axis=1)
    raised_gate = jnp.exp(chosen - jnp.max(chosen, axis=-1, keepdims=True))
    gate_values = raised_gate / jnp.sum(raised_gate, axis=-1, keepdims=True)
    expert_all = lax.all_gather(w_experts, ("fsdp", "context"), axis=0, tiled=True)
    hidden_units = expert_all.shape[3]
    flat_ids = experts.reshape(-1)
    sort_order = jnp.argsort(flat_ids, stable=True)
    undo_order = jnp.argsort(sort_order, stable=True)
    token_of = sort_order // top_count
    expert_ids = jnp.arange(expert_count, dtype=jnp.int32)
    group_sizes = jnp.sum((flat_ids[:, None] == expert_ids[None, :]).astype(jnp.int32), axis=0)
    sorted_inputs = jnp.take(mixed_in, token_of, axis=0)
    sorted_gates = jnp.take(gate_values.reshape(-1), sort_order)
    weights_in = jnp.transpose(expert_all[:, :, :2], (1, 0, 2, 3)).reshape(
        expert_count, model_width, 2 * hidden_units
    )
    weights_out = jnp.transpose(expert_all[:, :, 2], (1, 2, 0))
    assigned = flat_ids.shape[0]
    slab_rows = min(2048, assigned)
    moe_part = jnp.zeros((tok_rows, model_width), jnp.float32)
    gate_up_parts = []
    active_parts = []
    gate_dot_parts = []
    for slab_start in range(0, assigned, slab_rows):
        slab_sizes = block_groups(group_sizes, slab_start, slab_rows)
        slab_tokens = token_of[slab_start : slab_start + slab_rows]
        gate_up = lax.ragged_dot(
            sorted_inputs[slab_start : slab_start + slab_rows],
            weights_in,
            slab_sizes,
            preferred_element_type=jnp.float32,
        )
        gate_half = gate_up[:, :hidden_units]
        active = (gate_half * jax.nn.sigmoid(gate_half) * gate_up[:, hidden_units:]).astype(
            jnp.bfloat16
        )
        outputs = lax.ragged_dot(
            active, weights_out, slab_sizes, preferred_element_type=jnp.float32
        )
        moe_part = moe_part.at[slab_tokens].add(
            outputs * sorted_gates[slab_start : slab_start + slab_rows][:, None]
        )
        gate_dot_parts.append(
            jnp.sum(jnp.take(out_grad, slab_tokens, axis=0).astype(jnp.float32) * outputs, axis=-1)
        )
        gate_up_parts.append(gate_up)
        active_parts.append(active)
    gate_dot_part = jnp.take(jnp.concatenate(gate_dot_parts), undo_order).reshape(
        tok_rows, top_count
    )
    moe_sum, gate_dot = (
        lax.psum(moe_part.astype(jnp.bfloat16), "tensor").astype(jnp.float32),
        lax.psum(gate_dot_part.astype(jnp.bfloat16), "tensor").astype(jnp.float32),
    )
    output = (hidden_state + moe_sum).astype(jnp.bfloat16)
    attn_in, attn_out = (
        lax.all_gather(joined_projection_weight, ("fsdp", "context"), axis=0, tiled=True),
        lax.all_gather(w_o, ("fsdp", "context"), axis=0, tiled=True),
    )
    expert_all = lax.all_gather(w_experts, ("fsdp", "context"), axis=0, tiled=True)
    cotangent = out_grad.astype(jnp.float32)
    gate_slope = gate_values * (gate_dot - jnp.sum(gate_values * gate_dot, axis=-1, keepdims=True))
    picked = (experts[:, :, None] == expert_ids[None, None, :]).astype(jnp.float32)
    logit_grad = jnp.einsum("tk,tke->te", gate_slope, picked, precision=BEST_PRECISION).astype(
        jnp.bfloat16
    )
    router_term = outer_rows(mixed_in, logit_grad) * first_tensor
    router_back = times_transposed(logit_grad, router)
    weights_down = jnp.transpose(expert_all[:, :, 2], (1, 0, 2))
    weights_back = jnp.transpose(expert_all[:, :, :2], (1, 2, 3, 0)).reshape(
        expert_count, 2 * hidden_units, model_width
    )
    back_part = jnp.zeros((tok_rows, model_width), jnp.float32)
    scaled_parts = []
    slope_parts = []
    for slab_index, slab_start in enumerate(range(0, assigned, slab_rows)):
        slab_sizes = block_groups(group_sizes, slab_start, slab_rows)
        slab_tokens = token_of[slab_start : slab_start + slab_rows]
        scaled = (
            jnp.take(out_grad, slab_tokens, axis=0).astype(jnp.float32)
            * sorted_gates[slab_start : slab_start + slab_rows][:, None]
        ).astype(jnp.bfloat16)
        act_grad = lax.ragged_dot(
            scaled, weights_down, slab_sizes, preferred_element_type=jnp.float32
        )
        gate_half = gate_up_parts[slab_index][:, :hidden_units]
        up_half = gate_up_parts[slab_index][:, hidden_units:]
        gate_sigmoid = jax.nn.sigmoid(gate_half)
        gate_up_grad = jnp.concatenate(
            [
                act_grad * up_half * gate_sigmoid * (1.0 + gate_half * (1.0 - gate_sigmoid)),
                act_grad * gate_half * gate_sigmoid,
            ],
            axis=1,
        ).astype(jnp.bfloat16)
        back_part = back_part.at[slab_tokens].add(
            lax.ragged_dot(
                gate_up_grad, weights_back, slab_sizes, preferred_element_type=jnp.float32
            )
        )
        scaled_parts.append(scaled)
        slope_parts.append(gate_up_grad)
    sorted_scaled = jnp.concatenate(scaled_parts, axis=0)
    sorted_slopes = jnp.concatenate(slope_parts, axis=0)
    active_all = jnp.concatenate(active_parts, axis=0)
    numbers = lax.RaggedDotDimensionNumbers(
        dot_dimension_numbers=(([0], [0]), ([], [])),
        lhs_ragged_dimensions=[0],
        rhs_group_dimensions=[],
    )
    grad_in = lax.ragged_dot_general(
        sorted_inputs, sorted_slopes, group_sizes, numbers, preferred_element_type=jnp.float32
    )
    grad_out = lax.ragged_dot_general(
        sorted_scaled, active_all, group_sizes, numbers, preferred_element_type=jnp.float32
    )
    stacked = jnp.concatenate(
        [
            grad_in.reshape(
                expert_count, weight_rows * lax.axis_size(("fsdp", "context")), 2, hidden_units
            ),
            grad_out[:, :, None],
        ],
        axis=2,
    )
    w_experts_grad = lax.psum_scatter(
        jnp.transpose(stacked, (1, 0, 2, 3)).astype(jnp.bfloat16),
        ("fsdp", "context"),
        scatter_dimension=0,
        tiled=True,
    ).astype(jnp.float32)
    moe_back = lax.psum(back_part, "tensor") + router_back
    unit_grad = moe_back * gain_moe
    state_grad = cotangent + inverse_moe * (
        unit_grad - unit_moe * jnp.mean(unit_grad * unit_moe, axis=-1, keepdims=True)
    )
    moe_gain_term = jnp.sum(moe_back * unit_moe, axis=0) * first_tensor
    branch_grad = state_grad.astype(jnp.bfloat16)
    attended_grad = jnp.dot(branch_grad, attn_out, preferred_element_type=jnp.float32).astype(
        jnp.bfloat16
    )
    w_o_grad = lax.psum_scatter(
        outer_rows(branch_grad, attended).astype(jnp.bfloat16),
        ("fsdp", "context"),
        scatter_dimension=0,
        tiled=True,
    ).astype(jnp.float32)
    key_grad = jnp.zeros((sequence_length, head_groups, head_size), jnp.float32)
    value_grad = jnp.zeros((sequence_length, head_groups, head_size), jnp.float32)
    query_parts = []
    for block_number, first_row in enumerate(range(0, tok_rows, rows_per_block)):
        grouped_heads, scores = block_scores(first_row)
        attn_probs = jnp.exp(scores - log_totals[block_number])
        attn_low = attn_probs.astype(jnp.bfloat16)
        mixed_grad = attended_grad.reshape(
            rows_per_block, head_groups, queries_per_group, head_size
        )
        prob_grad = jnp.einsum(
            "qghd,kgd->ghqk", mixed_grad, all_values, preferred_element_type=jnp.float32
        )
        score_grad = (
            attn_probs * (prob_grad - jnp.sum(attn_probs * prob_grad, axis=-1, keepdims=True))
        ).astype(jnp.bfloat16)
        block_of_queries = (
            jnp.einsum("ghqk,kgd->qghd", score_grad, all_keys, preferred_element_type=jnp.float32)
            * score_scale
        )
        query_parts.append(block_of_queries.reshape(rows_per_block, local_heads, head_size))
        key_grad = (
            jnp.einsum(
                "ghqk,qghd->kgd", score_grad, grouped_heads, preferred_element_type=jnp.float32
            )
            * score_scale
        )
        value_grad = jnp.einsum(
            "ghqk,qghd->kgd", attn_low, mixed_grad, preferred_element_type=jnp.float32
        )
    pair_grad = lax.psum_scatter(
        jnp.concatenate([key_grad, value_grad], axis=-1).astype(jnp.bfloat16),
        "context",
        scatter_dimension=0,
        tiled=True,
    ).astype(jnp.float32)
    query_grad = query_parts[0]
    pullback = jax.vjp(prepare, query_raw, key_raw, gain_query, gain_key)[1]
    query_back, key_back, q_gain_term, k_gain_term = pullback(
        (query_grad, pair_grad[:, :, :head_size])
    )
    projected_grad = (
        jnp.concatenate(
            [
                query_back.reshape(tok_rows, head_groups, queries_per_group, head_size),
                key_back[:, :, None],
                pair_grad[:, :, None, head_size:],
            ],
            axis=2,
        )
        .reshape(tok_rows, -1)
        .astype(jnp.bfloat16)
    )
    normed_grad = lax.psum(
        times_transposed(projected_grad, attn_in).astype(jnp.bfloat16), "tensor"
    ).astype(jnp.float32)
    w_qkv_grad = lax.psum_scatter(
        outer_rows(normalized_input, projected_grad).astype(jnp.bfloat16),
        ("fsdp", "context"),
        scatter_dimension=0,
        tiled=True,
    ).astype(jnp.float32)
    unit_back = normed_grad * gain_attn
    inputs_grad = (
        state_grad
        + inverse_attn
        * (unit_back - unit_attn * jnp.mean(unit_back * unit_attn, axis=-1, keepdims=True))
    ).astype(jnp.bfloat16)
    attn_gain_term = jnp.sum(normed_grad * unit_attn, axis=0) * first_tensor
    attn_gain_grad, q_gain_grad, k_gain_grad, moe_gain_grad, router_grad = lax.psum(
        (attn_gain_term, q_gain_term, k_gain_term, moe_gain_term, router_term),
        ("fsdp", "context", "tensor"),
    )
    return (
        output,
        inputs_grad,
        attn_gain_grad,
        w_qkv_grad,
        q_gain_grad,
        k_gain_grad,
        w_o_grad,
        moe_gain_grad,
        router_grad,
        w_experts_grad,
    )


SPREAD = ("fsdp", "context")
VMEM_BYTES = 60 * 2**20


def flip_pairs(size, bit):
    return [(place, place ^ bit) for place in range(size)]


def flip(array, name, bit):
    return lax.ppermute(array, name, flip_pairs(lax.axis_size(name), bit))


def nothing_kernel(*refs):
    pass


def after(array, *others):
    anywhere = pl.BlockSpec(memory_space=pl.ANY)
    return pl.pallas_call(
        nothing_kernel,
        in_specs=[anywhere] * (1 + len(others)),
        out_specs=anywhere,
        out_shape=jax.ShapeDtypeStruct(array.shape, array.dtype),
        input_output_aliases={0: 0},
        name="after",
    )(array, *others)


def add_low(left_side, right_side):
    return (left_side.astype(jnp.float32) + right_side.astype(jnp.float32)).astype(jnp.bfloat16)


def partner_bits():
    size = lax.axis_size("tensor")
    return [size >> step for step in range(1, size.bit_length())]


def partner_order():
    order = [0]
    for bit in partner_bits():
        order = order + [offset ^ bit for offset in order]
    return order


def own_first(array):
    place = lax.axis_index("tensor")
    rows = array.shape[0] // lax.axis_size("tensor")
    return jnp.concatenate(
        [
            lax.dynamic_slice_in_dim(array, (place ^ offset) * rows, rows)
            for offset in partner_order()
        ],
        axis=0,
    )


def own_back(array):
    place = lax.axis_index("tensor")
    order = partner_order()
    rows = array.shape[0] // len(order)
    slot_of = jnp.array([order.index(offset) for offset in range(len(order))], jnp.int32)
    return jnp.concatenate(
        [
            lax.dynamic_slice_in_dim(array, slot_of[place ^ block] * rows, rows)
            for block in range(len(order))
        ],
        axis=0,
    )


def tensor_gather_rows(piece):
    for bit in partner_bits():
        piece = jnp.concatenate([piece, flip(piece, "tensor", bit)], axis=0)
    return piece


def tensor_scatter_rows(half_of):
    bits = partner_bits()
    theirs = flip(half_of(1), "tensor", bits[-1])
    total = add_low(half_of(0), theirs)
    for bit in bits[-2::-1]:
        rows = total.shape[0] // 2
        total = add_low(total[:rows], flip(total[rows:], "tensor", bit))
    return total


def shift(array, step):
    size = lax.axis_size("fsdp")
    return lax.ppermute(array, "fsdp", [(start, (start + step) % size) for start in range(size)])


def spread_pieces(piece, waits=()):
    pairs = []
    for step in range(lax.axis_size("fsdp")):
        if step:
            if step <= len(waits):
                piece = after(piece, *waits[step - 1])
            piece = shift(piece, 1)
        pairs.append((piece, flip(piece, "context", 1)))
    return pairs


def step_place(step):
    return (lax.axis_index("fsdp") - step) % lax.axis_size("fsdp")


def pair_places(step):
    column = 2 * step_place(step)
    side = lax.axis_index("context")
    return column + side, column + 1 - side


def in_order(pairs):
    rows, columns = pairs[0][0].shape
    whole = jnp.zeros((2 * len(pairs) * rows, columns), pairs[0][0].dtype)
    for step, pair in enumerate(pairs):
        for place, piece in zip(pair_places(step), pair):
            whole = lax.dynamic_update_slice_in_dim(whole, piece, place * rows, 0)
    return whole


def context_scatter(array, *earlier):
    place = lax.axis_index("context")
    blocks = array.reshape(lax.axis_size("fsdp"), 2, -1, array.shape[1])
    mine = lax.dynamic_index_in_dim(blocks, place, 1, keepdims=False)
    theirs = lax.dynamic_index_in_dim(blocks, 1 - place, 1, keepdims=False)
    if earlier:
        mine = after(mine, *earlier)
    return add_low(mine, flip(theirs, "context", 1))


def sum_everywhere(array):
    for name in ("tensor", "context", "fsdp"):
        bit = 1
        while bit < lax.axis_size(name):
            array = array + flip(array, name, bit)
            bit *= 2
    return array


def nt_dot(left_side, right_side):
    return lax.dot_general(
        left_side, right_side, (((1,), (1,)), ((), ())), preferred_element_type=jnp.float32
    )


def nn_dot(left_side, right_side):
    return jnp.dot(left_side, right_side, preferred_element_type=jnp.float32)


def unit_rows(raw):
    inverse = lax.rsqrt(jnp.mean(raw * raw, axis=-1, keepdims=True) + EPSILON)
    return raw * inverse, inverse


def turn(array, half_size):
    return pltpu.roll(array, half_size, 1)


def attend_kernel(scale, raw_ref, cosine_ref, sine_ref, gain_ref, key_ref, value_ref, bias_ref, out_ref):
    half_size = raw_ref.shape[1] // 2
    unit, _ = unit_rows(raw_ref[...])
    scaled = unit * gain_ref[...]
    query = scaled * cosine_ref[...] + turn(scaled, half_size) * sine_ref[...]
    scores = nt_dot(key_ref[...], query.astype(jnp.bfloat16)) * scale + bias_ref[...]
    raised = jnp.exp(scores - jnp.max(scores, axis=0, keepdims=True))
    probs = (raised / jnp.sum(raised, axis=0, keepdims=True)).astype(jnp.bfloat16)
    out_ref[...] = nn_dot(value_ref[...], probs).T.astype(jnp.bfloat16)


def attend(projected, cosine, sine, gain, keys, values_turned, bias, heads, scale):
    rows, size = cosine.shape
    length = keys.shape[0]
    whole = lambda shape: pl.BlockSpec(shape, lambda head: (0, 0))
    by_head = pl.BlockSpec((rows, size), lambda head: (0, head))
    return pl.pallas_call(
        functools.partial(attend_kernel, scale),
        grid=(heads,),
        in_specs=[
            by_head,
            whole((rows, size)),
            whole((rows, size)),
            whole((1, size)),
            whole((length, size)),
            whole((size, length)),
            whole((length, rows)),
        ],
        out_specs=by_head,
        out_shape=jax.ShapeDtypeStruct((rows, heads * size), jnp.bfloat16),
        compiler_params=pltpu.CompilerParams(vmem_limit_bytes=VMEM_BYTES),
        cost_estimate=pl.CostEstimate(
            flops=8 * heads * rows * length * size,
            bytes_accessed=8 * heads * rows * size + 4 * rows * length,
            transcendentals=heads * rows * length,
        ),
        name="attend",
    )(projected, cosine, sine, gain, keys, values_turned, bias)


def attend_back_kernel(
    scale,
    raw_ref,
    cosine_ref,
    sine_ref,
    gain_ref,
    key_ref,
    key_turned_ref,
    value_ref,
    bias_ref,
    grad_ref,
    raw_grad_ref,
    key_grad_ref,
    value_grad_ref,
    gain_grad_ref,
):
    half_size = raw_ref.shape[1] // 2
    first = pl.program_id(0) == 0
    unit, inverse = unit_rows(raw_ref[...])
    scaled = unit * gain_ref[...]
    query = (scaled * cosine_ref[...] + turn(scaled, half_size) * sine_ref[...]).astype(
        jnp.bfloat16
    )
    out_grad = grad_ref[...]
    scores = nt_dot(key_ref[...], query) * scale + bias_ref[...]
    raised = jnp.exp(scores - jnp.max(scores, axis=0, keepdims=True))
    probs = raised / jnp.sum(raised, axis=0, keepdims=True)
    prob_grad = nt_dot(value_ref[...], out_grad)
    weighted = probs * prob_grad
    score_grad = (weighted - probs * jnp.sum(weighted, axis=0, keepdims=True)).astype(jnp.bfloat16)
    key_part = nn_dot(score_grad, query) * scale
    value_part = nn_dot(probs.astype(jnp.bfloat16), out_grad)
    query_grad = (nn_dot(key_turned_ref[...], score_grad) * scale).T
    scaled_grad = query_grad * cosine_ref[...] + turn(query_grad * sine_ref[...], half_size)
    gain_part = jnp.sum(
        (scaled_grad * unit).reshape(-1, 8, scaled_grad.shape[1]), axis=0
    )
    unit_grad = scaled_grad * gain_ref[...]
    raw_grad = inverse * (unit_grad - unit * jnp.mean(unit_grad * unit, axis=-1, keepdims=True))
    raw_grad_ref[...] = raw_grad.astype(jnp.bfloat16)

    @pl.when(first)
    def _():
        key_grad_ref[...] = key_part
        value_grad_ref[...] = value_part
        gain_grad_ref[...] = gain_part

    @pl.when(jnp.logical_not(first))
    def _():
        key_grad_ref[...] += key_part
        value_grad_ref[...] += value_part
        gain_grad_ref[...] += gain_part


def attend_back(projected, cosine, sine, gain, keys, values, bias, grads, heads, scale):
    rows, size = cosine.shape
    length = keys.shape[0]
    whole = lambda shape: pl.BlockSpec(shape, lambda head: (0, 0))
    by_head = pl.BlockSpec((rows, size), lambda head: (0, head))
    return pl.pallas_call(
        functools.partial(attend_back_kernel, scale),
        grid=(heads,),
        in_specs=[
            by_head,
            whole((rows, size)),
            whole((rows, size)),
            whole((1, size)),
            whole((length, size)),
            whole((size, length)),
            whole((length, size)),
            whole((length, rows)),
            by_head,
        ],
        out_specs=[by_head, whole((length, size)), whole((length, size)), whole((8, size))],
        out_shape=[
            jax.ShapeDtypeStruct((rows, heads * size), jnp.bfloat16),
            jax.ShapeDtypeStruct((length, size), jnp.float32),
            jax.ShapeDtypeStruct((length, size), jnp.float32),
            jax.ShapeDtypeStruct((8, size), jnp.float32),
        ],
        compiler_params=pltpu.CompilerParams(vmem_limit_bytes=VMEM_BYTES),
        cost_estimate=pl.CostEstimate(
            flops=20 * heads * rows * length * size,
            bytes_accessed=8 * heads * rows * size + 4 * rows * length,
            transcendentals=heads * rows * length,
        ),
        name="attend_back",
    )(projected, cosine, sine, gain, keys, keys.T, values, bias, grads)


def experts_kernel(
    local_experts,
    sides,
    gate_lanes,
    first_ref,
    token_ref,
    gate_ref,
    grad_ref,
    *refs,
):
    chunks = 2 * local_experts
    parts = refs[: chunks * sides]
    result_ref, back_ref, active_ref, slope_ref = refs[chunks * sides : chunks * sides + 4]
    inward, outward, actives, slopes, sems = refs[chunks * sides + 4 :]
    blocks, _, hidden_units, depth = parts[0].shape
    units = sides * hidden_units
    width = token_ref.shape[1]

    @pl.when(pl.program_id(0) == 0)
    def _():
        for chunk in range(chunks):
            for side in range(sides):
                part = parts[chunk * sides + side]
                for kind in range(3):
                    place = inward if kind < 2 else outward
                    rows = ((chunk * 2 + kind) if kind < 2 else chunk) * units
                    rows = pl.ds(rows + side * hidden_units, hidden_units)
                    for block in range(blocks):
                        pltpu.make_async_copy(
                            part.at[block, kind],
                            place.at[rows, pl.ds(block * depth, depth)],
                            sems.at[chunk, kind // 2],
                        ).start()

    def body(first_step):
        tokens = token_ref[...]
        grads = grad_ref[...]
        lanes = lax.broadcasted_iota(jnp.int32, gate_ref.shape, 1)
        all_gates = gate_ref[...].astype(jnp.float32)
        dots = jnp.zeros(gate_ref.shape, jnp.float32)
        for chunk in range(chunks):
            in_rows = pl.ds(chunk * 2 * units, 2 * units)
            out_rows = pl.ds(chunk * units, units)
            if first_step:
                whole_in, whole_out = inward.at[in_rows], outward.at[out_rows]
                pltpu.make_async_copy(whole_in, whole_in, sems.at[chunk, 0]).wait()
                pltpu.make_async_copy(whole_out, whole_out, sems.at[chunk, 1]).wait()
            expert = first_ref[0] + chunk % local_experts
            gate_up = nt_dot(tokens, inward[in_rows, :])
            down_back = nt_dot(grads, outward[out_rows, :])
            here = (lanes == expert) | (lanes == expert + gate_lanes)
            gate = jnp.sum(jnp.where(here, all_gates, 0.0), axis=-1, keepdims=True)
            gate_half, up_half = gate_up[:, :units], gate_up[:, units:]
            sigmoid = jax.nn.sigmoid(gate_half)
            silu = gate_half * sigmoid
            active = silu * up_half
            act_grad = down_back * gate
            gate_slope = act_grad * up_half * (sigmoid + silu * (1.0 - sigmoid))
            gate_dot = jnp.sum(active * down_back, axis=-1, keepdims=True)
            dots = dots + jnp.where(lanes == expert, gate_dot, 0.0)
            low_active = (active * gate).astype(jnp.bfloat16)
            low_slopes = jnp.concatenate([gate_slope, act_grad * silu], axis=1)
            low_slopes = low_slopes.astype(jnp.bfloat16)
            actives[:, out_rows] = low_active
            slopes[:, in_rows] = low_slopes
            active_ref[out_rows, :] = low_active.T
            slope_ref[in_rows, :] = low_slopes.T
        back_ref[:, :width] = nn_dot(slopes[...], inward[...]).astype(jnp.bfloat16)
        back_ref[:, width:] = dots.astype(jnp.bfloat16)
        result_ref[...] = nn_dot(actives[...], outward[...]).astype(jnp.bfloat16)

    @pl.when(pl.program_id(0) == 0)
    def _():
        body(True)

    @pl.when(pl.program_id(0) > 0)
    def _():
        body(False)


def run_experts(first_expert, tokens, grads, parts, local_experts, gate_lanes):
    rows, width = grads.shape
    lanes = tokens.shape[1] - width
    sides = len(parts) // (2 * local_experts)
    units = 2 * local_experts * sides * parts[0].shape[2]
    block = min(256, rows)
    by_row = lambda columns, place: pl.BlockSpec((block, columns), lambda row, first: (row, place))
    by_column = lambda count: pl.BlockSpec((count, block), lambda row, first: (0, row))
    return pl.pallas_call(
        functools.partial(experts_kernel, local_experts, sides, gate_lanes),
        grid_spec=pltpu.PrefetchScalarGridSpec(
            num_scalar_prefetch=1,
            grid=(rows // block,),
            in_specs=[by_row(width, 0), by_row(lanes, width // lanes), by_row(width, 0)]
            + [pl.BlockSpec(memory_space=pl.ANY)] * len(parts),
            out_specs=[
                by_row(width, 0),
                by_row(width + lanes, 0),
                by_column(units),
                by_column(2 * units),
            ],
            scratch_shapes=[
                pltpu.VMEM((2 * units, width), jnp.bfloat16),
                pltpu.VMEM((units, width), jnp.bfloat16),
                pltpu.VMEM((block, units), jnp.bfloat16),
                pltpu.VMEM((block, 2 * units), jnp.bfloat16),
                pltpu.SemaphoreType.DMA((2 * local_experts, 2)),
            ],
        ),
        out_shape=[
            jax.ShapeDtypeStruct((rows, width), jnp.bfloat16),
            jax.ShapeDtypeStruct((rows, width + lanes), jnp.bfloat16),
            jax.ShapeDtypeStruct((units, rows), jnp.bfloat16),
            jax.ShapeDtypeStruct((2 * units, rows), jnp.bfloat16),
        ],
        compiler_params=pltpu.CompilerParams(vmem_limit_bytes=VMEM_BYTES),
        cost_estimate=pl.CostEstimate(
            flops=12 * rows * width * units,
            bytes_accessed=6 * units * (width + rows) + 8 * rows * width,
            transcendentals=rows * units,
        ),
        name="experts",
    )(first_expert.reshape(1), tokens, tokens, grads, *parts)


def expert_grads_kernel(hidden_units, slope_ref, active_ref, token_ref, grad_ref, *refs):
    sides = active_ref.shape[0] // hidden_units
    depth = refs[-1].shape[2]
    inward = nn_dot(slope_ref[...], token_ref[...])
    outward = nn_dot(active_ref[...], grad_ref[...])
    received, outs = refs[: len(refs) - sides], refs[len(refs) - sides :]
    if len(refs) == 1:
        received, outs = (), refs * sides
    for side in range(sides):
        for kind in range(3):
            start = ((kind * sides if kind < 2 else 0) + side) * hidden_units
            wide = (inward if kind < 2 else outward)[start : start + hidden_units]
            place = kind * hidden_units
            whole = (side * 3 + kind) * hidden_units
            for block in range(refs[-1].shape[0]):
                rows = wide[:, block * depth : (block + 1) * depth]
                if received:
                    more = received[0][block, whole : whole + hidden_units]
                    rows = rows + more.astype(jnp.float32)
                into = place if received else whole
                outs[side][block, into : into + hidden_units] = rows.astype(jnp.bfloat16)


def expert_grads(chunk, slopes, actives, tokens, grads, chunks, sides, blocks, received=None):
    rows, width = grads.shape
    depth = width // blocks
    units = actives.shape[0] // chunks
    step = 2 if blocks % 2 == 0 else 1
    by_block = lambda count: pl.BlockSpec((step, count, depth), lambda column: (column, 0, 0))
    shape = lambda count: jax.ShapeDtypeStruct((blocks, count, depth), jnp.bfloat16)
    alone = received is None
    return pl.pallas_call(
        functools.partial(expert_grads_kernel, units // sides),
        grid=(blocks // step,),
        in_specs=[
            pl.BlockSpec((2 * units, rows), lambda column: (chunk, 0)),
            pl.BlockSpec((units, rows), lambda column: (chunk, 0)),
            pl.BlockSpec((rows, step * depth), lambda column: (0, column)),
            pl.BlockSpec((rows, step * depth), lambda column: (0, column)),
        ]
        + ([] if alone else [by_block(3 * units)]),
        out_specs=by_block(3 * units) if alone else [by_block(3 * units // sides)] * sides,
        out_shape=shape(3 * units) if alone else [shape(3 * units // sides)] * sides,
        compiler_params=pltpu.CompilerParams(vmem_limit_bytes=VMEM_BYTES),
        cost_estimate=pl.CostEstimate(
            flops=6 * units * rows * width,
            bytes_accessed=6 * units * (rows + width) + 4 * rows * width,
            transcendentals=0,
        ),
        name="expert_grads",
    )(slopes, actives, tokens, grads, *([] if alone else [received]))


def expert_parallel_shards(
    inputs,
    attn_gain,
    joined_projection_weight,
    q_gain,
    k_gain,
    w_o,
    moe_gain,
    router,
    w_experts,
    segments,
    experts,
    out_grad,
):
    tok_rows, model_width = inputs.shape
    head_size = q_gain.shape[0]
    half_size = head_size // 2
    tensor_size = lax.axis_size("tensor")
    heads = QUERY_HEADS // KEY_VALUE_HEADS
    expert_count = router.shape[1]
    spread_size = lax.axis_size(SPREAD)
    local_experts = expert_count // spread_size
    hidden_units = w_experts.shape[3]
    slice_rows = w_experts.shape[0]
    own_rows = tok_rows // tensor_size
    context_place = lax.axis_index("context")
    own_start = lax.axis_index("tensor") * own_rows
    first_expert = lax.axis_index(SPREAD) * local_experts
    gain_attn = attn_gain.astype(jnp.float32)
    gain_moe = moe_gain.astype(jnp.float32)
    gain_query = q_gain.astype(jnp.float32)[None]
    gain_key = k_gain.astype(jnp.float32)
    score_scale = head_size ** (-0.5)

    attn_in_pairs = spread_pieces(joined_projection_weight)
    attn_in = in_order(attn_in_pairs)
    attn_out = lax.all_gather(
        after(w_o, attn_in_pairs[len(attn_in_pairs) // 2][0]), SPREAD, axis=0, tiled=True
    )
    own_grad = lax.dynamic_slice_in_dim(out_grad, own_start, own_rows)

    sent_weights = jnp.transpose(w_experts, (1, 2, 3, 0)).reshape(
        spread_size, local_experts, 3, hidden_units, slice_rows
    )
    ordered = own_first(inputs)
    own_index = own_first(jnp.arange(tok_rows, dtype=jnp.int32))
    own_tokens = context_place * tok_rows + own_index
    all_tokens = jnp.concatenate([own_tokens, (1 - context_place) * tok_rows + own_index])
    token_segments = jnp.take(segments, all_tokens)
    positions = jnp.take(doc_positions(segments), own_tokens)
    allowed = (token_segments[:, None] == token_segments[None, :tok_rows]) & (
        all_tokens[:, None] <= own_tokens[None, :]
    )
    bias = jnp.where(allowed, 0.0, NEGATIVE).astype(jnp.float32)
    inverse_angles = ROPE_THETA ** (
        -2.0 * jnp.arange(half_size, dtype=jnp.float32) / head_size
    )
    angles = positions.astype(jnp.float32)[:, None] * inverse_angles[None, :]
    cosine = jnp.concatenate([jnp.cos(angles)] * 2, axis=-1)
    half_sine = jnp.sin(angles)
    sine = jnp.concatenate([-half_sine, half_sine], axis=-1)

    residual = ordered.astype(jnp.float32)
    inverse_attn = lax.rsqrt(jnp.mean(residual * residual, axis=-1, keepdims=True) + EPSILON)
    normalized_input = (residual * inverse_attn * gain_attn).astype(jnp.bfloat16)
    projected = jnp.zeros((tok_rows, joined_projection_weight.shape[1]), jnp.float32)
    for step, pair in enumerate(attn_in_pairs):
        for place, piece in zip(pair_places(step), pair):
            columns = lax.dynamic_slice_in_dim(
                normalized_input, place * slice_rows, slice_rows, axis=1
            )
            projected = projected + nn_dot(columns, piece)
    weight_parts = [
        lax.all_to_all(after(sent_weights[:, 0], projected), SPREAD, 0, 0, tiled=True)
    ]
    key_raw = projected[:, heads * head_size : (heads + 1) * head_size]
    value_raw = projected[:, (heads + 1) * head_size :]

    def prepare_key(raw, gain):
        scaled = norm_rows(raw, gain)
        swapped = jnp.concatenate([scaled[:, half_size:], scaled[:, :half_size]], axis=-1)
        return scaled * cosine + swapped * sine

    key_values = jnp.concatenate([prepare_key(key_raw, gain_key), value_raw], axis=-1).astype(
        jnp.bfloat16
    )
    pairs = jnp.concatenate([key_values, flip(key_values, "context", 1)], axis=0)
    keys, values = pairs[:, :head_size], pairs[:, head_size:]
    attended = attend(
        projected,
        cosine,
        sine,
        gain_query,
        keys,
        values.T,
        bias,
        heads,
        score_scale,
    )
    all_grads = lax.all_gather(after(own_grad, attn_out), SPREAD, axis=0, tiled=True)
    weight_parts = [after(weight_parts[0], attended)]
    for expert in range(1, local_experts):
        sent = after(sent_weights[:, expert], weight_parts[-1])
        weight_parts.append(lax.all_to_all(sent, SPREAD, 0, 0, tiled=True))
    wide_bit, core_bit = partner_bits()
    wide_parts = [flip(part, "tensor", wide_bit) for part in weight_parts]
    half_rows = tok_rows // 2
    attn_sum = tensor_scatter_rows(
        lambda half: nt_dot(
            attended[half * half_rows : (half + 1) * half_rows], attn_out
        ).astype(jnp.bfloat16)
    )

    own_inputs = ordered[:own_rows].astype(jnp.float32)
    own_experts = lax.dynamic_slice_in_dim(experts, own_start, own_rows)
    hidden_state = own_inputs + attn_sum.astype(jnp.float32)
    inverse_moe = lax.rsqrt(jnp.mean(hidden_state * hidden_state, axis=-1, keepdims=True) + EPSILON)
    unit_moe = hidden_state * inverse_moe
    mixed_in = (unit_moe * gain_moe).astype(jnp.bfloat16)
    logits = nn_dot(mixed_in, router)
    expert_ids = jnp.arange(expert_count, dtype=jnp.int32)
    picked = jnp.any(own_experts[:, :, None] == expert_ids[None, None, :], axis=1)
    peak = jnp.max(jnp.where(picked, logits, -jnp.inf), axis=-1, keepdims=True)
    raised_gate = jnp.where(picked, jnp.exp(jnp.minimum(logits - peak, 0.0)), 0.0)
    gate_values = raised_gate / jnp.sum(raised_gate, axis=-1, keepdims=True)
    gate_high = gate_values.astype(jnp.bfloat16)
    gate_low = (gate_values - gate_high.astype(jnp.float32)).astype(jnp.bfloat16)
    lane_pad = 128 - 2 * expert_count
    payload = jnp.concatenate(
        [mixed_in, gate_high, gate_low, jnp.zeros((own_rows, lane_pad), jnp.bfloat16)], axis=1
    )
    tokens = in_order(
        spread_pieces(payload, [(weight_parts[0],), (wide_parts[0],), (weight_parts[-1],)])
    )
    own_parts, other_parts = [], []
    for pair in zip(weight_parts, wide_parts):
        pair = [pair[0], after(pair[1], tokens)]
        own_parts += pair
        other_parts += [flip(array, "tensor", core_bit) for array in pair]

    results, backs, actives, slopes = run_experts(
        first_expert, tokens, all_grads, own_parts + other_parts, local_experts, expert_count
    )
    grads_of = functools.partial(
        expert_grads,
        slopes=slopes,
        actives=actives,
        tokens=tokens,
        grads=all_grads,
        chunks=2 * local_experts,
        sides=len(partner_bits()),
        blocks=spread_size,
    )
    received = [
        flip(grads_of(local_experts + expert), "tensor", core_bit)
        for expert in range(local_experts)
    ]
    own_sums = [
        grads_of(expert, received=received[expert]) for expert in range(local_experts)
    ]
    exchange = lambda sums: add_low(sums[0], flip(sums[1], "tensor", wide_bit))
    expert_sums = [exchange(own_sums[0])]
    result_sum = context_scatter(results)
    back_total = after(
        lax.psum_scatter(backs, SPREAD, scatter_dimension=0, tiled=True),
        expert_sums[0],
        own_sums[-1][0],
        result_sum,
    )
    moe_sum = lax.psum_scatter(after(result_sum, back_total), "fsdp")
    expert_backs = [lax.all_to_all(expert_sums[0], SPREAD, 0, 0, tiled=True)]
    cotangent = own_grad.astype(jnp.float32)
    gate_dot = back_total[:, model_width : model_width + expert_count].astype(jnp.float32)
    logit_grad = (
        gate_values * (gate_dot - jnp.sum(gate_values * gate_dot, axis=-1, keepdims=True))
    ).astype(jnp.bfloat16)
    router_term = outer_rows(logit_grad, mixed_in)
    moe_back = back_total[:, :model_width].astype(jnp.float32) + nt_dot(logit_grad, router)
    unit_grad = moe_back * gain_moe
    state_grad = cotangent + inverse_moe * (
        unit_grad - unit_moe * jnp.mean(unit_grad * unit_moe, axis=-1, keepdims=True)
    )
    moe_gain_term = jnp.sum(moe_back * unit_moe, axis=0, keepdims=True)
    branch_grad = tensor_gather_rows(state_grad.astype(jnp.bfloat16))
    for mine, theirs in own_sums[1:]:
        expert_sums.append(exchange((mine, after(theirs, branch_grad))))
    w_o_part = outer_rows(branch_grad, attended).astype(jnp.bfloat16)
    attended_grad = after(nn_dot(branch_grad, attn_out).astype(jnp.bfloat16), w_o_part)

    query_back, key_grad, value_grad, q_gain_rows = attend_back(
        projected, cosine, sine, gain_query, keys, values, bias, attended_grad, heads, score_scale
    )
    w_o_sum = context_scatter(w_o_part, key_grad)
    for sums in expert_sums[1:]:
        expert_backs.append(
            lax.all_to_all(after(sums, expert_backs[-1]), SPREAD, 0, 0, tiled=True)
        )
    w_experts_grad = (
        jnp.stack(expert_backs, axis=1)
        .reshape(expert_count, 3, hidden_units, slice_rows)
        .astype(jnp.float32)
        .transpose(3, 0, 1, 2)
    )
    w_o_grad = lax.psum_scatter(w_o_sum, "fsdp").astype(jnp.float32)
    pair_grad = jnp.concatenate([key_grad, value_grad], axis=-1)
    sent_pairs = after(
        pair_grad[tok_rows:].astype(jnp.bfloat16), expert_backs[0], *expert_sums[1:]
    )
    pair_grad = pair_grad[:tok_rows] + flip(sent_pairs, "context", 1).astype(jnp.float32)
    key_back, k_gain_term = jax.vjp(prepare_key, key_raw, gain_key)[1](pair_grad[:, :head_size])
    projected_grad = jnp.concatenate(
        [
            query_back,
            key_back.astype(jnp.bfloat16),
            pair_grad[:, head_size:].astype(jnp.bfloat16),
        ],
        axis=1,
    )
    own_output = (
        hidden_state + after(moe_sum, projected_grad).astype(jnp.float32)
    ).astype(jnp.bfloat16)
    output = own_back(tensor_gather_rows(own_output))
    w_qkv_grad = lax.psum_scatter(
        outer_rows(normalized_input, projected_grad).astype(jnp.bfloat16),
        SPREAD,
        scatter_dimension=0,
        tiled=True,
    ).astype(jnp.float32)
    normed_grad = tensor_scatter_rows(
        lambda half: nt_dot(
            projected_grad[half * half_rows : (half + 1) * half_rows], attn_in
        ).astype(jnp.bfloat16)
    ).astype(jnp.float32)
    own_inverse = inverse_attn[:own_rows]
    own_unit = own_inputs * own_inverse
    unit_back = normed_grad * gain_attn
    own_inputs_grad = (
        state_grad
        + own_inverse
        * (unit_back - own_unit * jnp.mean(unit_back * own_unit, axis=-1, keepdims=True))
    ).astype(jnp.bfloat16)
    inputs_grad = own_back(tensor_gather_rows(own_inputs_grad))
    attn_gain_term = jnp.sum(normed_grad * own_unit, axis=0)
    gain_terms = jnp.concatenate([jnp.sum(q_gain_rows, axis=0), k_gain_term])
    sums = sum_everywhere(
        jnp.concatenate(
            [
                router_term,
                moe_gain_term,
                attn_gain_term[None],
                jnp.pad(gain_terms, (0, model_width - gain_terms.shape[0]))[None],
            ],
            axis=0,
        )
    )
    gain_sums = sums[expert_count + 2]
    return (
        output,
        inputs_grad,
        sums[expert_count + 1],
        w_qkv_grad,
        gain_sums[:head_size],
        gain_sums[head_size : 2 * head_size],
        w_o_grad,
        sums[expert_count],
        sums[:expert_count].T,
        w_experts_grad,
    )


def choose_shards(mesh, arrays):
    sizes = mesh.shape
    spread = sizes["fsdp"] * sizes["context"]
    tok_rows, width = arrays[0].shape
    head_size, expert_count = arrays[3].shape[0], arrays[7].shape[1]
    fits = (
        expert_count % spread == 0
        and 2 * expert_count <= 128
        and tok_rows % (32 * sizes["tensor"]) == 0
        and width % 128 == 0
        and head_size % 128 == 0
        and sizes["tensor"] == KEY_VALUE_HEADS
        and sizes["context"] == 2
        and sizes["fsdp"] & (sizes["fsdp"] - 1) == 0
    )
    return expert_parallel_shards if fits else shards


def solution(mesh):
    def by_shapes(*arrays):
        return choose_shards(mesh, arrays)(*arrays)

    return jax.shard_map(
        by_shapes,
        mesh=mesh,
        in_specs=(
            P(("fsdp", "context"), None),
            P(),
            P(("fsdp", "context"), "tensor"),
            P(),
            P(),
            P(("fsdp", "context"), "tensor"),
            P(),
            P(),
            P(("fsdp", "context"), None, None, "tensor"),
            P("fsdp"),
            P(("fsdp", "context"), None),
            P(("fsdp", "context"), None),
        ),
        out_specs=(
            P(("fsdp", "context"), None),
            P(("fsdp", "context"), None),
            P(),
            P(("fsdp", "context"), "tensor"),
            P(),
            P(),
            P(("fsdp", "context"), "tensor"),
            P(),
            P(),
            P(("fsdp", "context"), None, None, "tensor"),
        ),
        check_vma=False,
    )
```

```python
import functools

import jax
import jax.numpy as jnp
from jax import lax
from jax.experimental import pallas as pl
from jax.experimental.pallas import tpu as pltpu
from jax.sharding import PartitionSpec as P

QUERY_HEADS = 32
KEY_VALUE_HEADS = 4


EPSILON = 1e-06
ROPE_THETA = 1000000.0
NEGATIVE = -1e30
BEST_PRECISION = lax.Precision.HIGHEST


def norm_rows(matrix, scaling):
    return matrix * lax.rsqrt(jnp.mean(matrix * matrix, axis=-1, keepdims=True) + EPSILON) * scaling


def doc_positions(segment_ids):
    index_all = jnp.arange(segment_ids.shape[0], dtype=jnp.int32)
    starts = jnp.concatenate(
        [jnp.ones((1,), jnp.int32), (segment_ids[1:] != segment_ids[:-1]).astype(jnp.int32)]
    )
    return index_all - lax.cummax(index_all * starts, axis=0)


def rotate(tensor_array, positions):
    half_size = tensor_array.shape[-1] // 2
    inverse = ROPE_THETA ** (
        -2.0 * jnp.arange(half_size, dtype=jnp.float32) / tensor_array.shape[-1]
    )
    angles = positions.astype(jnp.float32)[:, None] * inverse[None, :]
    cosine = jnp.concatenate([jnp.cos(angles), jnp.cos(angles)], axis=-1)[:, None, :]
    sine_table = jnp.concatenate([jnp.sin(angles), jnp.sin(angles)], axis=-1)[:, None, :]
    turned = jnp.concatenate(
        [-tensor_array[..., half_size:], tensor_array[..., :half_size]], axis=-1
    )
    return tensor_array * cosine + turned * sine_table


def block_groups(group_sizes, first_row, row_count):
    group_ends = jnp.cumsum(group_sizes)
    begins = group_ends - group_sizes
    clipped_end = jnp.clip(group_ends, first_row, first_row + row_count)
    clipped_begin = jnp.clip(begins, first_row, first_row + row_count)
    return clipped_end - clipped_begin


def times_transposed(left_side, right_side):
    return lax.dot_general(
        left_side, right_side, (((1,), (1,)), ((), ())), preferred_element_type=jnp.float32
    )


def outer_rows(left_side, right_side):
    return lax.dot_general(
        left_side, right_side, (((0,), (0,)), ((), ())), preferred_element_type=jnp.float32
    )


def shards(
    inputs,
    attn_gain,
    joined_projection_weight,
    q_gain,
    k_gain,
    w_o,
    moe_gain,
    router,
    w_experts,
    segments,
    experts,
    out_grad,
):
    tok_rows, model_width = inputs.shape
    head_size = q_gain.shape[0]
    head_groups = KEY_VALUE_HEADS // lax.axis_size("tensor")
    queries_per_group = QUERY_HEADS // KEY_VALUE_HEADS
    local_heads = head_groups * queries_per_group
    top_count = experts.shape[1]
    expert_count = router.shape[1]
    sequence_length = segments.shape[0]
    weight_rows = joined_projection_weight.shape[0]
    span_start = lax.axis_index("context") * tok_rows
    first_tensor = (lax.axis_index("tensor") == 0).astype(jnp.float32)
    gain_attn = attn_gain.astype(jnp.float32)
    gain_moe = moe_gain.astype(jnp.float32)
    gain_query = q_gain.astype(jnp.float32)
    gain_key = k_gain.astype(jnp.float32)
    token_index = jnp.arange(sequence_length, dtype=jnp.int32)
    positions = lax.dynamic_slice_in_dim(doc_positions(segments), span_start, tok_rows)
    local_segments = lax.dynamic_slice_in_dim(segments, span_start, tok_rows)
    local_index = span_start + jnp.arange(tok_rows, dtype=jnp.int32)
    rows_per_block = min(512, tok_rows)
    score_scale = head_size ** (-0.5)
    attn_in, attn_out = (
        lax.all_gather(joined_projection_weight, ("fsdp", "context"), axis=0, tiled=True),
        lax.all_gather(w_o, ("fsdp", "context"), axis=0, tiled=True),
    )
    residual = inputs.astype(jnp.float32)
    inverse_attn = lax.rsqrt(jnp.mean(residual * residual, axis=-1, keepdims=True) + EPSILON)
    unit_attn = residual * inverse_attn
    normalized_input = (unit_attn * gain_attn).astype(jnp.bfloat16)
    projected_rows = jnp.dot(normalized_input, attn_in, preferred_element_type=jnp.float32).reshape(
        tok_rows, head_groups, queries_per_group + 2, head_size
    )
    query_raw = projected_rows[:, :, :queries_per_group].reshape(tok_rows, local_heads, head_size)
    key_raw = projected_rows[:, :, queries_per_group]
    value_raw = projected_rows[:, :, queries_per_group + 1]

    def prepare(query_part, key_part, query_gain, key_gain):
        return (
            rotate(norm_rows(query_part, query_gain), positions),
            rotate(norm_rows(key_part, key_gain), positions),
        )

    query_rot, key_rot = prepare(query_raw, key_raw, gain_query, gain_key)
    queries = query_rot.astype(jnp.bfloat16)
    key_values = jnp.concatenate([key_rot, value_raw], axis=-1).astype(jnp.bfloat16)
    gathered_pairs = lax.all_gather(key_values, "context", axis=0, tiled=True)
    all_keys = gathered_pairs[:, :, :head_size]
    all_values = gathered_pairs[:, :, head_size:]

    def block_scores(first_row):
        grouped_heads = queries.reshape(rows_per_block, head_groups, queries_per_group, head_size)
        scores = (
            jnp.einsum(
                "qghd,kgd->ghqk", grouped_heads, all_keys, preferred_element_type=jnp.float32
            )
            * score_scale
        )
        same_doc = local_segments[first_row : first_row + rows_per_block, None] == segments[None, :]
        earlier = local_index[first_row : first_row + rows_per_block, None] >= token_index[None, :]
        return (grouped_heads, jnp.where((same_doc & earlier)[None, None], scores, NEGATIVE))

    first_row = 0
    grouped_heads, scores = block_scores(first_row)
    row_peak = jnp.max(scores, axis=-1, keepdims=True)
    raised = jnp.exp(scores - row_peak)
    summed = jnp.sum(raised, axis=-1, keepdims=True)
    attn_probs = (raised / summed).astype(jnp.bfloat16)
    mixed_block = jnp.einsum(
        "ghqk,kgd->qghd", attn_probs, all_values, preferred_element_type=jnp.float32
    )
    mixed_parts = mixed_block.reshape(rows_per_block, local_heads * head_size)
    log_totals = [row_peak + jnp.log(summed)]
    attended = mixed_parts.astype(jnp.bfloat16)
    attn_sum = lax.psum(times_transposed(attended, attn_out), "tensor")
    hidden_state = residual + attn_sum
    inverse_moe = lax.rsqrt(jnp.mean(hidden_state * hidden_state, axis=-1, keepdims=True) + EPSILON)
    unit_moe = hidden_state * inverse_moe
    mixed_in = (unit_moe * gain_moe).astype(jnp.bfloat16)
    logits = jnp.dot(mixed_in, router, preferred_element_type=jnp.float32)
    chosen = jnp.take_along_axis(logits, experts, axis=1)
    raised_gate = jnp.exp(chosen - jnp.max(chosen, axis=-1, keepdims=True))
    gate_values = raised_gate / jnp.sum(raised_gate, axis=-1, keepdims=True)
    expert_all = lax.all_gather(w_experts, ("fsdp", "context"), axis=0, tiled=True)
    hidden_units = expert_all.shape[3]
    flat_ids = experts.reshape(-1)
    sort_order = jnp.argsort(flat_ids, stable=True)
    undo_order = jnp.argsort(sort_order, stable=True)
    token_of = sort_order // top_count
    expert_ids = jnp.arange(expert_count, dtype=jnp.int32)
    group_sizes = jnp.sum((flat_ids[:, None] == expert_ids[None, :]).astype(jnp.int32), axis=0)
    sorted_inputs = jnp.take(mixed_in, token_of, axis=0)
    sorted_gates = jnp.take(gate_values.reshape(-1), sort_order)
    weights_in = jnp.transpose(expert_all[:, :, :2], (1, 0, 2, 3)).reshape(
        expert_count, model_width, 2 * hidden_units
    )
    weights_out = jnp.transpose(expert_all[:, :, 2], (1, 2, 0))
    assigned = flat_ids.shape[0]
    slab_rows = min(2048, assigned)
    moe_part = jnp.zeros((tok_rows, model_width), jnp.float32)
    gate_up_parts = []
    active_parts = []
    gate_dot_parts = []
    for slab_start in range(0, assigned, slab_rows):
        slab_sizes = block_groups(group_sizes, slab_start, slab_rows)
        slab_tokens = token_of[slab_start : slab_start + slab_rows]
        gate_up = lax.ragged_dot(
            sorted_inputs[slab_start : slab_start + slab_rows],
            weights_in,
            slab_sizes,
            preferred_element_type=jnp.float32,
        )
        gate_half = gate_up[:, :hidden_units]
        active = (gate_half * jax.nn.sigmoid(gate_half) * gate_up[:, hidden_units:]).astype(
            jnp.bfloat16
        )
        outputs = lax.ragged_dot(
            active, weights_out, slab_sizes, preferred_element_type=jnp.float32
        )
        moe_part = moe_part.at[slab_tokens].add(
            outputs * sorted_gates[slab_start : slab_start + slab_rows][:, None]
        )
        gate_dot_parts.append(
            jnp.sum(jnp.take(out_grad, slab_tokens, axis=0).astype(jnp.float32) * outputs, axis=-1)
        )
        gate_up_parts.append(gate_up)
        active_parts.append(active)
    gate_dot_part = jnp.take(jnp.concatenate(gate_dot_parts), undo_order).reshape(
        tok_rows, top_count
    )
    moe_sum, gate_dot = (
        lax.psum(moe_part.astype(jnp.bfloat16), "tensor").astype(jnp.float32),
        lax.psum(gate_dot_part.astype(jnp.bfloat16), "tensor").astype(jnp.float32),
    )
    output = (hidden_state + moe_sum).astype(jnp.bfloat16)
    attn_in, attn_out = (
        lax.all_gather(joined_projection_weight, ("fsdp", "context"), axis=0, tiled=True),
        lax.all_gather(w_o, ("fsdp", "context"), axis=0, tiled=True),
    )
    expert_all = lax.all_gather(w_experts, ("fsdp", "context"), axis=0, tiled=True)
    cotangent = out_grad.astype(jnp.float32)
    gate_slope = gate_values * (gate_dot - jnp.sum(gate_values * gate_dot, axis=-1, keepdims=True))
    picked = (experts[:, :, None] == expert_ids[None, None, :]).astype(jnp.float32)
    logit_grad = jnp.einsum("tk,tke->te", gate_slope, picked, precision=BEST_PRECISION).astype(
        jnp.bfloat16
    )
    router_term = outer_rows(mixed_in, logit_grad) * first_tensor
    router_back = times_transposed(logit_grad, router)
    weights_down = jnp.transpose(expert_all[:, :, 2], (1, 0, 2))
    weights_back = jnp.transpose(expert_all[:, :, :2], (1, 2, 3, 0)).reshape(
        expert_count, 2 * hidden_units, model_width
    )
    back_part = jnp.zeros((tok_rows, model_width), jnp.float32)
    scaled_parts = []
    slope_parts = []
    for slab_index, slab_start in enumerate(range(0, assigned, slab_rows)):
        slab_sizes = block_groups(group_sizes, slab_start, slab_rows)
        slab_tokens = token_of[slab_start : slab_start + slab_rows]
        scaled = (
            jnp.take(out_grad, slab_tokens, axis=0).astype(jnp.float32)
            * sorted_gates[slab_start : slab_start + slab_rows][:, None]
        ).astype(jnp.bfloat16)
        act_grad = lax.ragged_dot(
            scaled, weights_down, slab_sizes, preferred_element_type=jnp.float32
        )
        gate_half = gate_up_parts[slab_index][:, :hidden_units]
        up_half = gate_up_parts[slab_index][:, hidden_units:]
        gate_sigmoid = jax.nn.sigmoid(gate_half)
        gate_up_grad = jnp.concatenate(
            [
                act_grad * up_half * gate_sigmoid * (1.0 + gate_half * (1.0 - gate_sigmoid)),
                act_grad * gate_half * gate_sigmoid,
            ],
            axis=1,
        ).astype(jnp.bfloat16)
        back_part = back_part.at[slab_tokens].add(
            lax.ragged_dot(
                gate_up_grad, weights_back, slab_sizes, preferred_element_type=jnp.float32
            )
        )
        scaled_parts.append(scaled)
        slope_parts.append(gate_up_grad)
    sorted_scaled = jnp.concatenate(scaled_parts, axis=0)
    sorted_slopes = jnp.concatenate(slope_parts, axis=0)
    active_all = jnp.concatenate(active_parts, axis=0)
    numbers = lax.RaggedDotDimensionNumbers(
        dot_dimension_numbers=(([0], [0]), ([], [])),
        lhs_ragged_dimensions=[0],
        rhs_group_dimensions=[],
    )
    grad_in = lax.ragged_dot_general(
        sorted_inputs, sorted_slopes, group_sizes, numbers, preferred_element_type=jnp.float32
    )
    grad_out = lax.ragged_dot_general(
        sorted_scaled, active_all, group_sizes, numbers, preferred_element_type=jnp.float32
    )
    stacked = jnp.concatenate(
        [
            grad_in.reshape(
                expert_count, weight_rows * lax.axis_size(("fsdp", "context")), 2, hidden_units
            ),
            grad_out[:, :, None],
        ],
        axis=2,
    )
    w_experts_grad = lax.psum_scatter(
        jnp.transpose(stacked, (1, 0, 2, 3)).astype(jnp.bfloat16),
        ("fsdp", "context"),
        scatter_dimension=0,
        tiled=True,
    ).astype(jnp.float32)
    moe_back = lax.psum(back_part, "tensor") + router_back
    unit_grad = moe_back * gain_moe
    state_grad = cotangent + inverse_moe * (
        unit_grad - unit_moe * jnp.mean(unit_grad * unit_moe, axis=-1, keepdims=True)
    )
    moe_gain_term = jnp.sum(moe_back * unit_moe, axis=0) * first_tensor
    branch_grad = state_grad.astype(jnp.bfloat16)
    attended_grad = jnp.dot(branch_grad, attn_out, preferred_element_type=jnp.float32).astype(
        jnp.bfloat16
    )
    w_o_grad = lax.psum_scatter(
        outer_rows(branch_grad, attended).astype(jnp.bfloat16),
        ("fsdp", "context"),
        scatter_dimension=0,
        tiled=True,
    ).astype(jnp.float32)
    key_grad = jnp.zeros((sequence_length, head_groups, head_size), jnp.float32)
    value_grad = jnp.zeros((sequence_length, head_groups, head_size), jnp.float32)
    query_parts = []
    for block_number, first_row in enumerate(range(0, tok_rows, rows_per_block)):
        grouped_heads, scores = block_scores(first_row)
        attn_probs = jnp.exp(scores - log_totals[block_number])
        attn_low = attn_probs.astype(jnp.bfloat16)
        mixed_grad = attended_grad.reshape(
            rows_per_block, head_groups, queries_per_group, head_size
        )
        prob_grad = jnp.einsum(
            "qghd,kgd->ghqk", mixed_grad, all_values, preferred_element_type=jnp.float32
        )
        score_grad = (
            attn_probs * (prob_grad - jnp.sum(attn_probs * prob_grad, axis=-1, keepdims=True))
        ).astype(jnp.bfloat16)
        block_of_queries = (
            jnp.einsum("ghqk,kgd->qghd", score_grad, all_keys, preferred_element_type=jnp.float32)
            * score_scale
        )
        query_parts.append(block_of_queries.reshape(rows_per_block, local_heads, head_size))
        key_grad = (
            jnp.einsum(
                "ghqk,qghd->kgd", score_grad, grouped_heads, preferred_element_type=jnp.float32
            )
            * score_scale
        )
        value_grad = jnp.einsum(
            "ghqk,qghd->kgd", attn_low, mixed_grad, preferred_element_type=jnp.float32
        )
    pair_grad = lax.psum_scatter(
        jnp.concatenate([key_grad, value_grad], axis=-1).astype(jnp.bfloat16),
        "context",
        scatter_dimension=0,
        tiled=True,
    ).astype(jnp.float32)
    query_grad = query_parts[0]
    pullback = jax.vjp(prepare, query_raw, key_raw, gain_query, gain_key)[1]
    query_back, key_back, q_gain_term, k_gain_term = pullback(
        (query_grad, pair_grad[:, :, :head_size])
    )
    projected_grad = (
        jnp.concatenate(
            [
                query_back.reshape(tok_rows, head_groups, queries_per_group, head_size),
                key_back[:, :, None],
                pair_grad[:, :, None, head_size:],
            ],
            axis=2,
        )
        .reshape(tok_rows, -1)
        .astype(jnp.bfloat16)
    )
    normed_grad = lax.psum(
        times_transposed(projected_grad, attn_in).astype(jnp.bfloat16), "tensor"
    ).astype(jnp.float32)
    w_qkv_grad = lax.psum_scatter(
        outer_rows(normalized_input, projected_grad).astype(jnp.bfloat16),
        ("fsdp", "context"),
        scatter_dimension=0,
        tiled=True,
    ).astype(jnp.float32)
    unit_back = normed_grad * gain_attn
    inputs_grad = (
        state_grad
        + inverse_attn
        * (unit_back - unit_attn * jnp.mean(unit_back * unit_attn, axis=-1, keepdims=True))
    ).astype(jnp.bfloat16)
    attn_gain_term = jnp.sum(normed_grad * unit_attn, axis=0) * first_tensor
    attn_gain_grad, q_gain_grad, k_gain_grad, moe_gain_grad, router_grad = lax.psum(
        (attn_gain_term, q_gain_term, k_gain_term, moe_gain_term, router_term),
        ("fsdp", "context", "tensor"),
    )
    return (
        output,
        inputs_grad,
        attn_gain_grad,
        w_qkv_grad,
        q_gain_grad,
        k_gain_grad,
        w_o_grad,
        moe_gain_grad,
        router_grad,
        w_experts_grad,
    )


SPREAD = ("fsdp", "context")
VMEM_BYTES = 60 * 2**20


def flip_pairs(size, bit):
    return [(place, place ^ bit) for place in range(size)]


def flip(array, name, bit):
    return lax.ppermute(array, name, flip_pairs(lax.axis_size(name), bit))


def nothing_kernel(*refs):
    pass


def after(array, *others):
    anywhere = pl.BlockSpec(memory_space=pl.ANY)
    return pl.pallas_call(
        nothing_kernel,
        in_specs=[anywhere] * (1 + len(others)),
        out_specs=anywhere,
        out_shape=jax.ShapeDtypeStruct(array.shape, array.dtype),
        input_output_aliases={0: 0},
        name="after",
    )(array, *others)


def add_low(left_side, right_side):
    return (left_side.astype(jnp.float32) + right_side.astype(jnp.float32)).astype(jnp.bfloat16)


def partner_bits():
    size = lax.axis_size("tensor")
    return [size >> step for step in range(1, size.bit_length())]


def partner_order():
    order = [0]
    for bit in partner_bits():
        order = order + [offset ^ bit for offset in order]
    return order


def own_first(array):
    place = lax.axis_index("tensor")
    rows = array.shape[0] // lax.axis_size("tensor")
    return jnp.concatenate(
        [
            lax.dynamic_slice_in_dim(array, (place ^ offset) * rows, rows)
            for offset in partner_order()
        ],
        axis=0,
    )


def own_back(array):
    place = lax.axis_index("tensor")
    order = partner_order()
    rows = array.shape[0] // len(order)
    slot_of = jnp.array([order.index(offset) for offset in range(len(order))], jnp.int32)
    return jnp.concatenate(
        [
            lax.dynamic_slice_in_dim(array, slot_of[place ^ block] * rows, rows)
            for block in range(len(order))
        ],
        axis=0,
    )


def tensor_gather_rows(piece):
    for bit in partner_bits():
        piece = jnp.concatenate([piece, flip(piece, "tensor", bit)], axis=0)
    return piece


def tensor_scatter_rows(half_of):
    bits = partner_bits()
    theirs = flip(half_of(1), "tensor", bits[-1])
    total = add_low(half_of(0), theirs)
    for bit in bits[-2::-1]:
        rows = total.shape[0] // 2
        total = add_low(total[:rows], flip(total[rows:], "tensor", bit))
    return total


def shift(array, step):
    size = lax.axis_size("fsdp")
    return lax.ppermute(array, "fsdp", [(start, (start + step) % size) for start in range(size)])


def spread_pieces(piece, waits=()):
    pairs = []
    for step in range(lax.axis_size("fsdp")):
        if step:
            if step <= len(waits):
                piece = after(piece, *waits[step - 1])
            piece = shift(piece, 1)
        pairs.append((piece, flip(piece, "context", 1)))
    return pairs


def step_place(step):
    return (lax.axis_index("fsdp") - step) % lax.axis_size("fsdp")


def pair_places(step):
    column = 2 * step_place(step)
    side = lax.axis_index("context")
    return column + side, column + 1 - side


def in_order(pairs):
    rows, columns = pairs[0][0].shape
    whole = jnp.zeros((2 * len(pairs) * rows, columns), pairs[0][0].dtype)
    for step, pair in enumerate(pairs):
        for place, piece in zip(pair_places(step), pair):
            whole = lax.dynamic_update_slice_in_dim(whole, piece, place * rows, 0)
    return whole


def scatter_steps(pair_of, waits):
    total = None
    for number, step in enumerate(reversed(range(lax.axis_size("fsdp")))):
        mine, theirs = pair_of(step)
        if number < len(waits) and waits[number]:
            mine = after(mine, *waits[number])
        part = mine.astype(jnp.float32) + flip(theirs, "context", 1).astype(jnp.float32)
        if total is not None:
            part = part + shift(total, -1).astype(jnp.float32)
        total = part.astype(jnp.bfloat16)
    return total


def row_pairs(array, rows):
    return lambda step: [
        lax.dynamic_slice_in_dim(array, place * rows, rows) for place in pair_places(step)
    ]


def context_scatter(array, *earlier):
    place = lax.axis_index("context")
    blocks = array.reshape(lax.axis_size("fsdp"), 2, -1, array.shape[1])
    mine = lax.dynamic_index_in_dim(blocks, place, 1, keepdims=False)
    theirs = lax.dynamic_index_in_dim(blocks, 1 - place, 1, keepdims=False)
    if earlier:
        mine = after(mine, *earlier)
    return add_low(mine, flip(theirs, "context", 1))


def sum_everywhere(array):
    for name in ("tensor", "context", "fsdp"):
        bit = 1
        while bit < lax.axis_size(name):
            array = array + flip(array, name, bit)
            bit *= 2
    return array


def nt_dot(left_side, right_side):
    return lax.dot_general(
        left_side, right_side, (((1,), (1,)), ((), ())), preferred_element_type=jnp.float32
    )


def nn_dot(left_side, right_side):
    return jnp.dot(left_side, right_side, preferred_element_type=jnp.float32)


def unit_rows(raw):
    inverse = lax.rsqrt(jnp.mean(raw * raw, axis=-1, keepdims=True) + EPSILON)
    return raw * inverse, inverse


def turn(array, half_size):
    return pltpu.roll(array, half_size, 1)


def attend_kernel(scale, raw_ref, cosine_ref, sine_ref, gain_ref, key_ref, value_ref, bias_ref, out_ref):
    half_size = raw_ref.shape[1] // 2
    unit, _ = unit_rows(raw_ref[...])
    scaled = unit * gain_ref[...]
    query = scaled * cosine_ref[...] + turn(scaled, half_size) * sine_ref[...]
    scores = nt_dot(key_ref[...], query.astype(jnp.bfloat16)) * scale + bias_ref[...]
    raised = jnp.exp(scores - jnp.max(scores, axis=0, keepdims=True))
    probs = (raised / jnp.sum(raised, axis=0, keepdims=True)).astype(jnp.bfloat16)
    out_ref[...] = nn_dot(value_ref[...], probs).T.astype(jnp.bfloat16)


def attend(projected, cosine, sine, gain, keys, values_turned, bias, heads, scale):
    rows, size = cosine.shape
    length = keys.shape[0]
    whole = lambda shape: pl.BlockSpec(shape, lambda head: (0, 0))
    by_head = pl.BlockSpec((rows, size), lambda head: (0, head))
    return pl.pallas_call(
        functools.partial(attend_kernel, scale),
        grid=(heads,),
        in_specs=[
            by_head,
            whole((rows, size)),
            whole((rows, size)),
            whole((1, size)),
            whole((length, size)),
            whole((size, length)),
            whole((length, rows)),
        ],
        out_specs=by_head,
        out_shape=jax.ShapeDtypeStruct((rows, heads * size), jnp.bfloat16),
        compiler_params=pltpu.CompilerParams(vmem_limit_bytes=VMEM_BYTES),
        cost_estimate=pl.CostEstimate(
            flops=8 * heads * rows * length * size,
            bytes_accessed=8 * heads * rows * size + 4 * rows * length,
            transcendentals=heads * rows * length,
        ),
        name="attend",
    )(projected, cosine, sine, gain, keys, values_turned, bias)


def attend_back_kernel(
    scale,
    raw_ref,
    cosine_ref,
    sine_ref,
    gain_ref,
    key_ref,
    key_turned_ref,
    value_ref,
    bias_ref,
    grad_ref,
    raw_grad_ref,
    key_grad_ref,
    value_grad_ref,
    gain_grad_ref,
):
    half_size = raw_ref.shape[1] // 2
    first = pl.program_id(0) == 0
    unit, inverse = unit_rows(raw_ref[...])
    scaled = unit * gain_ref[...]
    query = (scaled * cosine_ref[...] + turn(scaled, half_size) * sine_ref[...]).astype(
        jnp.bfloat16
    )
    out_grad = grad_ref[...]
    scores = nt_dot(key_ref[...], query) * scale + bias_ref[...]
    raised = jnp.exp(scores - jnp.max(scores, axis=0, keepdims=True))
    probs = raised / jnp.sum(raised, axis=0, keepdims=True)
    prob_grad = nt_dot(value_ref[...], out_grad)
    weighted = probs * prob_grad
    score_grad = (weighted - probs * jnp.sum(weighted, axis=0, keepdims=True)).astype(jnp.bfloat16)
    key_part = nn_dot(score_grad, query) * scale
    value_part = nn_dot(probs.astype(jnp.bfloat16), out_grad)
    query_grad = (nn_dot(key_turned_ref[...], score_grad) * scale).T
    scaled_grad = query_grad * cosine_ref[...] + turn(query_grad * sine_ref[...], half_size)
    gain_part = jnp.sum(
        (scaled_grad * unit).reshape(-1, 8, scaled_grad.shape[1]), axis=0
    )
    unit_grad = scaled_grad * gain_ref[...]
    raw_grad = inverse * (unit_grad - unit * jnp.mean(unit_grad * unit, axis=-1, keepdims=True))
    raw_grad_ref[...] = raw_grad.astype(jnp.bfloat16)

    @pl.when(first)
    def _():
        key_grad_ref[...] = key_part
        value_grad_ref[...] = value_part
        gain_grad_ref[...] = gain_part

    @pl.when(jnp.logical_not(first))
    def _():
        key_grad_ref[...] += key_part
        value_grad_ref[...] += value_part
        gain_grad_ref[...] += gain_part


def attend_back(projected, cosine, sine, gain, keys, values, bias, grads, heads, scale):
    rows, size = cosine.shape
    length = keys.shape[0]
    whole = lambda shape: pl.BlockSpec(shape, lambda head: (0, 0))
    by_head = pl.BlockSpec((rows, size), lambda head: (0, head))
    return pl.pallas_call(
        functools.partial(attend_back_kernel, scale),
        grid=(heads,),
        in_specs=[
            by_head,
            whole((rows, size)),
            whole((rows, size)),
            whole((1, size)),
            whole((length, size)),
            whole((size, length)),
            whole((length, size)),
            whole((length, rows)),
            by_head,
        ],
        out_specs=[by_head, whole((length, size)), whole((length, size)), whole((8, size))],
        out_shape=[
            jax.ShapeDtypeStruct((rows, heads * size), jnp.bfloat16),
            jax.ShapeDtypeStruct((length, size), jnp.float32),
            jax.ShapeDtypeStruct((length, size), jnp.float32),
            jax.ShapeDtypeStruct((8, size), jnp.float32),
        ],
        compiler_params=pltpu.CompilerParams(vmem_limit_bytes=VMEM_BYTES),
        cost_estimate=pl.CostEstimate(
            flops=20 * heads * rows * length * size,
            bytes_accessed=8 * heads * rows * size + 4 * rows * length,
            transcendentals=heads * rows * length,
        ),
        name="attend_back",
    )(projected, cosine, sine, gain, keys, keys.T, values, bias, grads)


def experts_kernel(
    local_experts,
    sides,
    gate_lanes,
    first_ref,
    token_ref,
    gate_ref,
    grad_ref,
    *refs,
):
    chunks = 2 * local_experts
    parts = refs[: chunks * sides]
    result_ref, back_ref, active_ref, slope_ref = refs[chunks * sides : chunks * sides + 4]
    inward, outward, actives, slopes, sems = refs[chunks * sides + 4 :]
    blocks, _, hidden_units, depth = parts[0].shape
    units = sides * hidden_units
    width = token_ref.shape[1]

    @pl.when(pl.program_id(0) == 0)
    def _():
        for chunk in range(chunks):
            for side in range(sides):
                part = parts[chunk * sides + side]
                for kind in range(3):
                    place = inward if kind < 2 else outward
                    rows = ((chunk * 2 + kind) if kind < 2 else chunk) * units
                    rows = pl.ds(rows + side * hidden_units, hidden_units)
                    for block in range(blocks):
                        pltpu.make_async_copy(
                            part.at[block, kind],
                            place.at[rows, pl.ds(block * depth, depth)],
                            sems.at[chunk, kind // 2],
                        ).start()

    def body(first_step):
        tokens = token_ref[...]
        grads = grad_ref[...]
        lanes = lax.broadcasted_iota(jnp.int32, gate_ref.shape, 1)
        all_gates = gate_ref[...].astype(jnp.float32)
        dots = jnp.zeros(gate_ref.shape, jnp.float32)
        for chunk in range(chunks):
            in_rows = pl.ds(chunk * 2 * units, 2 * units)
            out_rows = pl.ds(chunk * units, units)
            if first_step:
                whole_in, whole_out = inward.at[in_rows], outward.at[out_rows]
                pltpu.make_async_copy(whole_in, whole_in, sems.at[chunk, 0]).wait()
                pltpu.make_async_copy(whole_out, whole_out, sems.at[chunk, 1]).wait()
            expert = first_ref[0] + chunk % local_experts
            gate_up = nt_dot(tokens, inward[in_rows, :])
            down_back = nt_dot(grads, outward[out_rows, :])
            here = (lanes == expert) | (lanes == expert + gate_lanes)
            gate = jnp.sum(jnp.where(here, all_gates, 0.0), axis=-1, keepdims=True)
            gate_half, up_half = gate_up[:, :units], gate_up[:, units:]
            sigmoid = jax.nn.sigmoid(gate_half)
            silu = gate_half * sigmoid
            active = silu * up_half
            act_grad = down_back * gate
            gate_slope = act_grad * up_half * (sigmoid + silu * (1.0 - sigmoid))
            gate_dot = jnp.sum(active * down_back, axis=-1, keepdims=True)
            dots = dots + jnp.where(lanes == expert, gate_dot, 0.0)
            low_active = (active * gate).astype(jnp.bfloat16)
            low_slopes = jnp.concatenate([gate_slope, act_grad * silu], axis=1)
            low_slopes = low_slopes.astype(jnp.bfloat16)
            actives[:, out_rows] = low_active
            slopes[:, in_rows] = low_slopes
            active_ref[out_rows, :] = low_active.T
            slope_ref[in_rows, :] = low_slopes.T
        back_ref[:, :width] = nn_dot(slopes[...], inward[...]).astype(jnp.bfloat16)
        back_ref[:, width:] = dots.astype(jnp.bfloat16)
        result_ref[...] = nn_dot(actives[...], outward[...]).astype(jnp.bfloat16)

    @pl.when(pl.program_id(0) == 0)
    def _():
        body(True)

    @pl.when(pl.program_id(0) > 0)
    def _():
        body(False)


def run_experts(first_expert, tokens, grads, parts, local_experts, gate_lanes):
    rows, width = grads.shape
    lanes = tokens.shape[1] - width
    sides = len(parts) // (2 * local_experts)
    units = 2 * local_experts * sides * parts[0].shape[2]
    block = min(256, rows)
    by_row = lambda columns, place: pl.BlockSpec((block, columns), lambda row, first: (row, place))
    by_column = lambda count: pl.BlockSpec((count, block), lambda row, first: (0, row))
    return pl.pallas_call(
        functools.partial(experts_kernel, local_experts, sides, gate_lanes),
        grid_spec=pltpu.PrefetchScalarGridSpec(
            num_scalar_prefetch=1,
            grid=(rows // block,),
            in_specs=[by_row(width, 0), by_row(lanes, width // lanes), by_row(width, 0)]
            + [pl.BlockSpec(memory_space=pl.ANY)] * len(parts),
            out_specs=[
                by_row(width, 0),
                by_row(width + lanes, 0),
                by_column(units),
                by_column(2 * units),
            ],
            scratch_shapes=[
                pltpu.VMEM((2 * units, width), jnp.bfloat16),
                pltpu.VMEM((units, width), jnp.bfloat16),
                pltpu.VMEM((block, units), jnp.bfloat16),
                pltpu.VMEM((block, 2 * units), jnp.bfloat16),
                pltpu.SemaphoreType.DMA((2 * local_experts, 2)),
            ],
        ),
        out_shape=[
            jax.ShapeDtypeStruct((rows, width), jnp.bfloat16),
            jax.ShapeDtypeStruct((rows, width + lanes), jnp.bfloat16),
            jax.ShapeDtypeStruct((units, rows), jnp.bfloat16),
            jax.ShapeDtypeStruct((2 * units, rows), jnp.bfloat16),
        ],
        compiler_params=pltpu.CompilerParams(vmem_limit_bytes=VMEM_BYTES),
        cost_estimate=pl.CostEstimate(
            flops=12 * rows * width * units,
            bytes_accessed=6 * units * (width + rows) + 8 * rows * width,
            transcendentals=rows * units,
        ),
        name="experts",
    )(first_expert.reshape(1), tokens, tokens, grads, *parts)


def expert_grads_kernel(hidden_units, slope_ref, active_ref, token_ref, grad_ref, *refs):
    sides = active_ref.shape[0] // hidden_units
    depth = refs[-1].shape[2]
    inward = nn_dot(slope_ref[...], token_ref[...])
    outward = nn_dot(active_ref[...], grad_ref[...])
    received, outs = refs[: len(refs) - sides], refs[len(refs) - sides :]
    if len(refs) == 1:
        received, outs = (), refs * sides
    for side in range(sides):
        for kind in range(3):
            start = ((kind * sides if kind < 2 else 0) + side) * hidden_units
            wide = (inward if kind < 2 else outward)[start : start + hidden_units]
            place = kind * hidden_units
            whole = (side * 3 + kind) * hidden_units
            for block in range(refs[-1].shape[0]):
                rows = wide[:, block * depth : (block + 1) * depth]
                if received:
                    more = received[0][block, whole : whole + hidden_units]
                    rows = rows + more.astype(jnp.float32)
                into = place if received else whole
                outs[side][block, into : into + hidden_units] = rows.astype(jnp.bfloat16)


def expert_grads(chunk, slopes, actives, tokens, grads, chunks, sides, blocks, received=None):
    rows, width = grads.shape
    depth = width // blocks
    units = actives.shape[0] // chunks
    step = 2 if blocks % 2 == 0 else 1
    by_block = lambda count: pl.BlockSpec((step, count, depth), lambda column: (column, 0, 0))
    shape = lambda count: jax.ShapeDtypeStruct((blocks, count, depth), jnp.bfloat16)
    alone = received is None
    return pl.pallas_call(
        functools.partial(expert_grads_kernel, units // sides),
        grid=(blocks // step,),
        in_specs=[
            pl.BlockSpec((2 * units, rows), lambda column: (chunk, 0)),
            pl.BlockSpec((units, rows), lambda column: (chunk, 0)),
            pl.BlockSpec((rows, step * depth), lambda column: (0, column)),
            pl.BlockSpec((rows, step * depth), lambda column: (0, column)),
        ]
        + ([] if alone else [by_block(3 * units)]),
        out_specs=by_block(3 * units) if alone else [by_block(3 * units // sides)] * sides,
        out_shape=shape(3 * units) if alone else [shape(3 * units // sides)] * sides,
        compiler_params=pltpu.CompilerParams(vmem_limit_bytes=VMEM_BYTES),
        cost_estimate=pl.CostEstimate(
            flops=6 * units * rows * width,
            bytes_accessed=6 * units * (rows + width) + 4 * rows * width,
            transcendentals=0,
        ),
        name="expert_grads",
    )(slopes, actives, tokens, grads, *([] if alone else [received]))


def expert_parallel_shards(
    inputs,
    attn_gain,
    joined_projection_weight,
    q_gain,
    k_gain,
    w_o,
    moe_gain,
    router,
    w_experts,
    segments,
    experts,
    out_grad,
):
    tok_rows, model_width = inputs.shape
    head_size = q_gain.shape[0]
    half_size = head_size // 2
    tensor_size = lax.axis_size("tensor")
    heads = QUERY_HEADS // KEY_VALUE_HEADS
    expert_count = router.shape[1]
    spread_size = lax.axis_size(SPREAD)
    local_experts = expert_count // spread_size
    hidden_units = w_experts.shape[3]
    slice_rows = w_experts.shape[0]
    own_rows = tok_rows // tensor_size
    context_place = lax.axis_index("context")
    own_start = lax.axis_index("tensor") * own_rows
    first_expert = lax.axis_index(SPREAD) * local_experts
    gain_attn = attn_gain.astype(jnp.float32)
    gain_moe = moe_gain.astype(jnp.float32)
    gain_query = q_gain.astype(jnp.float32)[None]
    gain_key = k_gain.astype(jnp.float32)
    score_scale = head_size ** (-0.5)

    attn_in_pairs = spread_pieces(joined_projection_weight)
    attn_in = in_order(attn_in_pairs)
    attn_out = lax.all_gather(
        after(w_o, attn_in_pairs[len(attn_in_pairs) // 2][0]), SPREAD, axis=0, tiled=True
    )
    own_grad = lax.dynamic_slice_in_dim(out_grad, own_start, own_rows)

    sent_weights = jnp.transpose(w_experts, (1, 2, 3, 0)).reshape(
        spread_size, local_experts, 3, hidden_units, slice_rows
    )
    ordered = own_first(inputs)
    own_index = own_first(jnp.arange(tok_rows, dtype=jnp.int32))
    own_tokens = context_place * tok_rows + own_index
    all_tokens = jnp.concatenate([own_tokens, (1 - context_place) * tok_rows + own_index])
    token_segments = jnp.take(segments, all_tokens)
    positions = jnp.take(doc_positions(segments), own_tokens)
    allowed = (token_segments[:, None] == token_segments[None, :tok_rows]) & (
        all_tokens[:, None] <= own_tokens[None, :]
    )
    bias = jnp.where(allowed, 0.0, NEGATIVE).astype(jnp.float32)
    inverse_angles = ROPE_THETA ** (
        -2.0 * jnp.arange(half_size, dtype=jnp.float32) / head_size
    )
    angles = positions.astype(jnp.float32)[:, None] * inverse_angles[None, :]
    cosine = jnp.concatenate([jnp.cos(angles)] * 2, axis=-1)
    half_sine = jnp.sin(angles)
    sine = jnp.concatenate([-half_sine, half_sine], axis=-1)

    residual = ordered.astype(jnp.float32)
    inverse_attn = lax.rsqrt(jnp.mean(residual * residual, axis=-1, keepdims=True) + EPSILON)
    normalized_input = (residual * inverse_attn * gain_attn).astype(jnp.bfloat16)
    projected = jnp.zeros((tok_rows, joined_projection_weight.shape[1]), jnp.float32)
    for step, pair in enumerate(attn_in_pairs):
        for place, piece in zip(pair_places(step), pair):
            columns = lax.dynamic_slice_in_dim(
                normalized_input, place * slice_rows, slice_rows, axis=1
            )
            projected = projected + nn_dot(columns, piece)
    weight_parts = [
        lax.all_to_all(after(sent_weights[:, 0], projected), SPREAD, 0, 0, tiled=True)
    ]
    all_grads = lax.all_gather(after(own_grad, projected), SPREAD, axis=0, tiled=True)
    key_raw = projected[:, heads * head_size : (heads + 1) * head_size]
    value_raw = projected[:, (heads + 1) * head_size :]

    def prepare_key(raw, gain):
        scaled = norm_rows(raw, gain)
        swapped = jnp.concatenate([scaled[:, half_size:], scaled[:, :half_size]], axis=-1)
        return scaled * cosine + swapped * sine

    key_values = jnp.concatenate([prepare_key(key_raw, gain_key), value_raw], axis=-1).astype(
        jnp.bfloat16
    )
    pairs = jnp.concatenate([key_values, flip(key_values, "context", 1)], axis=0)
    keys, values = pairs[:, :head_size], pairs[:, head_size:]
    attended = attend(
        projected,
        cosine,
        sine,
        gain_query,
        keys,
        values.T,
        bias,
        heads,
        score_scale,
    )
    weight_parts = [after(weight_parts[0], attended)]
    for expert in range(1, local_experts):
        sent = after(sent_weights[:, expert], weight_parts[-1])
        weight_parts.append(lax.all_to_all(sent, SPREAD, 0, 0, tiled=True))
    wide_bit, core_bit = partner_bits()
    wide_parts = [flip(part, "tensor", wide_bit) for part in weight_parts]
    half_rows = tok_rows // 2
    attn_sum = tensor_scatter_rows(
        lambda half: nt_dot(
            attended[half * half_rows : (half + 1) * half_rows], attn_out
        ).astype(jnp.bfloat16)
    )

    own_inputs = ordered[:own_rows].astype(jnp.float32)
    own_experts = lax.dynamic_slice_in_dim(experts, own_start, own_rows)
    hidden_state = own_inputs + attn_sum.astype(jnp.float32)
    inverse_moe = lax.rsqrt(jnp.mean(hidden_state * hidden_state, axis=-1, keepdims=True) + EPSILON)
    unit_moe = hidden_state * inverse_moe
    mixed_in = (unit_moe * gain_moe).astype(jnp.bfloat16)
    logits = nn_dot(mixed_in, router)
    expert_ids = jnp.arange(expert_count, dtype=jnp.int32)
    picked = jnp.any(own_experts[:, :, None] == expert_ids[None, None, :], axis=1)
    peak = jnp.max(jnp.where(picked, logits, -jnp.inf), axis=-1, keepdims=True)
    raised_gate = jnp.where(picked, jnp.exp(jnp.minimum(logits - peak, 0.0)), 0.0)
    gate_values = raised_gate / jnp.sum(raised_gate, axis=-1, keepdims=True)
    gate_high = gate_values.astype(jnp.bfloat16)
    gate_low = (gate_values - gate_high.astype(jnp.float32)).astype(jnp.bfloat16)
    lane_pad = 128 - 2 * expert_count
    payload = jnp.concatenate(
        [mixed_in, gate_high, gate_low, jnp.zeros((own_rows, lane_pad), jnp.bfloat16)], axis=1
    )
    tokens = in_order(
        spread_pieces(payload, [(weight_parts[0],), (wide_parts[0], all_grads), (weight_parts[-1],)])
    )
    own_parts, other_parts = [], []
    for pair in zip(weight_parts, wide_parts):
        pair = [pair[0], after(pair[1], tokens)]
        own_parts += pair
        other_parts += [flip(array, "tensor", core_bit) for array in pair]

    results, backs, actives, slopes = run_experts(
        first_expert, tokens, all_grads, own_parts + other_parts, local_experts, expert_count
    )
    grads_of = functools.partial(
        expert_grads,
        slopes=slopes,
        actives=actives,
        tokens=tokens,
        grads=all_grads,
        chunks=2 * local_experts,
        sides=len(partner_bits()),
        blocks=spread_size,
    )
    far_sums = [grads_of(local_experts + expert) for expert in range(local_experts)]
    own_sums = [
        grads_of(expert, received=flip(far_sums[expert], "tensor", core_bit))
        for expert in range(local_experts)
    ]
    exchange = lambda sums: add_low(sums[0], flip(sums[1], "tensor", wide_bit))
    moe_sum = lax.psum_scatter(results, SPREAD, scatter_dimension=0, tiled=True)
    expert_sums = [exchange(own_sums[0])]
    back_total = scatter_steps(
        row_pairs(backs, own_rows),
        [(), (far_sums[0],), (own_sums[0][0],), (far_sums[1], expert_sums[0])],
    )
    cotangent = own_grad.astype(jnp.float32)
    gate_dot = back_total[:, model_width : model_width + expert_count].astype(jnp.float32)
    logit_grad = (
        gate_values * (gate_dot - jnp.sum(gate_values * gate_dot, axis=-1, keepdims=True))
    ).astype(jnp.bfloat16)
    router_term = outer_rows(logit_grad, mixed_in)
    moe_back = back_total[:, :model_width].astype(jnp.float32) + nt_dot(logit_grad, router)
    unit_grad = moe_back * gain_moe
    state_grad = cotangent + inverse_moe * (
        unit_grad - unit_moe * jnp.mean(unit_grad * unit_moe, axis=-1, keepdims=True)
    )
    moe_gain_term = jnp.sum(moe_back * unit_moe, axis=0, keepdims=True)
    branch_grad = tensor_gather_rows(state_grad.astype(jnp.bfloat16))
    expert_backs = [lax.all_to_all(expert_sums[0], SPREAD, 0, 0, tiled=True)]
    w_o_part = outer_rows(branch_grad, attended).astype(jnp.bfloat16)
    attended_grad = nn_dot(after(branch_grad, own_sums[-1][0]), attn_out).astype(jnp.bfloat16)

    query_back, key_grad, value_grad, q_gain_rows = attend_back(
        projected, cosine, sine, gain_query, keys, values, bias, attended_grad, heads, score_scale
    )
    for mine, theirs in own_sums[1:]:
        expert_sums.append(exchange((after(mine, key_grad), after(theirs, branch_grad))))
    for sums in expert_sums[1:]:
        expert_backs.append(
            lax.all_to_all(after(sums, expert_backs[-1]), SPREAD, 0, 0, tiled=True)
        )
    w_experts_grad = (
        jnp.stack(expert_backs, axis=1)
        .reshape(expert_count, 3, hidden_units, slice_rows)
        .astype(jnp.float32)
        .transpose(3, 0, 1, 2)
    )
    pair_grad = jnp.concatenate([key_grad, value_grad], axis=-1)
    sent_pairs = after(pair_grad[tok_rows:].astype(jnp.bfloat16), expert_sums[0])
    pair_grad = pair_grad[:tok_rows] + flip(sent_pairs, "context", 1).astype(jnp.float32)
    key_back, k_gain_term = jax.vjp(prepare_key, key_raw, gain_key)[1](pair_grad[:, :head_size])
    projected_grad = jnp.concatenate(
        [
            query_back,
            key_back.astype(jnp.bfloat16),
            pair_grad[:, head_size:].astype(jnp.bfloat16),
        ],
        axis=1,
    )
    w_qkv_part = outer_rows(normalized_input, projected_grad).astype(jnp.bfloat16)
    w_qkv_rows = lax.psum_scatter(
        after(w_qkv_part, expert_sums[1], expert_backs[0]),
        SPREAD,
        scatter_dimension=0,
        tiled=True,
    )
    w_o_sum = context_scatter(w_o_part, w_qkv_part)
    late_grad = after(projected_grad, w_o_sum)
    w_o_rows = lax.all_to_all(
        after(w_o_sum, expert_backs[1]), "fsdp", 0, 0, tiled=True
    )
    w_o_grad = jnp.sum(w_o_rows.astype(jnp.float32), axis=0)
    w_qkv_grad = w_qkv_rows.astype(jnp.float32)
    own_output = (
        hidden_state + after(moe_sum, projected_grad).astype(jnp.float32)
    ).astype(jnp.bfloat16)
    output = own_back(tensor_gather_rows(own_output))
    normed_grad = tensor_scatter_rows(
        lambda half: nt_dot(
            late_grad[half * half_rows : (half + 1) * half_rows], attn_in
        ).astype(jnp.bfloat16)
    ).astype(jnp.float32)
    own_inverse = inverse_attn[:own_rows]
    own_unit = own_inputs * own_inverse
    unit_back = normed_grad * gain_attn
    own_inputs_grad = (
        state_grad
        + own_inverse
        * (unit_back - own_unit * jnp.mean(unit_back * own_unit, axis=-1, keepdims=True))
    ).astype(jnp.bfloat16)
    inputs_grad = own_back(tensor_gather_rows(own_inputs_grad))
    attn_gain_term = jnp.sum(normed_grad * own_unit, axis=0)
    gain_terms = jnp.concatenate([jnp.sum(q_gain_rows, axis=0), k_gain_term])
    sums = sum_everywhere(
        jnp.concatenate(
            [
                router_term,
                moe_gain_term,
                attn_gain_term[None],
                jnp.pad(gain_terms, (0, model_width - gain_terms.shape[0]))[None],
            ],
            axis=0,
        )
    )
    gain_sums = sums[expert_count + 2]
    return (
        output,
        inputs_grad,
        sums[expert_count + 1],
        w_qkv_grad,
        gain_sums[:head_size],
        gain_sums[head_size : 2 * head_size],
        w_o_grad,
        sums[expert_count],
        sums[:expert_count].T,
        w_experts_grad,
    )


def choose_shards(mesh, arrays):
    sizes = mesh.shape
    spread = sizes["fsdp"] * sizes["context"]
    tok_rows, width = arrays[0].shape
    head_size, expert_count = arrays[3].shape[0], arrays[7].shape[1]
    fits = (
        expert_count % spread == 0
        and 2 * expert_count <= 128
        and tok_rows % (32 * sizes["tensor"]) == 0
        and width % 128 == 0
        and head_size % 128 == 0
        and sizes["tensor"] == KEY_VALUE_HEADS
        and sizes["context"] == 2
        and sizes["fsdp"] & (sizes["fsdp"] - 1) == 0
    )
    return expert_parallel_shards if fits else shards


def solution(mesh):
    def by_shapes(*arrays):
        return choose_shards(mesh, arrays)(*arrays)

    return jax.shard_map(
        by_shapes,
        mesh=mesh,
        in_specs=(
            P(("fsdp", "context"), None),
            P(),
            P(("fsdp", "context"), "tensor"),
            P(),
            P(),
            P(("fsdp", "context"), "tensor"),
            P(),
            P(),
            P(("fsdp", "context"), None, None, "tensor"),
            P("fsdp"),
            P(("fsdp", "context"), None),
            P(("fsdp", "context"), None),
        ),
        out_specs=(
            P(("fsdp", "context"), None),
            P(("fsdp", "context"), None),
            P(),
            P(("fsdp", "context"), "tensor"),
            P(),
            P(),
            P(("fsdp", "context"), "tensor"),
            P(),
            P(),
            P(("fsdp", "context"), None, None, "tensor"),
        ),
        check_vma=False,
    )
```

```python
import functools

import jax
import jax.numpy as jnp
from jax import lax
from jax.experimental import pallas as pl
from jax.experimental.pallas import tpu as pltpu
from jax.sharding import PartitionSpec as P

QUERY_HEADS = 32
KEY_VALUE_HEADS = 4


EPSILON = 1e-06
ROPE_THETA = 1000000.0
NEGATIVE = -1e30
BEST_PRECISION = lax.Precision.HIGHEST


def norm_rows(matrix, scaling):
    return matrix * lax.rsqrt(jnp.mean(matrix * matrix, axis=-1, keepdims=True) + EPSILON) * scaling


def doc_positions(segment_ids):
    index_all = jnp.arange(segment_ids.shape[0], dtype=jnp.int32)
    starts = jnp.concatenate(
        [jnp.ones((1,), jnp.int32), (segment_ids[1:] != segment_ids[:-1]).astype(jnp.int32)]
    )
    return index_all - lax.cummax(index_all * starts, axis=0)


def rotate(tensor_array, positions):
    half_size = tensor_array.shape[-1] // 2
    inverse = ROPE_THETA ** (
        -2.0 * jnp.arange(half_size, dtype=jnp.float32) / tensor_array.shape[-1]
    )
    angles = positions.astype(jnp.float32)[:, None] * inverse[None, :]
    cosine = jnp.concatenate([jnp.cos(angles), jnp.cos(angles)], axis=-1)[:, None, :]
    sine_table = jnp.concatenate([jnp.sin(angles), jnp.sin(angles)], axis=-1)[:, None, :]
    turned = jnp.concatenate(
        [-tensor_array[..., half_size:], tensor_array[..., :half_size]], axis=-1
    )
    return tensor_array * cosine + turned * sine_table


def block_groups(group_sizes, first_row, row_count):
    group_ends = jnp.cumsum(group_sizes)
    begins = group_ends - group_sizes
    clipped_end = jnp.clip(group_ends, first_row, first_row + row_count)
    clipped_begin = jnp.clip(begins, first_row, first_row + row_count)
    return clipped_end - clipped_begin


def times_transposed(left_side, right_side):
    return lax.dot_general(
        left_side, right_side, (((1,), (1,)), ((), ())), preferred_element_type=jnp.float32
    )


def outer_rows(left_side, right_side):
    return lax.dot_general(
        left_side, right_side, (((0,), (0,)), ((), ())), preferred_element_type=jnp.float32
    )


def shards(
    inputs,
    attn_gain,
    joined_projection_weight,
    q_gain,
    k_gain,
    w_o,
    moe_gain,
    router,
    w_experts,
    segments,
    experts,
    out_grad,
):
    tok_rows, model_width = inputs.shape
    head_size = q_gain.shape[0]
    head_groups = KEY_VALUE_HEADS // lax.axis_size("tensor")
    queries_per_group = QUERY_HEADS // KEY_VALUE_HEADS
    local_heads = head_groups * queries_per_group
    top_count = experts.shape[1]
    expert_count = router.shape[1]
    sequence_length = segments.shape[0]
    weight_rows = joined_projection_weight.shape[0]
    span_start = lax.axis_index("context") * tok_rows
    first_tensor = (lax.axis_index("tensor") == 0).astype(jnp.float32)
    gain_attn = attn_gain.astype(jnp.float32)
    gain_moe = moe_gain.astype(jnp.float32)
    gain_query = q_gain.astype(jnp.float32)
    gain_key = k_gain.astype(jnp.float32)
    token_index = jnp.arange(sequence_length, dtype=jnp.int32)
    positions = lax.dynamic_slice_in_dim(doc_positions(segments), span_start, tok_rows)
    local_segments = lax.dynamic_slice_in_dim(segments, span_start, tok_rows)
    local_index = span_start + jnp.arange(tok_rows, dtype=jnp.int32)
    rows_per_block = min(512, tok_rows)
    score_scale = head_size ** (-0.5)
    attn_in, attn_out = (
        lax.all_gather(joined_projection_weight, ("fsdp", "context"), axis=0, tiled=True),
        lax.all_gather(w_o, ("fsdp", "context"), axis=0, tiled=True),
    )
    residual = inputs.astype(jnp.float32)
    inverse_attn = lax.rsqrt(jnp.mean(residual * residual, axis=-1, keepdims=True) + EPSILON)
    unit_attn = residual * inverse_attn
    normalized_input = (unit_attn * gain_attn).astype(jnp.bfloat16)
    projected_rows = jnp.dot(normalized_input, attn_in, preferred_element_type=jnp.float32).reshape(
        tok_rows, head_groups, queries_per_group + 2, head_size
    )
    query_raw = projected_rows[:, :, :queries_per_group].reshape(tok_rows, local_heads, head_size)
    key_raw = projected_rows[:, :, queries_per_group]
    value_raw = projected_rows[:, :, queries_per_group + 1]

    def prepare(query_part, key_part, query_gain, key_gain):
        return (
            rotate(norm_rows(query_part, query_gain), positions),
            rotate(norm_rows(key_part, key_gain), positions),
        )

    query_rot, key_rot = prepare(query_raw, key_raw, gain_query, gain_key)
    queries = query_rot.astype(jnp.bfloat16)
    key_values = jnp.concatenate([key_rot, value_raw], axis=-1).astype(jnp.bfloat16)
    gathered_pairs = lax.all_gather(key_values, "context", axis=0, tiled=True)
    all_keys = gathered_pairs[:, :, :head_size]
    all_values = gathered_pairs[:, :, head_size:]

    def block_scores(first_row):
        grouped_heads = queries.reshape(rows_per_block, head_groups, queries_per_group, head_size)
        scores = (
            jnp.einsum(
                "qghd,kgd->ghqk", grouped_heads, all_keys, preferred_element_type=jnp.float32
            )
            * score_scale
        )
        same_doc = local_segments[first_row : first_row + rows_per_block, None] == segments[None, :]
        earlier = local_index[first_row : first_row + rows_per_block, None] >= token_index[None, :]
        return (grouped_heads, jnp.where((same_doc & earlier)[None, None], scores, NEGATIVE))

    first_row = 0
    grouped_heads, scores = block_scores(first_row)
    row_peak = jnp.max(scores, axis=-1, keepdims=True)
    raised = jnp.exp(scores - row_peak)
    summed = jnp.sum(raised, axis=-1, keepdims=True)
    attn_probs = (raised / summed).astype(jnp.bfloat16)
    mixed_block = jnp.einsum(
        "ghqk,kgd->qghd", attn_probs, all_values, preferred_element_type=jnp.float32
    )
    mixed_parts = mixed_block.reshape(rows_per_block, local_heads * head_size)
    log_totals = [row_peak + jnp.log(summed)]
    attended = mixed_parts.astype(jnp.bfloat16)
    attn_sum = lax.psum(times_transposed(attended, attn_out), "tensor")
    hidden_state = residual + attn_sum
    inverse_moe = lax.rsqrt(jnp.mean(hidden_state * hidden_state, axis=-1, keepdims=True) + EPSILON)
    unit_moe = hidden_state * inverse_moe
    mixed_in = (unit_moe * gain_moe).astype(jnp.bfloat16)
    logits = jnp.dot(mixed_in, router, preferred_element_type=jnp.float32)
    chosen = jnp.take_along_axis(logits, experts, axis=1)
    raised_gate = jnp.exp(chosen - jnp.max(chosen, axis=-1, keepdims=True))
    gate_values = raised_gate / jnp.sum(raised_gate, axis=-1, keepdims=True)
    expert_all = lax.all_gather(w_experts, ("fsdp", "context"), axis=0, tiled=True)
    hidden_units = expert_all.shape[3]
    flat_ids = experts.reshape(-1)
    sort_order = jnp.argsort(flat_ids, stable=True)
    undo_order = jnp.argsort(sort_order, stable=True)
    token_of = sort_order // top_count
    expert_ids = jnp.arange(expert_count, dtype=jnp.int32)
    group_sizes = jnp.sum((flat_ids[:, None] == expert_ids[None, :]).astype(jnp.int32), axis=0)
    sorted_inputs = jnp.take(mixed_in, token_of, axis=0)
    sorted_gates = jnp.take(gate_values.reshape(-1), sort_order)
    weights_in = jnp.transpose(expert_all[:, :, :2], (1, 0, 2, 3)).reshape(
        expert_count, model_width, 2 * hidden_units
    )
    weights_out = jnp.transpose(expert_all[:, :, 2], (1, 2, 0))
    assigned = flat_ids.shape[0]
    slab_rows = min(2048, assigned)
    moe_part = jnp.zeros((tok_rows, model_width), jnp.float32)
    gate_up_parts = []
    active_parts = []
    gate_dot_parts = []
    for slab_start in range(0, assigned, slab_rows):
        slab_sizes = block_groups(group_sizes, slab_start, slab_rows)
        slab_tokens = token_of[slab_start : slab_start + slab_rows]
        gate_up = lax.ragged_dot(
            sorted_inputs[slab_start : slab_start + slab_rows],
            weights_in,
            slab_sizes,
            preferred_element_type=jnp.float32,
        )
        gate_half = gate_up[:, :hidden_units]
        active = (gate_half * jax.nn.sigmoid(gate_half) * gate_up[:, hidden_units:]).astype(
            jnp.bfloat16
        )
        outputs = lax.ragged_dot(
            active, weights_out, slab_sizes, preferred_element_type=jnp.float32
        )
        moe_part = moe_part.at[slab_tokens].add(
            outputs * sorted_gates[slab_start : slab_start + slab_rows][:, None]
        )
        gate_dot_parts.append(
            jnp.sum(jnp.take(out_grad, slab_tokens, axis=0).astype(jnp.float32) * outputs, axis=-1)
        )
        gate_up_parts.append(gate_up)
        active_parts.append(active)
    gate_dot_part = jnp.take(jnp.concatenate(gate_dot_parts), undo_order).reshape(
        tok_rows, top_count
    )
    moe_sum, gate_dot = (
        lax.psum(moe_part.astype(jnp.bfloat16), "tensor").astype(jnp.float32),
        lax.psum(gate_dot_part.astype(jnp.bfloat16), "tensor").astype(jnp.float32),
    )
    output = (hidden_state + moe_sum).astype(jnp.bfloat16)
    attn_in, attn_out = (
        lax.all_gather(joined_projection_weight, ("fsdp", "context"), axis=0, tiled=True),
        lax.all_gather(w_o, ("fsdp", "context"), axis=0, tiled=True),
    )
    expert_all = lax.all_gather(w_experts, ("fsdp", "context"), axis=0, tiled=True)
    cotangent = out_grad.astype(jnp.float32)
    gate_slope = gate_values * (gate_dot - jnp.sum(gate_values * gate_dot, axis=-1, keepdims=True))
    picked = (experts[:, :, None] == expert_ids[None, None, :]).astype(jnp.float32)
    logit_grad = jnp.einsum("tk,tke->te", gate_slope, picked, precision=BEST_PRECISION).astype(
        jnp.bfloat16
    )
    router_term = outer_rows(mixed_in, logit_grad) * first_tensor
    router_back = times_transposed(logit_grad, router)
    weights_down = jnp.transpose(expert_all[:, :, 2], (1, 0, 2))
    weights_back = jnp.transpose(expert_all[:, :, :2], (1, 2, 3, 0)).reshape(
        expert_count, 2 * hidden_units, model_width
    )
    back_part = jnp.zeros((tok_rows, model_width), jnp.float32)
    scaled_parts = []
    slope_parts = []
    for slab_index, slab_start in enumerate(range(0, assigned, slab_rows)):
        slab_sizes = block_groups(group_sizes, slab_start, slab_rows)
        slab_tokens = token_of[slab_start : slab_start + slab_rows]
        scaled = (
            jnp.take(out_grad, slab_tokens, axis=0).astype(jnp.float32)
            * sorted_gates[slab_start : slab_start + slab_rows][:, None]
        ).astype(jnp.bfloat16)
        act_grad = lax.ragged_dot(
            scaled, weights_down, slab_sizes, preferred_element_type=jnp.float32
        )
        gate_half = gate_up_parts[slab_index][:, :hidden_units]
        up_half = gate_up_parts[slab_index][:, hidden_units:]
        gate_sigmoid = jax.nn.sigmoid(gate_half)
        gate_up_grad = jnp.concatenate(
            [
                act_grad * up_half * gate_sigmoid * (1.0 + gate_half * (1.0 - gate_sigmoid)),
                act_grad * gate_half * gate_sigmoid,
            ],
            axis=1,
        ).astype(jnp.bfloat16)
        back_part = back_part.at[slab_tokens].add(
            lax.ragged_dot(
                gate_up_grad, weights_back, slab_sizes, preferred_element_type=jnp.float32
            )
        )
        scaled_parts.append(scaled)
        slope_parts.append(gate_up_grad)
    sorted_scaled = jnp.concatenate(scaled_parts, axis=0)
    sorted_slopes = jnp.concatenate(slope_parts, axis=0)
    active_all = jnp.concatenate(active_parts, axis=0)
    numbers = lax.RaggedDotDimensionNumbers(
        dot_dimension_numbers=(([0], [0]), ([], [])),
        lhs_ragged_dimensions=[0],
        rhs_group_dimensions=[],
    )
    grad_in = lax.ragged_dot_general(
        sorted_inputs, sorted_slopes, group_sizes, numbers, preferred_element_type=jnp.float32
    )
    grad_out = lax.ragged_dot_general(
        sorted_scaled, active_all, group_sizes, numbers, preferred_element_type=jnp.float32
    )
    stacked = jnp.concatenate(
        [
            grad_in.reshape(
                expert_count, weight_rows * lax.axis_size(("fsdp", "context")), 2, hidden_units
            ),
            grad_out[:, :, None],
        ],
        axis=2,
    )
    w_experts_grad = lax.psum_scatter(
        jnp.transpose(stacked, (1, 0, 2, 3)).astype(jnp.bfloat16),
        ("fsdp", "context"),
        scatter_dimension=0,
        tiled=True,
    ).astype(jnp.float32)
    moe_back = lax.psum(back_part, "tensor") + router_back
    unit_grad = moe_back * gain_moe
    state_grad = cotangent + inverse_moe * (
        unit_grad - unit_moe * jnp.mean(unit_grad * unit_moe, axis=-1, keepdims=True)
    )
    moe_gain_term = jnp.sum(moe_back * unit_moe, axis=0) * first_tensor
    branch_grad = state_grad.astype(jnp.bfloat16)
    attended_grad = jnp.dot(branch_grad, attn_out, preferred_element_type=jnp.float32).astype(
        jnp.bfloat16
    )
    w_o_grad = lax.psum_scatter(
        outer_rows(branch_grad, attended).astype(jnp.bfloat16),
        ("fsdp", "context"),
        scatter_dimension=0,
        tiled=True,
    ).astype(jnp.float32)
    key_grad = jnp.zeros((sequence_length, head_groups, head_size), jnp.float32)
    value_grad = jnp.zeros((sequence_length, head_groups, head_size), jnp.float32)
    query_parts = []
    for block_number, first_row in enumerate(range(0, tok_rows, rows_per_block)):
        grouped_heads, scores = block_scores(first_row)
        attn_probs = jnp.exp(scores - log_totals[block_number])
        attn_low = attn_probs.astype(jnp.bfloat16)
        mixed_grad = attended_grad.reshape(
            rows_per_block, head_groups, queries_per_group, head_size
        )
        prob_grad = jnp.einsum(
            "qghd,kgd->ghqk", mixed_grad, all_values, preferred_element_type=jnp.float32
        )
        score_grad = (
            attn_probs * (prob_grad - jnp.sum(attn_probs * prob_grad, axis=-1, keepdims=True))
        ).astype(jnp.bfloat16)
        block_of_queries = (
            jnp.einsum("ghqk,kgd->qghd", score_grad, all_keys, preferred_element_type=jnp.float32)
            * score_scale
        )
        query_parts.append(block_of_queries.reshape(rows_per_block, local_heads, head_size))
        key_grad = (
            jnp.einsum(
                "ghqk,qghd->kgd", score_grad, grouped_heads, preferred_element_type=jnp.float32
            )
            * score_scale
        )
        value_grad = jnp.einsum(
            "ghqk,qghd->kgd", attn_low, mixed_grad, preferred_element_type=jnp.float32
        )
    pair_grad = lax.psum_scatter(
        jnp.concatenate([key_grad, value_grad], axis=-1).astype(jnp.bfloat16),
        "context",
        scatter_dimension=0,
        tiled=True,
    ).astype(jnp.float32)
    query_grad = query_parts[0]
    pullback = jax.vjp(prepare, query_raw, key_raw, gain_query, gain_key)[1]
    query_back, key_back, q_gain_term, k_gain_term = pullback(
        (query_grad, pair_grad[:, :, :head_size])
    )
    projected_grad = (
        jnp.concatenate(
            [
                query_back.reshape(tok_rows, head_groups, queries_per_group, head_size),
                key_back[:, :, None],
                pair_grad[:, :, None, head_size:],
            ],
            axis=2,
        )
        .reshape(tok_rows, -1)
        .astype(jnp.bfloat16)
    )
    normed_grad = lax.psum(
        times_transposed(projected_grad, attn_in).astype(jnp.bfloat16), "tensor"
    ).astype(jnp.float32)
    w_qkv_grad = lax.psum_scatter(
        outer_rows(normalized_input, projected_grad).astype(jnp.bfloat16),
        ("fsdp", "context"),
        scatter_dimension=0,
        tiled=True,
    ).astype(jnp.float32)
    unit_back = normed_grad * gain_attn
    inputs_grad = (
        state_grad
        + inverse_attn
        * (unit_back - unit_attn * jnp.mean(unit_back * unit_attn, axis=-1, keepdims=True))
    ).astype(jnp.bfloat16)
    attn_gain_term = jnp.sum(normed_grad * unit_attn, axis=0) * first_tensor
    attn_gain_grad, q_gain_grad, k_gain_grad, moe_gain_grad, router_grad = lax.psum(
        (attn_gain_term, q_gain_term, k_gain_term, moe_gain_term, router_term),
        ("fsdp", "context", "tensor"),
    )
    return (
        output,
        inputs_grad,
        attn_gain_grad,
        w_qkv_grad,
        q_gain_grad,
        k_gain_grad,
        w_o_grad,
        moe_gain_grad,
        router_grad,
        w_experts_grad,
    )


SPREAD = ("fsdp", "context")
VMEM_BYTES = 60 * 2**20


def flip_pairs(size, bit):
    return [(place, place ^ bit) for place in range(size)]


def flip(array, name, bit):
    return lax.ppermute(array, name, flip_pairs(lax.axis_size(name), bit))


def nothing_kernel(*refs):
    pass


def after(array, *others):
    anywhere = pl.BlockSpec(memory_space=pl.ANY)
    return pl.pallas_call(
        nothing_kernel,
        in_specs=[anywhere] * (1 + len(others)),
        out_specs=anywhere,
        out_shape=jax.ShapeDtypeStruct(array.shape, array.dtype),
        input_output_aliases={0: 0},
        name="after",
    )(array, *others)


def add_low(left_side, right_side):
    return (left_side.astype(jnp.float32) + right_side.astype(jnp.float32)).astype(jnp.bfloat16)


def partner_bits():
    size = lax.axis_size("tensor")
    return [size >> step for step in range(1, size.bit_length())]


def partner_order():
    order = [0]
    for bit in partner_bits():
        order = order + [offset ^ bit for offset in order]
    return order


def own_first(array):
    place = lax.axis_index("tensor")
    rows = array.shape[0] // lax.axis_size("tensor")
    return jnp.concatenate(
        [
            lax.dynamic_slice_in_dim(array, (place ^ offset) * rows, rows)
            for offset in partner_order()
        ],
        axis=0,
    )


def own_back(array):
    place = lax.axis_index("tensor")
    order = partner_order()
    rows = array.shape[0] // len(order)
    slot_of = jnp.array([order.index(offset) for offset in range(len(order))], jnp.int32)
    return jnp.concatenate(
        [
            lax.dynamic_slice_in_dim(array, slot_of[place ^ block] * rows, rows)
            for block in range(len(order))
        ],
        axis=0,
    )


def tensor_gather_rows(piece):
    for bit in partner_bits():
        piece = jnp.concatenate([piece, flip(piece, "tensor", bit)], axis=0)
    return piece


def tensor_scatter_rows(half_of):
    bits = partner_bits()
    theirs = flip(half_of(1), "tensor", bits[-1])
    total = add_low(half_of(0), theirs)
    for bit in bits[-2::-1]:
        rows = total.shape[0] // 2
        total = add_low(total[:rows], flip(total[rows:], "tensor", bit))
    return total


def shift(array, step):
    size = lax.axis_size("fsdp")
    return lax.ppermute(array, "fsdp", [(start, (start + step) % size) for start in range(size)])


def spread_pieces(piece, waits=()):
    pairs = []
    for step in range(lax.axis_size("fsdp")):
        if step:
            if step <= len(waits):
                piece = after(piece, *waits[step - 1])
            piece = shift(piece, 1)
        pairs.append((piece, flip(piece, "context", 1)))
    return pairs


def step_place(step):
    return (lax.axis_index("fsdp") - step) % lax.axis_size("fsdp")


def pair_places(step):
    column = 2 * step_place(step)
    side = lax.axis_index("context")
    return column + side, column + 1 - side


def in_order(pairs):
    rows, columns = pairs[0][0].shape
    whole = jnp.zeros((2 * len(pairs) * rows, columns), pairs[0][0].dtype)
    for step, pair in enumerate(pairs):
        for place, piece in zip(pair_places(step), pair):
            whole = lax.dynamic_update_slice_in_dim(whole, piece, place * rows, 0)
    return whole


def scatter_steps(pair_of, waits):
    total = None
    for number, step in enumerate(reversed(range(lax.axis_size("fsdp")))):
        mine, theirs = pair_of(step)
        if number < len(waits) and waits[number]:
            mine = after(mine, *waits[number])
        part = mine.astype(jnp.float32) + flip(theirs, "context", 1).astype(jnp.float32)
        if total is not None:
            part = part + shift(total, -1).astype(jnp.float32)
        total = part.astype(jnp.bfloat16)
    return total


def row_pairs(array, rows):
    return lambda step: [
        lax.dynamic_slice_in_dim(array, place * rows, rows) for place in pair_places(step)
    ]


def context_scatter(array, *earlier):
    place = lax.axis_index("context")
    blocks = array.reshape(lax.axis_size("fsdp"), 2, -1, array.shape[1])
    mine = lax.dynamic_index_in_dim(blocks, place, 1, keepdims=False)
    theirs = lax.dynamic_index_in_dim(blocks, 1 - place, 1, keepdims=False)
    if earlier:
        mine = after(mine, *earlier)
    return add_low(mine, flip(theirs, "context", 1))


def sum_everywhere(array):
    for name in ("tensor", "context", "fsdp"):
        bit = 1
        while bit < lax.axis_size(name):
            array = array + flip(array, name, bit)
            bit *= 2
    return array


def nt_dot(left_side, right_side):
    return lax.dot_general(
        left_side, right_side, (((1,), (1,)), ((), ())), preferred_element_type=jnp.float32
    )


def nn_dot(left_side, right_side):
    return jnp.dot(left_side, right_side, preferred_element_type=jnp.float32)


def unit_rows(raw):
    inverse = lax.rsqrt(jnp.mean(raw * raw, axis=-1, keepdims=True) + EPSILON)
    return raw * inverse, inverse


def turn(array, half_size):
    return pltpu.roll(array, half_size, 1)


def attend_kernel(scale, raw_ref, cosine_ref, sine_ref, gain_ref, key_ref, value_ref, bias_ref, out_ref):
    half_size = raw_ref.shape[1] // 2
    unit, _ = unit_rows(raw_ref[...])
    scaled = unit * gain_ref[...]
    query = scaled * cosine_ref[...] + turn(scaled, half_size) * sine_ref[...]
    scores = nt_dot(key_ref[...], query.astype(jnp.bfloat16)) * scale + bias_ref[...]
    raised = jnp.exp(scores - jnp.max(scores, axis=0, keepdims=True))
    probs = (raised / jnp.sum(raised, axis=0, keepdims=True)).astype(jnp.bfloat16)
    out_ref[...] = nn_dot(value_ref[...], probs).T.astype(jnp.bfloat16)


def attend(projected, cosine, sine, gain, keys, values_turned, bias, heads, scale):
    rows, size = cosine.shape
    length = keys.shape[0]
    whole = lambda shape: pl.BlockSpec(shape, lambda head: (0, 0))
    by_head = pl.BlockSpec((rows, size), lambda head: (0, head))
    return pl.pallas_call(
        functools.partial(attend_kernel, scale),
        grid=(heads,),
        in_specs=[
            by_head,
            whole((rows, size)),
            whole((rows, size)),
            whole((1, size)),
            whole((length, size)),
            whole((size, length)),
            whole((length, rows)),
        ],
        out_specs=by_head,
        out_shape=jax.ShapeDtypeStruct((rows, heads * size), jnp.bfloat16),
        compiler_params=pltpu.CompilerParams(vmem_limit_bytes=VMEM_BYTES),
        cost_estimate=pl.CostEstimate(
            flops=8 * heads * rows * length * size,
            bytes_accessed=8 * heads * rows * size + 4 * rows * length,
            transcendentals=heads * rows * length,
        ),
        name="attend",
    )(projected, cosine, sine, gain, keys, values_turned, bias)


def attend_back_kernel(
    scale,
    raw_ref,
    cosine_ref,
    sine_ref,
    gain_ref,
    key_ref,
    key_turned_ref,
    value_ref,
    bias_ref,
    grad_ref,
    raw_grad_ref,
    key_grad_ref,
    value_grad_ref,
    gain_grad_ref,
):
    half_size = raw_ref.shape[1] // 2
    first = pl.program_id(0) == 0
    unit, inverse = unit_rows(raw_ref[...])
    scaled = unit * gain_ref[...]
    query = (scaled * cosine_ref[...] + turn(scaled, half_size) * sine_ref[...]).astype(
        jnp.bfloat16
    )
    out_grad = grad_ref[...]
    scores = nt_dot(key_ref[...], query) * scale + bias_ref[...]
    raised = jnp.exp(scores - jnp.max(scores, axis=0, keepdims=True))
    probs = raised / jnp.sum(raised, axis=0, keepdims=True)
    prob_grad = nt_dot(value_ref[...], out_grad)
    weighted = probs * prob_grad
    score_grad = (weighted - probs * jnp.sum(weighted, axis=0, keepdims=True)).astype(jnp.bfloat16)
    key_part = nn_dot(score_grad, query) * scale
    value_part = nn_dot(probs.astype(jnp.bfloat16), out_grad)
    query_grad = (nn_dot(key_turned_ref[...], score_grad) * scale).T
    scaled_grad = query_grad * cosine_ref[...] + turn(query_grad * sine_ref[...], half_size)
    gain_part = jnp.sum(
        (scaled_grad * unit).reshape(-1, 8, scaled_grad.shape[1]), axis=0
    )
    unit_grad = scaled_grad * gain_ref[...]
    raw_grad = inverse * (unit_grad - unit * jnp.mean(unit_grad * unit, axis=-1, keepdims=True))
    raw_grad_ref[...] = raw_grad.astype(jnp.bfloat16)

    @pl.when(first)
    def _():
        key_grad_ref[...] = key_part
        value_grad_ref[...] = value_part
        gain_grad_ref[...] = gain_part

    @pl.when(jnp.logical_not(first))
    def _():
        key_grad_ref[...] += key_part
        value_grad_ref[...] += value_part
        gain_grad_ref[...] += gain_part


def attend_back(projected, cosine, sine, gain, keys, values, bias, grads, heads, scale):
    rows, size = cosine.shape
    length = keys.shape[0]
    whole = lambda shape: pl.BlockSpec(shape, lambda head: (0, 0))
    by_head = pl.BlockSpec((rows, size), lambda head: (0, head))
    return pl.pallas_call(
        functools.partial(attend_back_kernel, scale),
        grid=(heads,),
        in_specs=[
            by_head,
            whole((rows, size)),
            whole((rows, size)),
            whole((1, size)),
            whole((length, size)),
            whole((size, length)),
            whole((length, size)),
            whole((length, rows)),
            by_head,
        ],
        out_specs=[by_head, whole((length, size)), whole((length, size)), whole((8, size))],
        out_shape=[
            jax.ShapeDtypeStruct((rows, heads * size), jnp.bfloat16),
            jax.ShapeDtypeStruct((length, size), jnp.float32),
            jax.ShapeDtypeStruct((length, size), jnp.float32),
            jax.ShapeDtypeStruct((8, size), jnp.float32),
        ],
        compiler_params=pltpu.CompilerParams(vmem_limit_bytes=VMEM_BYTES),
        cost_estimate=pl.CostEstimate(
            flops=20 * heads * rows * length * size,
            bytes_accessed=8 * heads * rows * size + 4 * rows * length,
            transcendentals=heads * rows * length,
        ),
        name="attend_back",
    )(projected, cosine, sine, gain, keys, keys.T, values, bias, grads)


def experts_kernel(
    local_experts,
    sides,
    gate_lanes,
    first_ref,
    token_ref,
    gate_ref,
    grad_ref,
    *refs,
):
    chunks = 2 * local_experts
    parts = refs[: chunks * sides]
    result_ref, back_ref, active_ref, slope_ref = refs[chunks * sides : chunks * sides + 4]
    inward, outward, actives, slopes, sems = refs[chunks * sides + 4 :]
    blocks, _, hidden_units, depth = parts[0].shape
    units = sides * hidden_units
    width = token_ref.shape[1]

    @pl.when(pl.program_id(0) == 0)
    def _():
        for chunk in range(chunks):
            for side in range(sides):
                part = parts[chunk * sides + side]
                for kind in range(3):
                    place = inward if kind < 2 else outward
                    rows = ((chunk * 2 + kind) if kind < 2 else chunk) * units
                    rows = pl.ds(rows + side * hidden_units, hidden_units)
                    for block in range(blocks):
                        pltpu.make_async_copy(
                            part.at[block, kind],
                            place.at[rows, pl.ds(block * depth, depth)],
                            sems.at[chunk, kind // 2],
                        ).start()

    def body():
        tokens = token_ref[...]
        grads = grad_ref[...]
        lanes = lax.broadcasted_iota(jnp.int32, gate_ref.shape, 1)
        all_gates = gate_ref[...].astype(jnp.float32)
        dots = jnp.zeros(gate_ref.shape, jnp.float32)
        for chunk in range(chunks):
            in_rows = pl.ds(chunk * 2 * units, 2 * units)
            out_rows = pl.ds(chunk * units, units)

            @pl.when(pl.program_id(0) == 0)
            def _():
                whole_in, whole_out = inward.at[in_rows], outward.at[out_rows]
                pltpu.make_async_copy(whole_in, whole_in, sems.at[chunk, 0]).wait()
                pltpu.make_async_copy(whole_out, whole_out, sems.at[chunk, 1]).wait()

            expert = first_ref[0] + chunk % local_experts
            gate_up = nt_dot(tokens, inward[in_rows, :])
            down_back = nt_dot(grads, outward[out_rows, :])
            here = (lanes == expert) | (lanes == expert + gate_lanes)
            gate = jnp.sum(jnp.where(here, all_gates, 0.0), axis=-1, keepdims=True)
            gate_half, up_half = gate_up[:, :units], gate_up[:, units:]
            sigmoid = jax.nn.sigmoid(gate_half)
            silu = gate_half * sigmoid
            active = silu * up_half
            act_grad = down_back * gate
            gate_slope = act_grad * up_half * (sigmoid + silu * (1.0 - sigmoid))
            gate_dot = jnp.sum(active * down_back, axis=-1, keepdims=True)
            dots = dots + jnp.where(lanes == expert, gate_dot, 0.0)
            low_active = (active * gate).astype(jnp.bfloat16)
            low_slopes = jnp.concatenate([gate_slope, act_grad * silu], axis=1)
            low_slopes = low_slopes.astype(jnp.bfloat16)
            actives[:, out_rows] = low_active
            slopes[:, in_rows] = low_slopes
            active_ref[out_rows, :] = low_active.T
            slope_ref[in_rows, :] = low_slopes.T
        back_ref[:, :width] = nn_dot(slopes[...], inward[...]).astype(jnp.bfloat16)
        back_ref[:, width:] = dots.astype(jnp.bfloat16)
        result_ref[...] = nn_dot(actives[...], outward[...]).astype(jnp.bfloat16)

    body()


def run_experts(first_expert, tokens, grads, parts, local_experts, gate_lanes):
    rows, width = grads.shape
    lanes = tokens.shape[1] - width
    sides = len(parts) // (2 * local_experts)
    units = 2 * local_experts * sides * parts[0].shape[2]
    block = min(256, rows)
    by_row = lambda columns, place: pl.BlockSpec((block, columns), lambda row, first: (row, place))
    by_column = lambda count: pl.BlockSpec((count, block), lambda row, first: (0, row))
    return pl.pallas_call(
        functools.partial(experts_kernel, local_experts, sides, gate_lanes),
        grid_spec=pltpu.PrefetchScalarGridSpec(
            num_scalar_prefetch=1,
            grid=(rows // block,),
            in_specs=[by_row(width, 0), by_row(lanes, width // lanes), by_row(width, 0)]
            + [pl.BlockSpec(memory_space=pl.ANY)] * len(parts),
            out_specs=[
                by_row(width, 0),
                by_row(width + lanes, 0),
                by_column(units),
                by_column(2 * units),
            ],
            scratch_shapes=[
                pltpu.VMEM((2 * units, width), jnp.bfloat16),
                pltpu.VMEM((units, width), jnp.bfloat16),
                pltpu.VMEM((block, units), jnp.bfloat16),
                pltpu.VMEM((block, 2 * units), jnp.bfloat16),
                pltpu.SemaphoreType.DMA((2 * local_experts, 2)),
            ],
        ),
        out_shape=[
            jax.ShapeDtypeStruct((rows, width), jnp.bfloat16),
            jax.ShapeDtypeStruct((rows, width + lanes), jnp.bfloat16),
            jax.ShapeDtypeStruct((units, rows), jnp.bfloat16),
            jax.ShapeDtypeStruct((2 * units, rows), jnp.bfloat16),
        ],
        compiler_params=pltpu.CompilerParams(vmem_limit_bytes=VMEM_BYTES),
        cost_estimate=pl.CostEstimate(
            flops=12 * rows * width * units,
            bytes_accessed=6 * units * (width + rows) + 8 * rows * width,
            transcendentals=rows * units,
        ),
        name="experts",
    )(first_expert.reshape(1), tokens, tokens, grads, *parts)


def expert_grads_kernel(hidden_units, slope_ref, active_ref, token_ref, grad_ref, *refs):
    sides = active_ref.shape[0] // hidden_units
    depth = refs[-1].shape[2]
    inward = nn_dot(slope_ref[...], token_ref[...])
    outward = nn_dot(active_ref[...], grad_ref[...])
    received, outs = refs[: len(refs) - sides], refs[len(refs) - sides :]
    if len(refs) == 1:
        received, outs = (), refs * sides
    for side in range(sides):
        for kind in range(3):
            start = ((kind * sides if kind < 2 else 0) + side) * hidden_units
            wide = (inward if kind < 2 else outward)[start : start + hidden_units]
            place = kind * hidden_units
            whole = (side * 3 + kind) * hidden_units
            for block in range(refs[-1].shape[0]):
                rows = wide[:, block * depth : (block + 1) * depth]
                if received:
                    more = received[0][block, whole : whole + hidden_units]
                    rows = rows + more.astype(jnp.float32)
                into = place if received else whole
                outs[side][block, into : into + hidden_units] = rows.astype(jnp.bfloat16)


def expert_grads(chunk, slopes, actives, tokens, grads, chunks, sides, blocks, received=None):
    rows, width = grads.shape
    depth = width // blocks
    units = actives.shape[0] // chunks
    step = 2 if blocks % 2 == 0 else 1
    by_block = lambda count: pl.BlockSpec((step, count, depth), lambda column: (column, 0, 0))
    shape = lambda count: jax.ShapeDtypeStruct((blocks, count, depth), jnp.bfloat16)
    alone = received is None
    return pl.pallas_call(
        functools.partial(expert_grads_kernel, units // sides),
        grid=(blocks // step,),
        in_specs=[
            pl.BlockSpec((2 * units, rows), lambda column: (chunk, 0)),
            pl.BlockSpec((units, rows), lambda column: (chunk, 0)),
            pl.BlockSpec((rows, step * depth), lambda column: (0, column)),
            pl.BlockSpec((rows, step * depth), lambda column: (0, column)),
        ]
        + ([] if alone else [by_block(3 * units)]),
        out_specs=by_block(3 * units) if alone else [by_block(3 * units // sides)] * sides,
        out_shape=shape(3 * units) if alone else [shape(3 * units // sides)] * sides,
        compiler_params=pltpu.CompilerParams(vmem_limit_bytes=VMEM_BYTES),
        cost_estimate=pl.CostEstimate(
            flops=6 * units * rows * width,
            bytes_accessed=6 * units * (rows + width) + 4 * rows * width,
            transcendentals=0,
        ),
        name="expert_grads",
    )(slopes, actives, tokens, grads, *([] if alone else [received]))


def expert_parallel_shards(
    inputs,
    attn_gain,
    joined_projection_weight,
    q_gain,
    k_gain,
    w_o,
    moe_gain,
    router,
    w_experts,
    segments,
    experts,
    out_grad,
):
    tok_rows, model_width = inputs.shape
    head_size = q_gain.shape[0]
    half_size = head_size // 2
    tensor_size = lax.axis_size("tensor")
    heads = QUERY_HEADS // KEY_VALUE_HEADS
    expert_count = router.shape[1]
    spread_size = lax.axis_size(SPREAD)
    local_experts = expert_count // spread_size
    hidden_units = w_experts.shape[3]
    slice_rows = w_experts.shape[0]
    own_rows = tok_rows // tensor_size
    context_place = lax.axis_index("context")
    own_start = lax.axis_index("tensor") * own_rows
    first_expert = lax.axis_index(SPREAD) * local_experts
    gain_attn = attn_gain.astype(jnp.float32)
    gain_moe = moe_gain.astype(jnp.float32)
    gain_query = q_gain.astype(jnp.float32)[None]
    gain_key = k_gain.astype(jnp.float32)
    score_scale = head_size ** (-0.5)

    attn_in_pairs = spread_pieces(joined_projection_weight)
    attn_in = in_order(attn_in_pairs)
    attn_out = lax.all_gather(
        after(w_o, attn_in_pairs[len(attn_in_pairs) // 2][0]), SPREAD, axis=0, tiled=True
    )
    own_grad = lax.dynamic_slice_in_dim(out_grad, own_start, own_rows)

    sent_weights = jnp.transpose(w_experts, (1, 2, 3, 0)).reshape(
        spread_size, local_experts, 3, hidden_units, slice_rows
    )
    ordered = own_first(inputs)
    own_index = own_first(jnp.arange(tok_rows, dtype=jnp.int32))
    own_tokens = context_place * tok_rows + own_index
    all_tokens = jnp.concatenate([own_tokens, (1 - context_place) * tok_rows + own_index])
    token_segments = jnp.take(segments, all_tokens)
    positions = jnp.take(doc_positions(segments), own_tokens)
    allowed = (token_segments[:, None] == token_segments[None, :tok_rows]) & (
        all_tokens[:, None] <= own_tokens[None, :]
    )
    bias = jnp.where(allowed, 0.0, NEGATIVE).astype(jnp.float32)
    inverse_angles = ROPE_THETA ** (
        -2.0 * jnp.arange(half_size, dtype=jnp.float32) / head_size
    )
    angles = positions.astype(jnp.float32)[:, None] * inverse_angles[None, :]
    cosine = jnp.concatenate([jnp.cos(angles)] * 2, axis=-1)
    half_sine = jnp.sin(angles)
    sine = jnp.concatenate([-half_sine, half_sine], axis=-1)

    residual = ordered.astype(jnp.float32)
    inverse_attn = lax.rsqrt(jnp.mean(residual * residual, axis=-1, keepdims=True) + EPSILON)
    normalized_input = (residual * inverse_attn * gain_attn).astype(jnp.bfloat16)
    projected = jnp.zeros((tok_rows, joined_projection_weight.shape[1]), jnp.float32)
    for step, pair in enumerate(attn_in_pairs):
        for place, piece in zip(pair_places(step), pair):
            columns = lax.dynamic_slice_in_dim(
                normalized_input, place * slice_rows, slice_rows, axis=1
            )
            projected = projected + nn_dot(columns, piece)
    weight_parts = [
        lax.all_to_all(after(sent_weights[:, 0], projected), SPREAD, 0, 0, tiled=True)
    ]
    all_grads = lax.all_gather(after(own_grad, projected), SPREAD, axis=0, tiled=True)
    key_raw = projected[:, heads * head_size : (heads + 1) * head_size]
    value_raw = projected[:, (heads + 1) * head_size :]

    def prepare_key(raw, gain):
        scaled = norm_rows(raw, gain)
        swapped = jnp.concatenate([scaled[:, half_size:], scaled[:, :half_size]], axis=-1)
        return scaled * cosine + swapped * sine

    key_values = jnp.concatenate([prepare_key(key_raw, gain_key), value_raw], axis=-1).astype(
        jnp.bfloat16
    )
    pairs = jnp.concatenate([key_values, flip(key_values, "context", 1)], axis=0)
    keys, values = pairs[:, :head_size], pairs[:, head_size:]
    attended = attend(
        projected,
        cosine,
        sine,
        gain_query,
        keys,
        values.T,
        bias,
        heads,
        score_scale,
    )
    weight_parts = [after(weight_parts[0], attended)]
    for expert in range(1, local_experts):
        sent = after(sent_weights[:, expert], weight_parts[-1])
        weight_parts.append(lax.all_to_all(sent, SPREAD, 0, 0, tiled=True))
    wide_bit, core_bit = partner_bits()
    wide_parts = [flip(part, "tensor", wide_bit) for part in weight_parts]
    half_rows = tok_rows // 2
    attn_sum = tensor_scatter_rows(
        lambda half: nt_dot(
            attended[half * half_rows : (half + 1) * half_rows], attn_out
        ).astype(jnp.bfloat16)
    )

    own_inputs = ordered[:own_rows].astype(jnp.float32)
    own_experts = lax.dynamic_slice_in_dim(experts, own_start, own_rows)
    hidden_state = own_inputs + attn_sum.astype(jnp.float32)
    inverse_moe = lax.rsqrt(jnp.mean(hidden_state * hidden_state, axis=-1, keepdims=True) + EPSILON)
    unit_moe = hidden_state * inverse_moe
    mixed_in = (unit_moe * gain_moe).astype(jnp.bfloat16)
    logits = nn_dot(mixed_in, router)
    expert_ids = jnp.arange(expert_count, dtype=jnp.int32)
    picked = jnp.any(own_experts[:, :, None] == expert_ids[None, None, :], axis=1)
    peak = jnp.max(jnp.where(picked, logits, -jnp.inf), axis=-1, keepdims=True)
    raised_gate = jnp.where(picked, jnp.exp(jnp.minimum(logits - peak, 0.0)), 0.0)
    gate_values = raised_gate / jnp.sum(raised_gate, axis=-1, keepdims=True)
    gate_high = gate_values.astype(jnp.bfloat16)
    gate_low = (gate_values - gate_high.astype(jnp.float32)).astype(jnp.bfloat16)
    lane_pad = 128 - 2 * expert_count
    payload = jnp.concatenate(
        [mixed_in, gate_high, gate_low, jnp.zeros((own_rows, lane_pad), jnp.bfloat16)], axis=1
    )
    tokens = in_order(
        spread_pieces(payload, [(weight_parts[0],), (wide_parts[0], all_grads), (weight_parts[-1],)])
    )
    own_parts, other_parts = [], []
    for pair in zip(weight_parts, wide_parts):
        pair = [pair[0], after(pair[1], tokens)]
        own_parts += pair
        other_parts += [flip(array, "tensor", core_bit) for array in pair]

    results, backs, actives, slopes = run_experts(
        first_expert, tokens, all_grads, own_parts + other_parts, local_experts, expert_count
    )
    grads_of = functools.partial(
        expert_grads,
        slopes=slopes,
        actives=actives,
        tokens=tokens,
        grads=all_grads,
        chunks=2 * local_experts,
        sides=len(partner_bits()),
        blocks=spread_size,
    )
    far_sums = [grads_of(local_experts + expert) for expert in range(local_experts)]
    own_sums = [
        grads_of(expert, received=flip(far_sums[expert], "tensor", core_bit))
        for expert in range(local_experts)
    ]
    exchange = lambda sums: add_low(sums[0], flip(sums[1], "tensor", wide_bit))
    moe_sum = lax.psum_scatter(results, SPREAD, scatter_dimension=0, tiled=True)
    expert_sums = [exchange(own_sums[0])]
    back_total = scatter_steps(
        row_pairs(backs, own_rows),
        [(), (far_sums[0],), (own_sums[0][0],), (far_sums[1], expert_sums[0])],
    )
    cotangent = own_grad.astype(jnp.float32)
    gate_dot = back_total[:, model_width : model_width + expert_count].astype(jnp.float32)
    logit_grad = (
        gate_values * (gate_dot - jnp.sum(gate_values * gate_dot, axis=-1, keepdims=True))
    ).astype(jnp.bfloat16)
    router_term = outer_rows(logit_grad, mixed_in)
    moe_back = back_total[:, :model_width].astype(jnp.float32) + nt_dot(logit_grad, router)
    unit_grad = moe_back * gain_moe
    state_grad = cotangent + inverse_moe * (
        unit_grad - unit_moe * jnp.mean(unit_grad * unit_moe, axis=-1, keepdims=True)
    )
    moe_gain_term = jnp.sum(moe_back * unit_moe, axis=0, keepdims=True)
    branch_grad = tensor_gather_rows(state_grad.astype(jnp.bfloat16))
    expert_backs = [lax.all_to_all(expert_sums[0], SPREAD, 0, 0, tiled=True)]
    w_o_part = outer_rows(branch_grad, attended).astype(jnp.bfloat16)
    attended_grad = nn_dot(after(branch_grad, own_sums[-1][0]), attn_out).astype(jnp.bfloat16)

    query_back, key_grad, value_grad, q_gain_rows = attend_back(
        projected, cosine, sine, gain_query, keys, values, bias, attended_grad, heads, score_scale
    )
    for mine, theirs in own_sums[1:]:
        expert_sums.append(exchange((after(mine, key_grad), after(theirs, branch_grad))))
    for sums in expert_sums[1:]:
        expert_backs.append(
            lax.all_to_all(after(sums, expert_backs[-1]), SPREAD, 0, 0, tiled=True)
        )
    w_experts_grad = (
        jnp.stack(expert_backs, axis=1)
        .reshape(expert_count, 3, hidden_units, slice_rows)
        .astype(jnp.float32)
        .transpose(3, 0, 1, 2)
    )
    pair_grad = jnp.concatenate([key_grad, value_grad], axis=-1)
    sent_pairs = after(pair_grad[tok_rows:].astype(jnp.bfloat16), expert_sums[0])
    pair_grad = pair_grad[:tok_rows] + flip(sent_pairs, "context", 1).astype(jnp.float32)
    key_back, k_gain_term = jax.vjp(prepare_key, key_raw, gain_key)[1](pair_grad[:, :head_size])
    projected_grad = jnp.concatenate(
        [
            query_back,
            key_back.astype(jnp.bfloat16),
            pair_grad[:, head_size:].astype(jnp.bfloat16),
        ],
        axis=1,
    )
    w_qkv_part = outer_rows(normalized_input, projected_grad).astype(jnp.bfloat16)
    w_qkv_rows = lax.psum_scatter(
        after(w_qkv_part, expert_sums[1], expert_backs[0]),
        SPREAD,
        scatter_dimension=0,
        tiled=True,
    )
    w_o_sum = context_scatter(w_o_part, w_qkv_part)
    late_grad = after(projected_grad, w_o_sum)
    w_o_rows = lax.all_to_all(
        after(w_o_sum, expert_backs[1]), "fsdp", 0, 0, tiled=True
    )
    w_o_grad = jnp.sum(w_o_rows.astype(jnp.float32), axis=0)
    w_qkv_grad = w_qkv_rows.astype(jnp.float32)
    own_output = (
        hidden_state + after(moe_sum, projected_grad).astype(jnp.float32)
    ).astype(jnp.bfloat16)
    output = own_back(tensor_gather_rows(own_output))
    normed_grad = tensor_scatter_rows(
        lambda half: nt_dot(
            late_grad[half * half_rows : (half + 1) * half_rows], attn_in
        ).astype(jnp.bfloat16)
    ).astype(jnp.float32)
    own_inverse = inverse_attn[:own_rows]
    own_unit = own_inputs * own_inverse
    unit_back = normed_grad * gain_attn
    own_inputs_grad = (
        state_grad
        + own_inverse
        * (unit_back - own_unit * jnp.mean(unit_back * own_unit, axis=-1, keepdims=True))
    ).astype(jnp.bfloat16)
    inputs_grad = own_back(tensor_gather_rows(own_inputs_grad))
    attn_gain_term = jnp.sum(normed_grad * own_unit, axis=0)
    gain_terms = jnp.concatenate([jnp.sum(q_gain_rows, axis=0), k_gain_term])
    sums = sum_everywhere(
        jnp.concatenate(
            [
                router_term,
                moe_gain_term,
                attn_gain_term[None],
                jnp.pad(gain_terms, (0, model_width - gain_terms.shape[0]))[None],
            ],
            axis=0,
        )
    )
    gain_sums = sums[expert_count + 2]
    return (
        output,
        inputs_grad,
        sums[expert_count + 1],
        w_qkv_grad,
        gain_sums[:head_size],
        gain_sums[head_size : 2 * head_size],
        w_o_grad,
        sums[expert_count],
        sums[:expert_count].T,
        w_experts_grad,
    )


def choose_shards(mesh, arrays):
    sizes = mesh.shape
    spread = sizes["fsdp"] * sizes["context"]
    tok_rows, width = arrays[0].shape
    head_size, expert_count = arrays[3].shape[0], arrays[7].shape[1]
    fits = (
        expert_count % spread == 0
        and 2 * expert_count <= 128
        and tok_rows % (32 * sizes["tensor"]) == 0
        and width % 128 == 0
        and head_size % 128 == 0
        and sizes["tensor"] == KEY_VALUE_HEADS
        and sizes["context"] == 2
        and sizes["fsdp"] & (sizes["fsdp"] - 1) == 0
    )
    return expert_parallel_shards if fits else shards


def solution(mesh):
    def by_shapes(*arrays):
        return choose_shards(mesh, arrays)(*arrays)

    return jax.shard_map(
        by_shapes,
        mesh=mesh,
        in_specs=(
            P(("fsdp", "context"), None),
            P(),
            P(("fsdp", "context"), "tensor"),
            P(),
            P(),
            P(("fsdp", "context"), "tensor"),
            P(),
            P(),
            P(("fsdp", "context"), None, None, "tensor"),
            P("fsdp"),
            P(("fsdp", "context"), None),
            P(("fsdp", "context"), None),
        ),
        out_specs=(
            P(("fsdp", "context"), None),
            P(("fsdp", "context"), None),
            P(),
            P(("fsdp", "context"), "tensor"),
            P(),
            P(),
            P(("fsdp", "context"), "tensor"),
            P(),
            P(),
            P(("fsdp", "context"), None, None, "tensor"),
        ),
        check_vma=False,
    )
```
